32 devices in a mesh: group: 2 (over x), dp: 16 (over z, y, core).
Axes of the slice: x: 2, y: 2, z: 4, core: 2. Of those that a mesh axis runs over, the one named last changes fastest.
Arguments:
- tokens: bfloat16 [512, 4096], P(('group', 'dp')), parts along dimension 0, may hold values from -6 to 6
- cotangent: bfloat16 [512, 8192], P('group', 'dp'), parts along dimension 0, may hold values from -0.75 to 0.75
- token_weight: float32 [512], P('group'), parts along dimension 0, may hold values from 0.5 to 1.5
- weight: bfloat16 [4096, 8192], P(None, 'dp'), may hold values from -0.09375 to 0.09375
- moment_one: bfloat16 [4096, 8192], P(None, 'dp'), may hold values from -6 to 6
- moment_two: bfloat16 [4096, 8192], P(None, 'dp'), may hold values from 0.003 to 10
- adjoint: float32 [4096, 8192], P(None, 'dp'), may hold values from -5 to 5
Outputs:
- theta_bar: float32 [8192, 8192], P('group', 'dp'), parts along dimension 0
- token_scores: float32 [512], P(('group', 'dp')), parts along dimension 0
The draws below stay inside these ranges and needn't reach their ends.
There are 2 independent parts, one for each index of `group`. The reference program is written for one: setup_inputs(seed, part) draws one part's arguments, and reference() takes and returns one part's arrays. A program takes and returns all parts, laid end to end along the dimension named above; an argument that names none is the same for every part. Nothing has to cross between parts.
All inputs are finite; a program needn't handle non-finite values.
Results may differ from the reference program's by a relative error of at most 0.0038.
Values may be sent and summed in bfloat16 or wider, within the bound.
No kernel may reach another device: no remote copies, remote signals or barrier semaphores. Data moves between devices by JAX's collectives and lax.ppermute only.
A program may use at most 128 MiB of HBM per device.

```python
import math
import jax
import jax.numpy as jnp
from jax import lax

D = 4096
FW = 8192
TOKENS = 256


def moment_fields(key):
    key = jax.random.fold_in(key, 7)
    key_one, key_rows, key_cols, key_base = jax.random.split(key, 4)
    ln_ten = math.log(10.0)
    one = jax.random.truncated_normal(key_one, -6.0, 6.0, (D, FW), jnp.float32)
    rows = jnp.exp(jax.random.uniform(key_rows, (D, 1), jnp.float32) * ln_ten)
    cols = jnp.exp(jax.random.uniform(key_cols, (1, FW), jnp.float32) * ln_ten)
    base = jnp.exp(jax.random.uniform(key_base, (D, FW), jnp.float32, -1.2, 1.2))
    place = jnp.arange(FW, dtype=jnp.float32)[None, :] / (FW - 1)
    trend = jnp.exp(-math.log(3.0) * place)
    two = 0.03 * base * rows * cols * trend
    return (one, two)


def draw_moment_one(key, part):
    one, two = moment_fields(key)
    return one.astype(jnp.bfloat16)


def draw_moment_two(key, part):
    one, two = moment_fields(key)
    return two.astype(jnp.bfloat16)


def draw_adjoint(key, part):
    one, two = moment_fields(key)
    ratio = one / jnp.sqrt(two + 0.05)
    noise_key = jax.random.fold_in(key, 11)
    along = 1.5 * jnp.tanh(ratio / 3.0)
    noise = 0.8 * jax.random.truncated_normal(noise_key, -4.0, 4.0, (D, FW), jnp.float32)
    return along + noise


def levels(rng, dims, cuts, least, high):
    def one(position, blocks):
        steps = jax.random.uniform(jax.random.fold_in(jax.random.fold_in(rng, 6), position), (blocks,), jnp.float32, least / len(cuts), high / len(cuts))
        return jnp.repeat(jnp.exp(steps), dims[position] // blocks).reshape((-1,) + (1,) * (len(dims) - position - 1))

    factor_of = one(*cuts[0])
    for cut in cuts[1:]:
        factor_of = factor_of * one(*cut)
    return factor_of


def normal_values(key, dims, scale, reach, shards=(), held_as=jnp.bfloat16):
    loudness = levels(key, dims, shards, -0.22, 0.18) if shards else 1.0
    result = jax.random.normal(key, dims, jnp.float32) * scale * loudness
    return jnp.minimum(jnp.maximum(result, -reach), reach).astype(held_as)


def setup_inputs(seed: int = 0, part: int = 0) -> dict:
    seeds = jax.random.split(jax.random.key(seed), 8)
    own_keys = jax.random.split(jax.random.fold_in(seeds[7], part), 8)
    return {
        "tokens": normal_values(own_keys[0], (TOKENS, D), 1.0, 6.0, ((0, 16),)),
        "cotangent": normal_values(own_keys[1], (TOKENS, FW), 0.05, 0.75, ((1, 16),)),
        "token_weight": jnp.clip(jax.random.uniform(own_keys[2], (TOKENS,), jnp.float32, 0.5, 1.5), 0.5, 1.5),
        "weight": normal_values(seeds[3], (D, FW), D ** -0.5, 0.09375, ((1, 16),)),
        "moment_one": draw_moment_one(jax.random.fold_in(seeds[7], 71), part),
        "moment_two": draw_moment_two(jax.random.fold_in(seeds[7], 71), part),
        "adjoint": draw_adjoint(jax.random.fold_in(seeds[7], 71), part),
    }


def slopes(gate):
    sig = jax.nn.sigmoid(gate)
    slope = sig * (1.0 + gate * (1.0 - sig))
    curve = sig * (1.0 - sig) * (2.0 + gate * (1.0 - 2.0 * sig))
    return (slope, curve)

def reference(tokens, cotangent, token_weight, weight, moment_one, moment_two, adjoint):
    gate = jnp.dot(tokens, weight, preferred_element_type=jnp.float32)
    slope, curve = slopes(gate)
    cot_f = cotangent.astype(jnp.float32)
    scaled = (token_weight[:, None] * cot_f * slope).astype(jnp.bfloat16)
    grad = lax.dot_general(tokens, scaled, (((0,), (0,)), ((), ())), preferred_element_type=jnp.float32)
    first = 0.9 * moment_one.astype(jnp.float32) + 0.1 * grad
    second = 0.95 * moment_two.astype(jnp.float32) + 0.05 * grad * grad
    root = jnp.sqrt(second)
    den = root + 1e-08
    upd = first / den
    count = D * FW
    sq = jnp.sum(upd * upd)
    cross = jnp.sum(adjoint * upd)
    rms = jnp.sqrt(sq / count)
    scale = 1.0 / jnp.maximum(1.0, rms)
    bind = jnp.where(rms > 1.0, 1.0 / (rms * rms * rms), 0.0)
    ubar = -0.01 * scale * adjoint + 0.01 * cross * bind / count * upd
    mbar = ubar / den
    vbar = -ubar * first / (den * den) / (2.0 * root)
    gbar = (0.1 * mbar + 0.1 * grad * vbar).astype(jnp.bfloat16)
    probe = jnp.dot(tokens, gbar, preferred_element_type=jnp.float32)
    bent = (token_weight[:, None] * cot_f * curve * probe).astype(jnp.bfloat16)
    theta_bar = 0.999 * adjoint + lax.dot_general(tokens, bent, (((0,), (0,)), ((), ())), preferred_element_type=jnp.float32)
    token_scores = lax.optimization_barrier(jnp.sum(cot_f * slope * probe, axis=1))
    return (theta_bar, token_scores)
```

```python
import functools

import jax
import jax.numpy as jnp
from jax import lax
from jax.experimental import pallas as pl
from jax.experimental.pallas import tpu as pltpu
from jax.sharding import PartitionSpec as P

TILE = 512
ROWS = 16
VMEM_BYTES = 56 << 20
TN = (((0,), (0,)), ((), ()))


def params():
    return pltpu.CompilerParams(vmem_limit_bytes=VMEM_BYTES, dimension_semantics=("arbitrary",))


def f32dot(a, b):
    return jnp.dot(a, b, preferred_element_type=jnp.float32)


def digits(n):
    return (n // 4, 2, 2)


def shift(value, n, slow, mid, core):
    z, y, c = digits(n)
    pairs = []
    for d in range(n):
        dz, dy, dc = d // (y * c), d // c % y, d % c
        source = ((dz + slow) % z * y + (dy + mid) % y) * c + (dc + core) % c
        pairs.append((source, d))
    return lax.ppermute(value, "dp", pairs)


def gather(tokens, n):
    z, y, c = digits(n)
    parts = {(0, 0, 0): tokens}
    for slow in range(1, z):
        parts[slow, 0, 0] = shift(tokens, n, slow, 0, 0)
    for slow in range(z):
        parts[slow, 1, 0] = shift(parts[slow, 0, 0], n, 0, 1, 0)
    for slow in range(z):
        for mid in range(y):
            parts[slow, mid, 1] = shift(parts[slow, mid, 0], n, 0, 0, 1)
    me = lax.axis_index("dp")
    mz, my, mc = me // (y * c), me // c % y, me % c
    places = [((mz + a) % z * y + (my + b) % y) * c + (mc + d) % c for a, b, d in parts]
    return list(parts.values()), jnp.stack(places).astype(jnp.int32)


def all_sum(value, n):
    z, y, c = digits(n)
    total = value
    for slow in range(1, z):
        total = total + shift(value, n, slow, 0, 0)
    return [total] + [shift(total, n, 0, a, b) for a, b in ((0, 1), (1, 0), (1, 1))]


def gate_kernel(n, places, *refs):
    parts = refs[:n]
    weight, cot, token_weight, tokens, turned, scaled, bend, score, rows, total = refs[n:]
    step = pl.program_id(0)
    height = parts[0].shape[0]
    for part, ref in enumerate(parts):
        at = pl.multiple_of(places[part] * height, height)
        rows[pl.ds(at, height), :] = ref[...]
    here = rows[...]
    tokens[...] = here
    turned[...] = here.T

    @pl.when(step == 0)
    def _():
        total[...] = jnp.zeros_like(total)

    total[...] += f32dot(here, weight[...])

    @pl.when(step == pl.num_programs(0) - 1)
    def _():
        gate = total[...]
        tw = jnp.transpose(jnp.broadcast_to(token_weight[...], (8, token_weight.shape[1])))[:, :1]
        cot_f = cot[...].astype(jnp.float32)
        sig = 1.0 / (1.0 + jnp.exp(-gate))
        slope = sig * (1.0 + gate * (1.0 - sig))
        curve = sig * (1.0 - sig) * (2.0 + gate * (1.0 - 2.0 * sig))
        scaled[...] = (tw * cot_f * slope).astype(jnp.bfloat16)
        bend[...] = tw * cot_f * curve
        score[...] = cot_f * slope


def gate_call(parts, places, weight, cot, token_weight):
    n = len(parts)
    height, depth = parts[0].shape
    count, width = cot.shape
    whole = lambda shape: pl.BlockSpec(shape, lambda i, s: (0, 0))
    return pl.pallas_call(
        functools.partial(gate_kernel, n),
        grid_spec=pltpu.PrefetchScalarGridSpec(
            num_scalar_prefetch=1,
            grid=(depth // TILE,),
            in_specs=[pl.BlockSpec((height, TILE), lambda i, s: (0, i))] * n
            + [
                pl.BlockSpec((TILE, width), lambda i, s: (i, 0)),
                whole((count, width)),
                whole((1, count)),
            ],
            out_specs=[
                pl.BlockSpec((count, TILE), lambda i, s: (0, i)),
                pl.BlockSpec((TILE, count), lambda i, s: (i, 0)),
                whole((count, width)),
                whole((count, width)),
                whole((count, width)),
            ],
            scratch_shapes=[pltpu.VMEM((count, TILE), jnp.bfloat16), pltpu.VMEM((count, width), jnp.float32)],
        ),
        out_shape=[
            jax.ShapeDtypeStruct((count, depth), jnp.bfloat16),
            jax.ShapeDtypeStruct((depth, count), jnp.bfloat16),
            jax.ShapeDtypeStruct((count, width), jnp.bfloat16),
            jax.ShapeDtypeStruct((count, width), jnp.float32),
            jax.ShapeDtypeStruct((count, width), jnp.float32),
        ],
        compiler_params=params(),
        name="gate",
    )(places, *parts, weight, cot, token_weight)


def update(grad, one, two):
    first = 0.9 * one.astype(jnp.float32) + 0.1 * grad
    second = 0.95 * two.astype(jnp.float32) + 0.05 * (grad * grad)
    over = lax.rsqrt(second)
    inv = pltpu.reciprocal(second * over + 1e-08, approx=True)
    return over, inv, first * inv


def fold(x):
    return jnp.sum(x.reshape(x.shape[0] // 8, 8, x.shape[1]), axis=0)


def step_kernel(tokens, turned, scaled, one, two, adjoint, score, along, across, stats, grad, va, vb, sums, lean):
    step = pl.program_id(0)
    tall, width = one.shape

    grad[...] = f32dot(turned[...], scaled[...])

    @pl.when(step == 0)
    def _():
        sums[...] = jnp.zeros_like(sums)
        along[...] = jnp.zeros_like(along)
        across[...] = jnp.zeros_like(across)
        sq = jnp.zeros((8, width), jnp.float32)
        cross = jnp.zeros((8, width), jnp.float32)
        for r in range(0, 256, ROWS):
            at = pl.ds(r, ROWS)
            _, _, upd = update(grad[at, :], one[at, :], two[at, :])
            sq += fold(upd * upd)
            cross += fold(adjoint[at, :] * upd)
        sq = jnp.sum(sq, keepdims=True)
        lean[...] = jnp.broadcast_to(
            jnp.where(sq > 256.0 * width, jnp.sum(cross, keepdims=True) / jnp.maximum(sq, 1.0), 0.0), lean.shape
        )

    guess = lean[0:1, 0:1]
    sq = sums[0]
    cross = sums[1]
    for r in range(0, tall, ROWS):
        at = pl.ds(r, ROWS)
        g, adj = grad[at, :], adjoint[at, :]
        over, inv, upd = update(g, one[at, :], two[at, :])
        sq += fold(upd * upd)
        cross += fold(adj * upd)
        pull = inv * (0.1 - 0.05 * (g * (upd * over)))
        va[at, :] = ((adj - guess * upd) * pull).astype(jnp.bfloat16)
        vb[at, :] = (upd * pull).astype(jnp.bfloat16)
    sums[0] = sq
    sums[1] = cross
    along[...] += f32dot(tokens[...], va[...])
    across[...] += f32dot(tokens[...], vb[...])

    @pl.when(step == pl.num_programs(0) - 1)
    def _():
        b = score[...] * across[...]
        a = score[...] * along[...] + guess * b

        def lanes(x):
            x = sum(x[:, i : i + 128] for i in range(0, width, 128))
            return jnp.sum(jnp.transpose(x), axis=0, keepdims=True)

        count = a.shape[0]
        one_row = lambda x: jnp.broadcast_to(jnp.sum(x, keepdims=True), (1, count))
        stats[0:1, :] = lanes(a)
        stats[1:2, :] = lanes(b)
        stats[2:3, :] = one_row(sums[0])
        stats[3:4, :] = one_row(sums[1])
        stats[4:8, :] = jnp.broadcast_to(guess, (4, count))


def step_call(tokens, turned, scaled, one, two, adjoint, score):
    count, depth = tokens.shape
    width = one.shape[1]
    whole = lambda shape: pl.BlockSpec(shape, lambda i: (0, 0))
    tile = pl.BlockSpec((TILE, width), lambda i: (i, 0))
    return pl.pallas_call(
        step_kernel,
        grid=(depth // TILE,),
        in_specs=[
            pl.BlockSpec((count, TILE), lambda i: (0, i)),
            pl.BlockSpec((TILE, count), lambda i: (i, 0)),
            whole((count, width)),
            tile,
            tile,
            tile,
            whole((count, width)),
        ],
        out_specs=[whole((count, width)), whole((count, width)), whole((8, count))],
        out_shape=[
            jax.ShapeDtypeStruct((count, width), jnp.float32),
            jax.ShapeDtypeStruct((count, width), jnp.float32),
            jax.ShapeDtypeStruct((8, count), jnp.float32),
        ],
        scratch_shapes=[
            pltpu.VMEM((TILE, width), jnp.float32),
            pltpu.VMEM((TILE, width), jnp.bfloat16),
            pltpu.VMEM((TILE, width), jnp.bfloat16),
            pltpu.VMEM((2, 8, width), jnp.float32),
            pltpu.VMEM((8, 128), jnp.float32),
        ],
        compiler_params=params(),
        name="step",
    )(tokens, turned, scaled, one, two, adjoint, score)


def theta_kernel(entries, s0, s1, s2, s3, own, along, across, bend, turned, adjoint, theta, scores, bent):
    @pl.when(pl.program_id(0) == 0)
    def _():
        total = s0[...] + s1[...] + (s2[...] + s3[...])
        sq, cross = total[2:3, 0:1], total[3:4, 0:1]
        rms = jnp.sqrt(sq / entries)
        scale = 1.0 / jnp.maximum(1.0, rms)
        bind = jnp.where(rms > 1.0, 1.0 / (rms * rms * rms), 0.0)
        lead = -0.01 * scale
        rest = 0.01 * cross * bind / entries
        scores[...] = lead * total[0:1, :] + rest * total[1:2, :]
        mixed = rest + lead * own[4:5, 0:1]
        bent[...] = (bend[...] * (lead * along[...] + mixed * across[...])).astype(jnp.bfloat16)

    theta[...] = 0.999 * adjoint[...] + f32dot(turned[...], bent[...])


def theta_call(entries, sums, own, along, across, bend, turned, adjoint):
    depth, width = adjoint.shape
    count = turned.shape[1]
    whole = lambda shape: pl.BlockSpec(shape, lambda i: (0, 0))
    tile = pl.BlockSpec((TILE, width), lambda i: (i, 0))
    return pl.pallas_call(
        functools.partial(theta_kernel, entries),
        grid=(depth // TILE,),
        in_specs=[whole((8, count))] * 5
        + [whole((count, width))] * 3
        + [pl.BlockSpec((TILE, count), lambda i: (i, 0)), tile],
        out_specs=[tile, whole((1, count))],
        out_shape=[
            jax.ShapeDtypeStruct((depth, width), jnp.float32),
            jax.ShapeDtypeStruct((1, count), jnp.float32),
        ],
        scratch_shapes=[pltpu.VMEM((count, width), jnp.bfloat16)],
        compiler_params=params(),
        name="theta",
    )(*sums, own, along, across, bend, turned, adjoint)


def shards(n, tokens, cotangent, token_weight, weight, moment_one, moment_two, adjoint):
    entries = float(adjoint.shape[0] * adjoint.shape[1] * n)
    parts, places = gather(tokens, n)
    rows, turned, scaled, bend, score = gate_call(
        parts, places, weight, cotangent, token_weight.reshape(1, -1)
    )
    along, across, stats = step_call(rows, turned, scaled, moment_one, moment_two, adjoint, score)
    sums = all_sum(stats, n)
    theta_bar, scores = theta_call(entries, sums, stats, along, across, bend, turned, adjoint)
    height = tokens.shape[0]
    token_scores = lax.dynamic_slice(scores[0], (lax.axis_index("dp") * height,), (height,))
    return (theta_bar, token_scores)


def solution(mesh):
    in_specs = (
        P(("group", "dp"), None),
        P("group", "dp"),
        P("group"),
        P(None, "dp"),
        P(None, "dp"),
        P(None, "dp"),
        P(None, "dp"),
    )
    out_specs = (P("group", "dp"), P(("group", "dp")))
    body = functools.partial(shards, mesh.shape["dp"])
    return jax.shard_map(body, mesh=mesh, in_specs=in_specs, out_specs=out_specs, check_vma=False)
```

```python
import functools

import jax
import jax.numpy as jnp
from jax import lax
from jax.experimental import pallas as pl
from jax.experimental.pallas import tpu as pltpu
from jax.sharding import PartitionSpec as P

TILE = 512
ROWS = 16
SAMPLE = 256
VMEM_BYTES = 18 << 20
RATIO = 0.1 / 0.05**0.5


def f32dot(a, b):
    return jnp.dot(a, b, preferred_element_type=jnp.float32)


def digits(n):
    return (n // 4, 2, 2)


def shift(value, n, slow, mid, core):
    z, y, c = digits(n)
    pairs = []
    for d in range(n):
        dz, dy, dc = d // (y * c), d // c % y, d % c
        source = ((dz + slow) % z * y + (dy + mid) % y) * c + (dc + core) % c
        pairs.append((source, d))
    return lax.ppermute(value, "dp", pairs)


def gather(tokens, n):
    z, y, c = digits(n)
    parts = {(0, 0, 0): tokens}
    for slow in range(1, z):
        parts[slow, 0, 0] = shift(tokens, n, slow, 0, 0)
    for slow in range(z):
        parts[slow, 1, 0] = shift(parts[slow, 0, 0], n, 0, 1, 0)
    for slow in range(z):
        for mid in range(y):
            parts[slow, mid, 1] = shift(parts[slow, mid, 0], n, 0, 0, 1)
    me = lax.axis_index("dp")
    mz, my, mc = me // (y * c), me // c % y, me % c
    places = [((mz + a) % z * y + (my + b) % y) * c + (mc + d) % c for a, b, d in parts]
    return list(parts.values()), jnp.stack(places).astype(jnp.int32)


def all_sum(value, n):
    z, y, c = digits(n)
    total = value
    for slow in range(1, z):
        total = total + shift(value, n, slow, 0, 0)
    return [total] + [shift(total, n, 0, a, b) for a, b in ((0, 1), (1, 0), (1, 1))]


def over_columns(row):
    return jnp.transpose(jnp.broadcast_to(row, (8, row.shape[1])))[:, :1]


def over_lanes(x):
    x = sum(x[:, i : i + 128] for i in range(0, x.shape[1], 128))
    return jnp.sum(jnp.transpose(x), axis=0, keepdims=True)


def fold(x):
    return jnp.sum(x.reshape(x.shape[0] // 8, 8, x.shape[1]), axis=0)


def update(grad, one, two):
    first = 9.0 * one.astype(jnp.float32) + grad
    second = 19.0 * two.astype(jnp.float32) + grad * grad
    over = lax.rsqrt(second)
    inv = pltpu.reciprocal(second * over + 1e-08 / 0.05**0.5, approx=True)
    return over, inv, first * inv


def replay_kernel(n, *refs):
    places, parts = refs[0], refs[1 : n + 1]
    (weight, cot, token_weight, one, two, adjoint) = refs[n + 1 : n + 7]
    (turned, along, across, bend, stats) = refs[n + 7 : n + 12]
    (tokens, scaled, score, g0, g1, a0, a1, b0, b1, sums) = refs[n + 12 :]
    grads, firsts, seconds = (g0, g1), (a0, a1), (b0, b1)
    height, depth = parts[0].shape
    count, width = cot.shape
    tiles = depth // TILE

    for part, ref in enumerate(parts):
        at = pl.multiple_of(places[part] * height, height)
        tokens[pl.ds(at, height), :] = ref[...]

    def span(i):
        return pl.ds(pl.multiple_of(i * TILE, TILE), TILE)

    along[...] = jnp.zeros_like(along)
    across[...] = jnp.zeros_like(across)

    def gate_step(i, _):
        here = tokens[:, span(i)]
        along[...] += f32dot(here, weight[span(i), :])
        turned[span(i), :] = here.T
        return 0

    lax.fori_loop(0, tiles, gate_step, 0)

    gate = along[...]
    weights = over_columns(token_weight[...])
    cot_f = cot[...].astype(jnp.float32)
    sig = 1.0 / (1.0 + jnp.exp(-gate))
    slope = sig * (1.0 + gate * (1.0 - sig))
    curve = sig * (1.0 - sig) * (2.0 + gate * (1.0 - 2.0 * sig))
    scaled[...] = (weights * cot_f * slope).astype(jnp.bfloat16)
    bend[...] = weights * cot_f * curve
    score[...] = cot_f * slope
    along[...] = jnp.zeros_like(along)

    def grad_tile(i, slot):
        grads[slot][...] = f32dot(turned[span(i), :], scaled[...])

    def probe_tile(i, slot):
        here = tokens[:, span(i)]
        along[...] += f32dot(here, firsts[slot][...])
        across[...] += f32dot(here, seconds[slot][...])

    def rows_of(i, slot, r):
        at = pl.ds(pl.multiple_of(i * TILE + r, ROWS), ROWS)
        return grads[slot][r : r + ROWS, :], one[at, :], two[at, :], adjoint[at, :]

    grad_tile(0, 0)
    sq = jnp.zeros((8, width), jnp.float32)
    cross = jnp.zeros((8, width), jnp.float32)
    for r in range(0, SAMPLE, ROWS):
        g, m1, m2, adj = rows_of(0, 0, r)
        _, _, upd = update(g, m1, m2)
        sq += fold(upd * upd)
        cross += fold(adj * upd)
    sq = jnp.sum(sq, keepdims=True)
    clipped = sq * RATIO**2 > float(SAMPLE * width)
    guess = jnp.where(clipped, jnp.sum(cross, keepdims=True) / jnp.maximum(sq, 1.0), 0.0)

    sums[...] = jnp.zeros_like(sums)

    def update_tile(i, slot):
        sq, cross = sums[0], sums[1]
        for r in range(0, TILE, ROWS):
            g, m1, m2, adj = rows_of(i, slot, r)
            over, inv, upd = update(g, m1, m2)
            sq += fold(upd * upd)
            cross += fold(adj * upd)
            pull = inv * (1.0 - g * (upd * over))
            firsts[slot][r : r + ROWS, :] = ((adj - guess * upd) * pull).astype(jnp.bfloat16)
            seconds[slot][r : r + ROWS, :] = (upd * pull).astype(jnp.bfloat16)
        sums[0] = sq
        sums[1] = cross

    grad_tile(1, 1)
    update_tile(0, 0)

    def pair(k, _):
        i = 2 * k + 1
        for j, slot in ((0, 1), (1, 0)):
            grad_tile(i + j + 1, 1 - slot)
            update_tile(i + j, slot)
            probe_tile(i + j - 1, 1 - slot)
        return 0

    lax.fori_loop(0, tiles // 2 - 1, pair, 0)
    update_tile(tiles - 1, 1)
    probe_tile(tiles - 2, 0)
    probe_tile(tiles - 1, 1)

    b = score[...] * across[...]
    a = score[...] * along[...] + guess * b
    whole = lambda x: jnp.broadcast_to(jnp.sum(x, keepdims=True), (1, count))
    stats[0:1, :] = RATIO * over_lanes(a)
    stats[1:2, :] = RATIO**2 * over_lanes(b)
    stats[2:3, :] = RATIO**2 * whole(sums[0])
    stats[3:4, :] = RATIO * whole(sums[1])
    stats[4:8, :] = jnp.broadcast_to(guess, (4, count))


def replay_call(places, parts, weight, cot, token_weight, one, two, adjoint):
    n = len(parts)
    depth = parts[0].shape[1]
    count, width = cot.shape
    vmem = pl.BlockSpec(memory_space=pltpu.VMEM)
    block = lambda dtype: pltpu.VMEM((TILE, width), dtype)
    return pl.pallas_call(
        functools.partial(replay_kernel, n),
        in_specs=[pl.BlockSpec(memory_space=pltpu.SMEM)] + [vmem] * (n + 6),
        out_specs=[vmem] * 5,
        out_shape=[
            pltpu.VMEM((depth, count), jnp.bfloat16),
            pltpu.VMEM((count, width), jnp.float32),
            pltpu.VMEM((count, width), jnp.float32),
            pltpu.VMEM((count, width), jnp.float32),
            pltpu.VMEM((8, count), jnp.float32),
        ],
        scratch_shapes=[
            pltpu.VMEM((count, depth), jnp.bfloat16),
            pltpu.VMEM((count, width), jnp.bfloat16),
            pltpu.VMEM((count, width), jnp.float32),
            block(jnp.float32),
            block(jnp.float32),
            block(jnp.bfloat16),
            block(jnp.bfloat16),
            block(jnp.bfloat16),
            block(jnp.bfloat16),
            pltpu.VMEM((2, 8, width), jnp.float32),
        ],
        compiler_params=pltpu.CompilerParams(vmem_limit_bytes=VMEM_BYTES),
        name="replay",
    )(places, *[resident(x) for x in (*parts, weight, cot, token_weight, one, two, adjoint)])


def resident(x):
    return pltpu.with_memory_space_constraint(x, pltpu.VMEM)


def theta_kernel(entries, s0, s1, s2, s3, own, along, across, bend, turned, adjoint, theta, scores, ready, sent):
    total = s0[...] + s1[...] + (s2[...] + s3[...])
    sq, cross = total[2:3, 0:1], total[3:4, 0:1]
    rms = jnp.sqrt(sq / entries)
    scale = 1.0 / jnp.maximum(1.0, rms)
    bind = jnp.where(rms > 1.0, 1.0 / (rms * rms * rms), 0.0)
    lead = -0.01 * scale
    rest = 0.01 * cross * bind / entries
    scores[...] = lead * total[0:1, :] + rest * total[1:2, :]
    lead_here = RATIO * lead
    rest_here = RATIO**2 * rest + lead_here * own[4:5, 0:1]
    bent = (bend[...] * (lead_here * along[...] + rest_here * across[...])).astype(jnp.bfloat16)

    def copy(i):
        at = pl.ds(i * TILE, TILE)
        return pltpu.make_async_copy(ready.at[at, :], theta.at[at, :], sent.at[i])

    tiles = theta.shape[0] // TILE
    for i in range(tiles):
        at = pl.ds(i * TILE, TILE)
        ready[at, :] = 0.999 * adjoint[at, :] + f32dot(turned[at, :], bent)
        copy(i).start()
    for i in range(tiles):
        copy(i).wait()


def theta_call(entries, sums, own, along, across, bend, turned, adjoint):
    depth, width = adjoint.shape
    count = turned.shape[1]
    vmem = pl.BlockSpec(memory_space=pltpu.VMEM)
    return pl.pallas_call(
        functools.partial(theta_kernel, entries),
        in_specs=[vmem] * 10,
        out_specs=[pl.BlockSpec(memory_space=pl.ANY), vmem],
        out_shape=[
            jax.ShapeDtypeStruct((depth, width), jnp.float32),
            jax.ShapeDtypeStruct((1, count), jnp.float32),
        ],
        scratch_shapes=[pltpu.VMEM((depth, width), jnp.float32), pltpu.SemaphoreType.DMA((depth // TILE,))],
        compiler_params=pltpu.CompilerParams(vmem_limit_bytes=VMEM_BYTES),
        name="theta",
    )(*[resident(x) for x in (*sums, own, along, across, bend, turned, adjoint)])


def shards(n, tokens, cotangent, token_weight, weight, moment_one, moment_two, adjoint):
    entries = float(adjoint.shape[0] * adjoint.shape[1] * n)
    parts, places = gather(tokens, n)
    turned, along, across, bend, stats = replay_call(
        places, parts, weight, cotangent, token_weight.reshape(1, -1), moment_one, moment_two, adjoint
    )
    sums = all_sum(stats, n)
    theta_bar, scores = theta_call(entries, sums, stats, along, across, bend, turned, adjoint)
    height = tokens.shape[0]
    token_scores = lax.dynamic_slice(scores[0], (lax.axis_index("dp") * height,), (height,))
    return (theta_bar, token_scores)


def solution(mesh):
    in_specs = (
        P(("group", "dp"), None),
        P("group", "dp"),
        P("group"),
        P(None, "dp"),
        P(None, "dp"),
        P(None, "dp"),
        P(None, "dp"),
    )
    out_specs = (P("group", "dp"), P(("group", "dp")))
    body = functools.partial(shards, mesh.shape["dp"])
    return jax.shard_map(body, mesh=mesh, in_specs=in_specs, out_specs=out_specs, check_vma=False)
```

```python
import functools

import jax
import jax.numpy as jnp
from jax import lax
from jax.experimental import pallas as pl
from jax.experimental.pallas import tpu as pltpu
from jax.sharding import PartitionSpec as P

TILE = 512
ROWS = 16
SAMPLE = 256
VMEM_BYTES = 28 << 20
RATIO = 0.1 / 0.05**0.5


def f32dot(a, b):
    return jnp.dot(a, b, preferred_element_type=jnp.float32)


def digits(n):
    return (n // 4, 2, 2)


def shift(value, n, slow, mid, core):
    z, y, c = digits(n)
    pairs = []
    for d in range(n):
        dz, dy, dc = d // (y * c), d // c % y, d % c
        source = ((dz + slow) % z * y + (dy + mid) % y) * c + (dc + core) % c
        pairs.append((source, d))
    return lax.ppermute(value, "dp", pairs)


def gather(tokens, n):
    z, y, c = digits(n)
    parts = {(0, 0, 0): tokens}
    for slow in range(1, z):
        parts[slow, 0, 0] = shift(tokens, n, slow, 0, 0)
    for slow in range(z):
        parts[slow, 1, 0] = shift(parts[slow, 0, 0], n, 0, 1, 0)
    for slow in range(z):
        for mid in range(y):
            parts[slow, mid, 1] = shift(parts[slow, mid, 0], n, 0, 0, 1)
    return parts


def owners(n, steps):
    z, y, c = digits(n)
    me = lax.axis_index("dp")
    mz, my, mc = me // (y * c), lax.rem(me // c, y), lax.rem(me, c)
    return [(lax.rem(mz + a, z) * y + lax.rem(my + b, y)) * c + lax.rem(mc + d, c) for a, b, d in steps]


def all_sum(value, n):
    z, y, c = digits(n)
    total = value
    for slow in range(1, z):
        total = total + shift(value, n, slow, 0, 0)
    return [total] + [shift(total, n, 0, a, b) for a, b in ((0, 1), (1, 0), (1, 1))]


def over_columns(row):
    return jnp.transpose(jnp.broadcast_to(row, (8, row.shape[1])))[:, :1]


def over_lanes(x):
    x = sum(x[:, i : i + 128] for i in range(0, x.shape[1], 128))
    return jnp.sum(jnp.transpose(x), axis=0, keepdims=True)


def fold(x):
    return jnp.sum(x.reshape(x.shape[0] // 8, 8, x.shape[1]), axis=0)


def update(grad, one, two):
    first = 9.0 * one.astype(jnp.float32) + grad
    second = 19.0 * two.astype(jnp.float32) + grad * grad
    over = lax.rsqrt(second)
    inv = pltpu.reciprocal(second * over + 1e-08 / 0.05**0.5, approx=True)
    return over, inv, first * inv


def replay_kernel(steps, *refs):
    n = len(steps)
    parts, far = refs[:n], refs[n : n + 6]
    (adjoint, turned, along, across, bend, stats) = refs[n + 6 : n + 12]
    (tokens, scaled, score, g0, g1, a0, a1, b0, b1, sums) = refs[n + 12 : n + 22]
    (weight, one, two, cot, token_weight, part_sem, tile_sem) = refs[n + 22 :]
    grads, firsts, seconds = (g0, g1), (a0, a1), (b0, b1)
    height, depth = parts[0].shape
    count, width = cot.shape
    tiles = depth // TILE

    def span(i):
        return pl.ds(pl.multiple_of(i * TILE, TILE), TILE)

    places = owners(n, steps)

    def part_copy(part):
        at = pl.multiple_of(places[part] * height, height)
        return pltpu.make_async_copy(parts[part], tokens.at[pl.ds(at, height), :], part_sem.at[part])

    near = (weight, one, two, adjoint)

    def tile_copy(which, i):
        return pltpu.make_async_copy(far[which].at[span(i), :], near[which].at[span(i), :], tile_sem.at[which, i])

    small = [
        pltpu.make_async_copy(far[4 + k], ref, part_sem.at[n + k]) for k, ref in enumerate((cot, token_weight))
    ]

    for part in range(n):
        part_copy(part).start()
    for i in range(tiles):
        tile_copy(0, i).start()
    for i in range(tiles):
        for which in (1, 2, 3):
            tile_copy(which, i).start()
    for copy in small:
        copy.start()
    for part in range(n):
        part_copy(part).wait()

    along[...] = jnp.zeros_like(along)
    across[...] = jnp.zeros_like(across)

    def gate_step(i, _):
        tile_copy(0, i).wait()
        here = tokens[:, span(i)]
        along[...] += f32dot(here, weight[span(i), :])
        turned[span(i), :] = here.T
        return 0

    lax.fori_loop(0, tiles, gate_step, 0)

    gate = along[...]
    for copy in small:
        copy.wait()
    weights = over_columns(token_weight[...])
    cot_f = cot[...].astype(jnp.float32)
    sig = 1.0 / (1.0 + jnp.exp(-gate))
    slope = sig * (1.0 + gate * (1.0 - sig))
    curve = sig * (1.0 - sig) * (2.0 + gate * (1.0 - 2.0 * sig))
    scaled[...] = (weights * cot_f * slope).astype(jnp.bfloat16)
    bend[...] = weights * cot_f * curve
    score[...] = cot_f * slope
    along[...] = jnp.zeros_like(along)

    def grad_tile(i, slot):
        grads[slot][...] = f32dot(turned[span(i), :], scaled[...])

    def probe_tile(i, slot):
        here = tokens[:, span(i)]
        along[...] += f32dot(here, firsts[slot][...])
        across[...] += f32dot(here, seconds[slot][...])

    def rows_of(i, slot, r):
        at = pl.ds(pl.multiple_of(i * TILE + r, ROWS), ROWS)
        return grads[slot][r : r + ROWS, :], one[at, :], two[at, :], adjoint[at, :]

    def arrive(i):
        for which in (1, 2, 3):
            tile_copy(which, i).wait()

    grad_tile(0, 0)
    arrive(0)
    sq = jnp.zeros((8, width), jnp.float32)
    cross = jnp.zeros((8, width), jnp.float32)
    for r in range(0, SAMPLE, ROWS):
        g, m1, m2, adj = rows_of(0, 0, r)
        _, _, upd = update(g, m1, m2)
        sq += fold(upd * upd)
        cross += fold(adj * upd)
    sq = jnp.sum(sq, keepdims=True)
    clipped = sq * RATIO**2 > float(SAMPLE * width)
    guess = jnp.where(clipped, jnp.sum(cross, keepdims=True) / jnp.maximum(sq, 1.0), 0.0)

    sums[...] = jnp.zeros_like(sums)

    def update_tile(i, slot):
        if not isinstance(i, int) or i > 0:
            arrive(i)
        sq, cross = sums[0], sums[1]
        for r in range(0, TILE, ROWS):
            g, m1, m2, adj = rows_of(i, slot, r)
            over, inv, upd = update(g, m1, m2)
            sq += fold(upd * upd)
            cross += fold(adj * upd)
            pull = inv * (1.0 - g * (upd * over))
            firsts[slot][r : r + ROWS, :] = ((adj - guess * upd) * pull).astype(jnp.bfloat16)
            seconds[slot][r : r + ROWS, :] = (upd * pull).astype(jnp.bfloat16)
        sums[0] = sq
        sums[1] = cross

    grad_tile(1, 1)
    update_tile(0, 0)

    def pair(k, _):
        i = 2 * k + 1
        for j, slot in ((0, 1), (1, 0)):
            grad_tile(i + j + 1, 1 - slot)
            update_tile(i + j, slot)
            probe_tile(i + j - 1, 1 - slot)
        return 0

    lax.fori_loop(0, tiles // 2 - 1, pair, 0)
    update_tile(tiles - 1, 1)
    probe_tile(tiles - 2, 0)
    probe_tile(tiles - 1, 1)

    b = score[...] * across[...]
    a = score[...] * along[...] + guess * b
    whole = lambda x: jnp.broadcast_to(jnp.sum(x, keepdims=True), (1, count))
    stats[0:1, :] = RATIO * over_lanes(a)
    stats[1:2, :] = RATIO**2 * over_lanes(b)
    stats[2:3, :] = RATIO**2 * whole(sums[0])
    stats[3:4, :] = RATIO * whole(sums[1])
    stats[4:8, :] = jnp.broadcast_to(guess, (4, count))


def replay_call(parts, weight, cot, token_weight, one, two, adjoint):
    steps = list(parts)
    n = len(steps)
    depth = weight.shape[0]
    count, width = cot.shape
    vmem = pl.BlockSpec(memory_space=pltpu.VMEM)
    far = pl.BlockSpec(memory_space=pl.ANY)
    block = lambda dtype: pltpu.VMEM((TILE, width), dtype)
    whole = lambda dtype: pltpu.VMEM((depth, width), dtype)
    return pl.pallas_call(
        functools.partial(replay_kernel, steps),
        in_specs=[far] * (n + 6),
        out_specs=[vmem] * 6,
        out_shape=[
            pltpu.VMEM((depth, width), jnp.float32),
            pltpu.VMEM((depth, count), jnp.bfloat16),
            pltpu.VMEM((count, width), jnp.float32),
            pltpu.VMEM((count, width), jnp.float32),
            pltpu.VMEM((count, width), jnp.float32),
            pltpu.VMEM((8, count), jnp.float32),
        ],
        scratch_shapes=[
            pltpu.VMEM((count, depth), jnp.bfloat16),
            pltpu.VMEM((count, width), jnp.bfloat16),
            pltpu.VMEM((count, width), jnp.float32),
            block(jnp.float32),
            block(jnp.float32),
            block(jnp.bfloat16),
            block(jnp.bfloat16),
            block(jnp.bfloat16),
            block(jnp.bfloat16),
            pltpu.VMEM((2, 8, width), jnp.float32),
            whole(jnp.bfloat16),
            whole(jnp.bfloat16),
            whole(jnp.bfloat16),
            pltpu.VMEM((count, width), jnp.bfloat16),
            pltpu.VMEM((1, count), jnp.float32),
            pltpu.SemaphoreType.DMA((n + 2,)),
            pltpu.SemaphoreType.DMA((4, depth // TILE)),
        ],
        compiler_params=pltpu.CompilerParams(vmem_limit_bytes=VMEM_BYTES),
        name="replay",
    )(
        *[in_hbm(x) if step == (0, 0, 0) else x for step, x in parts.items()],
        *[in_hbm(x) for x in (weight, one, two, adjoint, cot, token_weight)],
    )


def in_hbm(x):
    return pltpu.with_memory_space_constraint(x, pltpu.HBM)


def theta_kernel(n, entries, s0, s1, s2, s3, own, along, across, bend, turned, adjoint, theta, scores, ready, sent):
    total = s0[...] + s1[...] + (s2[...] + s3[...])
    sq, cross = total[2:3, 0:1], total[3:4, 0:1]
    rms = jnp.sqrt(sq / entries)
    scale = 1.0 / jnp.maximum(1.0, rms)
    bind = jnp.where(rms > 1.0, 1.0 / (rms * rms * rms), 0.0)
    lead = -0.01 * scale
    rest = 0.01 * cross * bind / entries
    mine = lead * total[0:8, :] + rest * pltpu.roll(total, 7, 0)
    count = total.shape[1]
    height = count // n
    mine = pltpu.roll(mine, lax.rem(count - lax.axis_index("dp") * height, count), 1)
    scores[...] = mine[0:1, 0:height]
    lead_here = RATIO * lead
    rest_here = RATIO**2 * rest + lead_here * own[4:5, 0:1]
    bent = (bend[...] * (lead_here * along[...] + rest_here * across[...])).astype(jnp.bfloat16)

    def copy(i):
        at = pl.ds(i * TILE, TILE)
        return pltpu.make_async_copy(ready.at[at, :], theta.at[at, :], sent.at[i])

    tiles = theta.shape[0] // TILE
    for i in range(tiles):
        at = pl.ds(i * TILE, TILE)
        ready[at, :] = 0.999 * adjoint[at, :] + f32dot(turned[at, :], bent)
        copy(i).start()
    for i in range(tiles):
        copy(i).wait()


def theta_call(n, entries, sums, own, along, across, bend, turned, adjoint):
    depth, width = adjoint.shape
    count = turned.shape[1]
    vmem = pl.BlockSpec(memory_space=pltpu.VMEM)
    return pl.pallas_call(
        functools.partial(theta_kernel, n, entries),
        in_specs=[vmem] * 10,
        out_specs=[pl.BlockSpec(memory_space=pl.ANY), vmem],
        out_shape=[
            jax.ShapeDtypeStruct((depth, width), jnp.float32),
            jax.ShapeDtypeStruct((1, count // n), jnp.float32),
        ],
        scratch_shapes=[pltpu.VMEM((depth, width), jnp.float32), pltpu.SemaphoreType.DMA((depth // TILE,))],
        compiler_params=pltpu.CompilerParams(vmem_limit_bytes=VMEM_BYTES),
        name="theta",
    )(*sums, own, along, across, bend, turned, adjoint)


def shards(n, tokens, cotangent, token_weight, weight, moment_one, moment_two, adjoint):
    entries = float(adjoint.shape[0] * adjoint.shape[1] * n)
    parts = gather(tokens, n)
    adjoint_near, turned, along, across, bend, stats = replay_call(
        parts, weight, cotangent, token_weight.reshape(1, -1), moment_one, moment_two, adjoint
    )
    sums = all_sum(stats, n)
    theta_bar, scores = theta_call(n, entries, sums, stats, along, across, bend, turned, adjoint_near)
    return (theta_bar, scores.reshape(-1))


def solution(mesh):
    in_specs = (
        P(("group", "dp"), None),
        P("group", "dp"),
        P("group"),
        P(None, "dp"),
        P(None, "dp"),
        P(None, "dp"),
        P(None, "dp"),
    )
    out_specs = (P("group", "dp"), P(("group", "dp")))
    body = functools.partial(shards, mesh.shape["dp"])
    return jax.shard_map(body, mesh=mesh, in_specs=in_specs, out_specs=out_specs, check_vma=False)
```

```python
import functools

import jax
import jax.numpy as jnp
from jax import lax
from jax.experimental import pallas as pl
from jax.experimental.pallas import tpu as pltpu
from jax.sharding import PartitionSpec as P

TILE = 512
ROWS = 16
SAMPLE = 256
VMEM_BYTES = 12 << 20
RATIO = 0.1 / 0.05**0.5


def f32dot(a, b):
    return jnp.dot(a, b, preferred_element_type=jnp.float32)


def digits(n):
    return (n // 4, 2, 2)


def shift(value, n, slow, mid, core):
    z, y, c = digits(n)
    pairs = []
    for d in range(n):
        dz, dy, dc = d // (y * c), d // c % y, d % c
        source = ((dz + slow) % z * y + (dy + mid) % y) * c + (dc + core) % c
        pairs.append((source, d))
    return lax.ppermute(value, "dp", pairs)


def ring(n):
    chips = n // 2
    return [*range(0, chips, 2), *range(chips - 1 - chips % 2, 0, -2)]


def along_ring(value, n, way):
    order = ring(n)
    pairs = []
    for i, chip in enumerate(order):
        source = order[(i - way) % len(order)]
        pairs += [(2 * source + core, 2 * chip + core) for core in (0, 1)]
    return lax.ppermute(value, "dp", pairs)


def gather(tokens, n, errands):
    parts = {(0, 0): tokens}
    chips = n // 2
    done = []
    token = None
    for hop in range(1, chips // 2 + 1):
        for way in (1, -1):
            if 2 * hop == chips and way == -1:
                continue
            here = parts[way * (hop - 1), 0]
            if token is not None:
                here = lax.optimization_barrier((here, token))[0]
            parts[way * hop, 0] = along_ring(here, n, way)
        token = None
        if errands[len(done) :]:
            result, token = errands[len(done)](parts[hop - 1, 0])
            done.append(result)
    for back, core in list(parts):
        parts[back, 1] = shift(parts[back, core], n, 0, 0, 1)
    return parts, done


def owners(n, steps):
    order = ring(n)
    me = lax.axis_index("dp")
    chip, core = me // 2, lax.rem(me, 2)
    at = jnp.where(lax.rem(chip, 2) == 0, chip // 2, n // 2 - 1 - chip // 2)
    places = []
    for back, other in steps:
        there = lax.rem(at - back + len(order), len(order))
        up = len(order) // 2
        source = jnp.where(there < up, 2 * there, 2 * (len(order) - 1 - there) + 1)
        places.append(2 * source + lax.rem(core + other, 2))
    return places


def all_sum(value, n):
    z, y, c = digits(n)
    total = value
    for slow in range(1, z):
        total = total + shift(value, n, slow, 0, 0)
    return [total] + [shift(total, n, 0, a, b) for a, b in ((0, 1), (1, 0), (1, 1))]


def over_columns(row):
    return jnp.transpose(jnp.broadcast_to(row, (8, row.shape[1])))[:, :1]


def over_lanes(x):
    x = sum(x[:, i : i + 128] for i in range(0, x.shape[1], 128))
    return jnp.sum(jnp.transpose(x), axis=0, keepdims=True)


def fold(x):
    return jnp.sum(x.reshape(x.shape[0] // 8, 8, x.shape[1]), axis=0)


def update(grad, one, two):
    first = one + grad
    second = two + grad * grad
    over = lax.rsqrt(second)
    inv = pltpu.reciprocal(second * over + 1e-08 / 0.05**0.5, approx=True)
    return over, inv, first * inv


def fetch_kernel(factor, far, after, near, token, raw, sem):
    target = near if factor is None else raw
    tiles = far.shape[0] // TILE

    def copy(i):
        at = pl.ds(pl.multiple_of(i * TILE, TILE), TILE)
        return pltpu.make_async_copy(far.at[at, :], target.at[at, :], sem.at[i])

    for i in range(tiles):
        copy(i).start()
    token[...] = jnp.zeros_like(token)

    def widen(i, _):
        copy(i).wait()
        if factor is not None:
            at = pl.ds(pl.multiple_of(i * TILE, TILE), TILE)
            near[at, :] = factor * raw[at, :].astype(jnp.float32)
        return 0

    lax.fori_loop(0, tiles, widen, 0)


def fetch(x, after, factor=None):
    dtype = x.dtype if factor is None else jnp.float32
    raw = (8, 128) if factor is None else x.shape
    return pl.pallas_call(
        functools.partial(fetch_kernel, factor),
        in_specs=[pl.BlockSpec(memory_space=pl.ANY)] * 2,
        out_specs=[pl.BlockSpec(memory_space=pltpu.VMEM)] * 2,
        out_shape=[pltpu.VMEM(x.shape, dtype), jax.ShapeDtypeStruct((8, 128), jnp.float32)],
        scratch_shapes=[pltpu.VMEM(raw, x.dtype), pltpu.SemaphoreType.DMA((x.shape[0] // TILE,))],
        compiler_params=pltpu.CompilerParams(vmem_limit_bytes=VMEM_BYTES),
        cost_estimate=pl.CostEstimate(flops=0, bytes_accessed=8 << 20, transcendentals=0),
        name="fetch",
    )(in_hbm(x), after)


def replay_kernel(steps, *refs):
    n = len(steps)
    parts, far = refs[:n], refs[n : n + 2]
    (weight, one, two, adjoint) = refs[n + 2 : n + 6]
    (turned, along, across, bend, stats) = refs[n + 6 : n + 11]
    (tokens, scaled, score, g0, g1, a0, a1, b0, b1, sums, cot, token_weight, part_sem) = refs[n + 11 :]
    grads, firsts, seconds = (g0, g1), (a0, a1), (b0, b1)
    height, depth = parts[0].shape
    count, width = cot.shape
    tiles = depth // TILE

    def span(i):
        return pl.ds(pl.multiple_of(i * TILE, TILE), TILE)

    places = owners(n, steps)

    def part_copy(part):
        at = pl.multiple_of(places[part] * height, height)
        return pltpu.make_async_copy(parts[part], tokens.at[pl.ds(at, height), :], part_sem.at[part])

    small = [
        pltpu.make_async_copy(far[k], ref, part_sem.at[n + k]) for k, ref in enumerate((cot, token_weight))
    ]

    for part in range(n):
        part_copy(part).start()
    for copy in small:
        copy.start()
    for part in range(n):
        part_copy(part).wait()

    along[...] = jnp.zeros_like(along)
    across[...] = jnp.zeros_like(across)

    def gate_step(i, _):
        here = tokens[:, span(i)]
        along[...] += f32dot(here, weight[span(i), :])
        turned[span(i), :] = here.T
        return 0

    lax.fori_loop(0, tiles, gate_step, 0)

    gate = along[...]
    for copy in small:
        copy.wait()
    weights = over_columns(token_weight[...])
    cot_f = cot[...].astype(jnp.float32)
    sig = 1.0 / (1.0 + jnp.exp(-gate))
    slope = sig * (1.0 + gate * (1.0 - sig))
    curve = sig * (1.0 - sig) * (2.0 + gate * (1.0 - 2.0 * sig))
    scaled[...] = (weights * cot_f * slope).astype(jnp.bfloat16)
    bend[...] = weights * cot_f * curve
    score[...] = cot_f * slope
    along[...] = jnp.zeros_like(along)

    def grad_tile(i, slot):
        grads[slot][...] = f32dot(turned[span(i), :], scaled[...])

    def probe_tile(i, slot):
        here = tokens[:, span(i)]
        along[...] += f32dot(here, firsts[slot][...])
        across[...] += f32dot(here, seconds[slot][...])

    def rows_of(i, slot, r):
        at = pl.ds(pl.multiple_of(i * TILE + r, ROWS), ROWS)
        return grads[slot][r : r + ROWS, :], one[at, :], two[at, :], adjoint[at, :]

    grad_tile(0, 0)
    sq = jnp.zeros((8, width), jnp.float32)
    cross = jnp.zeros((8, width), jnp.float32)
    for r in range(0, SAMPLE, ROWS):
        g, m1, m2, adj = rows_of(0, 0, r)
        _, _, upd = update(g, m1, m2)
        sq += fold(upd * upd)
        cross += fold(adj * upd)
    sq = jnp.sum(sq, keepdims=True)
    clipped = sq * RATIO**2 > float(SAMPLE * width)
    guess = jnp.where(clipped, jnp.sum(cross, keepdims=True) / jnp.maximum(sq, 1.0), 0.0)

    sums[...] = jnp.zeros_like(sums)

    def update_tile(i, slot):
        sq, cross = sums[0], sums[1]
        for r in range(0, TILE, ROWS):
            g, m1, m2, adj = rows_of(i, slot, r)
            over, inv, upd = update(g, m1, m2)
            sq += fold(upd * upd)
            cross += fold(adj * upd)
            pull = inv * (1.0 - g * (upd * over))
            firsts[slot][r : r + ROWS, :] = ((adj - guess * upd) * pull).astype(jnp.bfloat16)
            seconds[slot][r : r + ROWS, :] = (upd * pull).astype(jnp.bfloat16)
        sums[0] = sq
        sums[1] = cross

    grad_tile(1, 1)
    update_tile(0, 0)

    def pair(k, _):
        i = 2 * k + 1
        for j, slot in ((0, 1), (1, 0)):
            grad_tile(i + j + 1, 1 - slot)
            update_tile(i + j, slot)
            probe_tile(i + j - 1, 1 - slot)
        return 0

    lax.fori_loop(0, tiles // 2 - 1, pair, 0)
    update_tile(tiles - 1, 1)
    probe_tile(tiles - 2, 0)
    probe_tile(tiles - 1, 1)

    b = score[...] * across[...]
    a = score[...] * along[...] + guess * b
    whole = lambda x: jnp.broadcast_to(jnp.sum(x, keepdims=True), (1, count))
    stats[0:1, :] = RATIO * over_lanes(a)
    stats[1:2, :] = RATIO**2 * over_lanes(b)
    stats[2:3, :] = RATIO**2 * whole(sums[0])
    stats[3:4, :] = RATIO * whole(sums[1])
    stats[4:8, :] = jnp.broadcast_to(guess, (4, count))


def replay_call(parts, cot, token_weight, weight, one, two, adjoint):
    steps = list(parts)
    n = len(steps)
    depth = weight.shape[0]
    count, width = cot.shape
    vmem = pl.BlockSpec(memory_space=pltpu.VMEM)
    far = pl.BlockSpec(memory_space=pl.ANY)
    block = lambda dtype: pltpu.VMEM((TILE, width), dtype)
    return pl.pallas_call(
        functools.partial(replay_kernel, steps),
        in_specs=[far] * (n + 2) + [vmem] * 4,
        out_specs=[vmem] * 5,
        out_shape=[
            pltpu.VMEM((depth, count), jnp.bfloat16),
            pltpu.VMEM((count, width), jnp.float32),
            pltpu.VMEM((count, width), jnp.float32),
            pltpu.VMEM((count, width), jnp.float32),
            pltpu.VMEM((8, count), jnp.float32),
        ],
        scratch_shapes=[
            pltpu.VMEM((count, depth), jnp.bfloat16),
            pltpu.VMEM((count, width), jnp.bfloat16),
            pltpu.VMEM((count, width), jnp.float32),
            block(jnp.float32),
            block(jnp.float32),
            block(jnp.bfloat16),
            block(jnp.bfloat16),
            block(jnp.bfloat16),
            block(jnp.bfloat16),
            pltpu.VMEM((2, 8, width), jnp.float32),
            pltpu.VMEM((count, width), jnp.bfloat16),
            pltpu.VMEM((1, count), jnp.float32),
            pltpu.SemaphoreType.DMA((n + 2,)),
        ],
        compiler_params=pltpu.CompilerParams(vmem_limit_bytes=VMEM_BYTES),
        name="replay",
    )(
        *[in_hbm(x) if step == (0, 0) else x for step, x in parts.items()],
        *[in_hbm(x) for x in (cot, token_weight)],
        weight,
        one,
        two,
        adjoint,
    )


def in_hbm(x):
    return pltpu.with_memory_space_constraint(x, pltpu.HBM)


def theta_kernel(n, entries, s0, s1, s2, s3, own, along, across, bend, turned, adjoint, theta, scores, ready, sent):
    total = s0[...] + s1[...] + (s2[...] + s3[...])
    sq, cross = total[2:3, 0:1], total[3:4, 0:1]
    rms = jnp.sqrt(sq / entries)
    scale = 1.0 / jnp.maximum(1.0, rms)
    bind = jnp.where(rms > 1.0, 1.0 / (rms * rms * rms), 0.0)
    lead = -0.01 * scale
    rest = 0.01 * cross * bind / entries
    mine = lead * total[0:8, :] + rest * pltpu.roll(total, 7, 0)
    count = total.shape[1]
    height = count // n
    mine = pltpu.roll(mine, lax.rem(count - lax.axis_index("dp") * height, count), 1)
    scores[...] = mine[0:1, 0:height]
    lead_here = RATIO * lead
    rest_here = RATIO**2 * rest + lead_here * own[4:5, 0:1]
    bent = (bend[...] * (lead_here * along[...] + rest_here * across[...])).astype(jnp.bfloat16)

    def copy(i):
        at = pl.ds(i * TILE, TILE)
        return pltpu.make_async_copy(ready.at[at, :], theta.at[at, :], sent.at[i])

    tiles = theta.shape[0] // TILE
    for i in range(tiles):
        at = pl.ds(i * TILE, TILE)
        ready[at, :] = 0.999 * adjoint[at, :] + f32dot(turned[at, :], bent)
        copy(i).start()
    for i in range(tiles):
        copy(i).wait()


def theta_call(n, entries, sums, own, along, across, bend, turned, adjoint):
    depth, width = adjoint.shape
    count = turned.shape[1]
    vmem = pl.BlockSpec(memory_space=pltpu.VMEM)
    return pl.pallas_call(
        functools.partial(theta_kernel, n, entries),
        in_specs=[vmem] * 10,
        out_specs=[pl.BlockSpec(memory_space=pl.ANY), vmem],
        out_shape=[
            jax.ShapeDtypeStruct((depth, width), jnp.float32),
            jax.ShapeDtypeStruct((1, count // n), jnp.float32),
        ],
        scratch_shapes=[pltpu.VMEM((depth, width), jnp.float32), pltpu.SemaphoreType.DMA((depth // TILE,))],
        compiler_params=pltpu.CompilerParams(vmem_limit_bytes=VMEM_BYTES),
        name="theta",
    )(*sums, own, along, across, bend, turned, adjoint)


def shards(n, tokens, cotangent, token_weight, weight, moment_one, moment_two, adjoint):
    entries = float(adjoint.shape[0] * adjoint.shape[1] * n)
    errands = [
        lambda after: fetch(weight, after),
        lambda after: fetch(moment_one, after, 9.0),
        lambda after: fetch(moment_two, after, 19.0),
        lambda after: fetch(adjoint, after),
    ]
    parts, (weight_near, one, two, adjoint_near) = gather(tokens, n, errands)
    turned, along, across, bend, stats = replay_call(
        parts, cotangent, token_weight.reshape(1, -1), weight_near, one, two, adjoint_near
    )
    sums = all_sum(stats, n)
    theta_bar, scores = theta_call(n, entries, sums, stats, along, across, bend, turned, adjoint_near)
    return (theta_bar, scores.reshape(-1))


def solution(mesh):
    in_specs = (
        P(("group", "dp"), None),
        P("group", "dp"),
        P("group"),
        P(None, "dp"),
        P(None, "dp"),
        P(None, "dp"),
        P(None, "dp"),
    )
    out_specs = (P("group", "dp"), P(("group", "dp")))
    body = functools.partial(shards, mesh.shape["dp"])
    return jax.shard_map(body, mesh=mesh, in_specs=in_specs, out_specs=out_specs, check_vma=False)
```

```python
import functools

import jax
import jax.numpy as jnp
from jax import lax
from jax.experimental import pallas as pl
from jax.experimental.pallas import tpu as pltpu
from jax.sharding import PartitionSpec as P

TILE = 512
ROWS = 16
SAMPLE = 256
VMEM_BYTES = 16 << 20
RATIO = 0.1 / 0.05**0.5


def f32dot(a, b):
    return jnp.dot(a, b, preferred_element_type=jnp.float32)


def swapped(value, n, mask):
    return lax.ppermute(value, "dp", [(d ^ mask, d) for d in range(n)])


def ring(n):
    chips = n // 2
    return [*range(0, chips, 2), *range(chips - 1 - chips % 2, 0, -2)]


def along_ring(value, n, way):
    order = ring(n)
    pairs = []
    for i, chip in enumerate(order):
        source = order[(i - way) % len(order)]
        pairs += [(2 * source + core, 2 * chip + core) for core in (0, 1)]
    return lax.ppermute(value, "dp", pairs)


def gather(tokens, n, errands):
    parts = {(0, 0): tokens}
    chips = n // 2
    done = []
    token = None
    for hop in range(1, chips // 2 + 1):
        for way in (1, -1):
            if 2 * hop == chips and way == -1:
                continue
            here = parts[way * (hop - 1), 0]
            if token is not None:
                here = lax.optimization_barrier((here, token))[0]
            parts[way * hop, 0] = along_ring(here, n, way)
        token = None
        if errands[len(done) :]:
            result, token = errands[len(done)](parts[hop - 1, 0])
            done.append(result)
    for back, core in list(parts):
        parts[back, 1] = swapped(parts[back, core], n, 1)
    return parts, done


def owners(n, steps):
    order = ring(n)
    me = lax.axis_index("dp")
    chip, core = me // 2, lax.rem(me, 2)
    at = jnp.where(lax.rem(chip, 2) == 0, chip // 2, n // 2 - 1 - chip // 2)
    places = []
    for back, other in steps:
        there = lax.rem(at - back + len(order), len(order))
        up = len(order) // 2
        source = jnp.where(there < up, 2 * there, 2 * (len(order) - 1 - there) + 1)
        places.append(2 * source + lax.rem(core + other, 2))
    return places


def all_sum(value, n):
    total = value
    for mask in range(4, n, 4):
        total = total + swapped(value, n, mask)
    return [total] + [swapped(total, n, mask) for mask in (1, 2, 3)]


def over_columns(row):
    return jnp.transpose(jnp.broadcast_to(row, (8, row.shape[1])))[:, :1]


def over_lanes(x):
    x = sum(x[:, i : i + 128] for i in range(0, x.shape[1], 128))
    return jnp.sum(jnp.transpose(x), axis=0, keepdims=True)


def fold(x):
    return jnp.sum(x.reshape(x.shape[0] // 8, 8, x.shape[1]), axis=0)


def update(grad, one, two):
    first = one + grad
    second = 19.0 * two.astype(jnp.float32) + grad * grad
    over = lax.rsqrt(second)
    inv = pltpu.reciprocal(second * over + 1e-08 / 0.05**0.5, approx=True)
    return over, inv, first * inv


def fetch_kernel(factor, far, after, near, token, raw, sem):
    target = near if factor is None else raw
    tiles = far.shape[0] // TILE

    def copy(i):
        at = pl.ds(pl.multiple_of(i * TILE, TILE), TILE)
        return pltpu.make_async_copy(far.at[at, :], target.at[at, :], sem.at[i])

    for i in range(tiles):
        copy(i).start()
    token[...] = jnp.zeros_like(token)

    def widen(i, _):
        copy(i).wait()
        if factor is not None:
            at = pl.ds(pl.multiple_of(i * TILE, TILE), TILE)
            near[at, :] = factor * raw[at, :].astype(jnp.float32)
        return 0

    lax.fori_loop(0, tiles, widen, 0)


def fetch(x, after, factor=None):
    dtype = x.dtype if factor is None else jnp.float32
    raw = (8, 128) if factor is None else x.shape
    return pl.pallas_call(
        functools.partial(fetch_kernel, factor),
        in_specs=[pl.BlockSpec(memory_space=pl.ANY)] * 2,
        out_specs=[pl.BlockSpec(memory_space=pltpu.VMEM)] * 2,
        out_shape=[pltpu.VMEM(x.shape, dtype), jax.ShapeDtypeStruct((8, 128), jnp.float32)],
        scratch_shapes=[pltpu.VMEM(raw, x.dtype), pltpu.SemaphoreType.DMA((x.shape[0] // TILE,))],
        compiler_params=pltpu.CompilerParams(vmem_limit_bytes=VMEM_BYTES),
        cost_estimate=pl.CostEstimate(flops=0, bytes_accessed=8 << 20, transcendentals=0),
        name="fetch",
    )(in_hbm(x), after)


def replay_kernel(steps, *refs):
    n = len(steps)
    parts, far, (weight, one) = refs[:n], refs[n : n + 4], refs[n + 4 : n + 6]
    (adjoint, turned, along, across, bend, stats) = refs[n + 6 : n + 12]
    (tokens, scaled, score, g0, g1, a0, a1, b0, b1, sums) = refs[n + 12 : n + 22]
    (two, cot, token_weight, part_sem, tile_sem) = refs[n + 22 :]
    grads, firsts, seconds = (g0, g1), (a0, a1), (b0, b1)
    height, depth = parts[0].shape
    count, width = cot.shape
    tiles = depth // TILE

    def span(i):
        return pl.ds(pl.multiple_of(i * TILE, TILE), TILE)

    places = owners(n, steps)

    def part_copy(part):
        at = pl.multiple_of(places[part] * height, height)
        return pltpu.make_async_copy(parts[part], tokens.at[pl.ds(at, height), :], part_sem.at[part])

    small = [
        pltpu.make_async_copy(far[k], ref, part_sem.at[n + k]) for k, ref in enumerate((cot, token_weight))
    ]

    near = (two, adjoint)

    def tile_copy(which, i):
        return pltpu.make_async_copy(far[2 + which].at[span(i), :], near[which].at[span(i), :], tile_sem.at[which, i])

    for part in range(n):
        part_copy(part).start()
    for copy in small:
        copy.start()
    for part in range(n):
        part_copy(part).wait()

    along[...] = jnp.zeros_like(along)
    across[...] = jnp.zeros_like(across)

    def gate_step(i, _):
        tile_copy(0, i).start()
        tile_copy(1, i).start()
        here = tokens[:, span(i)]
        along[...] += f32dot(here, weight[span(i), :])
        turned[span(i), :] = here.T
        return 0

    lax.fori_loop(0, tiles, gate_step, 0)

    gate = along[...]
    for copy in small:
        copy.wait()
    weights = over_columns(token_weight[...])
    cot_f = cot[...].astype(jnp.float32)
    sig = 1.0 / (1.0 + jnp.exp(-gate))
    slope = sig * (1.0 + gate * (1.0 - sig))
    curve = sig * (1.0 - sig) * (2.0 + gate * (1.0 - 2.0 * sig))
    scaled[...] = (weights * cot_f * slope).astype(jnp.bfloat16)
    bend[...] = weights * cot_f * curve
    score[...] = cot_f * slope
    along[...] = jnp.zeros_like(along)

    def grad_tile(i, slot):
        grads[slot][...] = f32dot(turned[span(i), :], scaled[...])

    def probe_tile(i, slot):
        here = tokens[:, span(i)]
        along[...] += f32dot(here, firsts[slot][...])
        across[...] += f32dot(here, seconds[slot][...])

    def rows_of(i, slot, r):
        at = pl.ds(pl.multiple_of(i * TILE + r, ROWS), ROWS)
        return grads[slot][r : r + ROWS, :], one[at, :], two[at, :], adjoint[at, :]

    def arrive(i):
        tile_copy(0, i).wait()
        tile_copy(1, i).wait()

    grad_tile(0, 0)
    arrive(0)
    sq = jnp.zeros((8, width), jnp.float32)
    cross = jnp.zeros((8, width), jnp.float32)
    for r in range(0, SAMPLE, ROWS):
        g, m1, m2, adj = rows_of(0, 0, r)
        _, _, upd = update(g, m1, m2)
        sq += fold(upd * upd)
        cross += fold(adj * upd)
    sq = jnp.sum(sq, keepdims=True)
    clipped = sq * RATIO**2 > float(SAMPLE * width)
    guess = jnp.where(clipped, jnp.sum(cross, keepdims=True) / jnp.maximum(sq, 1.0), 0.0)

    sums[...] = jnp.zeros_like(sums)

    def update_tile(i, slot):
        if not isinstance(i, int) or i > 0:
            arrive(i)
        sq, cross = sums[0], sums[1]
        for r in range(0, TILE, ROWS):
            g, m1, m2, adj = rows_of(i, slot, r)
            over, inv, upd = update(g, m1, m2)
            sq += fold(upd * upd)
            cross += fold(adj * upd)
            pull = inv * (1.0 - g * (upd * over))
            firsts[slot][r : r + ROWS, :] = ((adj - guess * upd) * pull).astype(jnp.bfloat16)
            seconds[slot][r : r + ROWS, :] = (upd * pull).astype(jnp.bfloat16)
        sums[0] = sq
        sums[1] = cross

    grad_tile(1, 1)
    update_tile(0, 0)

    def pair(k, _):
        i = 2 * k + 1
        for j, slot in ((0, 1), (1, 0)):
            grad_tile(i + j + 1, 1 - slot)
            update_tile(i + j, slot)
            probe_tile(i + j - 1, 1 - slot)
        return 0

    lax.fori_loop(0, tiles // 2 - 1, pair, 0)
    update_tile(tiles - 1, 1)
    probe_tile(tiles - 2, 0)
    probe_tile(tiles - 1, 1)

    b = score[...] * across[...]
    a = score[...] * along[...] + guess * b
    whole = lambda x: jnp.broadcast_to(jnp.sum(x, keepdims=True), (1, count))
    stats[0:1, :] = RATIO * over_lanes(a)
    stats[1:2, :] = RATIO**2 * over_lanes(b)
    stats[2:3, :] = RATIO**2 * whole(sums[0])
    stats[3:4, :] = RATIO * whole(sums[1])
    stats[4:8, :] = jnp.broadcast_to(guess, (4, count))


def replay_call(parts, cot, token_weight, two, adjoint, weight, one):
    steps = list(parts)
    n = len(steps)
    depth = weight.shape[0]
    count, width = cot.shape
    vmem = pl.BlockSpec(memory_space=pltpu.VMEM)
    far = pl.BlockSpec(memory_space=pl.ANY)
    block = lambda dtype: pltpu.VMEM((TILE, width), dtype)
    return pl.pallas_call(
        functools.partial(replay_kernel, steps),
        in_specs=[far] * (n + 4) + [vmem] * 2,
        out_specs=[vmem] * 6,
        out_shape=[
            pltpu.VMEM((depth, width), jnp.float32),
            pltpu.VMEM((depth, count), jnp.bfloat16),
            pltpu.VMEM((count, width), jnp.float32),
            pltpu.VMEM((count, width), jnp.float32),
            pltpu.VMEM((count, width), jnp.float32),
            pltpu.VMEM((8, count), jnp.float32),
        ],
        scratch_shapes=[
            pltpu.VMEM((count, depth), jnp.bfloat16),
            pltpu.VMEM((count, width), jnp.bfloat16),
            pltpu.VMEM((count, width), jnp.float32),
            block(jnp.float32),
            block(jnp.float32),
            block(jnp.bfloat16),
            block(jnp.bfloat16),
            block(jnp.bfloat16),
            block(jnp.bfloat16),
            pltpu.VMEM((2, 8, width), jnp.float32),
            pltpu.VMEM((depth, width), jnp.bfloat16),
            pltpu.VMEM((count, width), jnp.bfloat16),
            pltpu.VMEM((1, count), jnp.float32),
            pltpu.SemaphoreType.DMA((n + 2,)),
            pltpu.SemaphoreType.DMA((2, depth // TILE)),
        ],
        compiler_params=pltpu.CompilerParams(vmem_limit_bytes=VMEM_BYTES),
        name="replay",
    )(
        *[in_hbm(x) if step == (0, 0) else x for step, x in parts.items()],
        *[in_hbm(x) for x in (cot, token_weight, two, adjoint)],
        weight,
        one,
    )


def in_hbm(x):
    return pltpu.with_memory_space_constraint(x, pltpu.HBM)


def theta_kernel(n, entries, s0, s1, s2, s3, own, along, across, bend, turned, adjoint, theta, scores, ready, sent):
    total = s0[...] + s1[...] + (s2[...] + s3[...])
    sq, cross = total[2:3, 0:1], total[3:4, 0:1]
    rms = jnp.sqrt(sq / entries)
    scale = 1.0 / jnp.maximum(1.0, rms)
    bind = jnp.where(rms > 1.0, 1.0 / (rms * rms * rms), 0.0)
    lead = -0.01 * scale
    rest = 0.01 * cross * bind / entries
    mine = lead * total[0:8, :] + rest * pltpu.roll(total, 7, 0)
    count = total.shape[1]
    height = count // n
    mine = pltpu.roll(mine, lax.rem(count - lax.axis_index("dp") * height, count), 1)
    scores[...] = mine[0:1, 0:height]
    lead_here = RATIO * lead
    rest_here = RATIO**2 * rest + lead_here * own[4:5, 0:1]
    bent = (bend[...] * (lead_here * along[...] + rest_here * across[...])).astype(jnp.bfloat16)

    def copy(i):
        at = pl.ds(i * TILE, TILE)
        return pltpu.make_async_copy(ready.at[at, :], theta.at[at, :], sent.at[i])

    tiles = theta.shape[0] // TILE
    for i in range(tiles):
        at = pl.ds(i * TILE, TILE)
        ready[at, :] = 0.999 * adjoint[at, :] + f32dot(turned[at, :], bent)
        copy(i).start()
    for i in range(tiles):
        copy(i).wait()


def theta_call(n, entries, sums, own, along, across, bend, turned, adjoint):
    depth, width = adjoint.shape
    count = turned.shape[1]
    vmem = pl.BlockSpec(memory_space=pltpu.VMEM)
    return pl.pallas_call(
        functools.partial(theta_kernel, n, entries),
        in_specs=[vmem] * 10,
        out_specs=[pl.BlockSpec(memory_space=pl.ANY), vmem],
        out_shape=[
            jax.ShapeDtypeStruct((depth, width), jnp.float32),
            jax.ShapeDtypeStruct((1, count // n), jnp.float32),
        ],
        scratch_shapes=[pltpu.VMEM((depth, width), jnp.float32), pltpu.SemaphoreType.DMA((depth // TILE,))],
        compiler_params=pltpu.CompilerParams(vmem_limit_bytes=VMEM_BYTES),
        name="theta",
    )(*sums, own, along, across, bend, turned, adjoint)


def shards(n, tokens, cotangent, token_weight, weight, moment_one, moment_two, adjoint):
    entries = float(adjoint.shape[0] * adjoint.shape[1] * n)
    errands = [
        lambda after: fetch(weight, after),
        lambda after: fetch(moment_one, after, 9.0),
    ]
    parts, (weight_near, one_near) = gather(tokens, n, errands)
    adjoint_near, turned, along, across, bend, stats = replay_call(
        parts, cotangent, token_weight.reshape(1, -1), moment_two, adjoint, weight_near, one_near
    )
    sums = all_sum(stats, n)
    theta_bar, scores = theta_call(n, entries, sums, stats, along, across, bend, turned, adjoint_near)
    return (theta_bar, scores.reshape(-1))


def solution(mesh):
    in_specs = (
        P(("group", "dp"), None),
        P("group", "dp"),
        P("group"),
        P(None, "dp"),
        P(None, "dp"),
        P(None, "dp"),
        P(None, "dp"),
    )
    out_specs = (P("group", "dp"), P(("group", "dp")))
    body = functools.partial(shards, mesh.shape["dp"])
    return jax.shard_map(body, mesh=mesh, in_specs=in_specs, out_specs=out_specs, check_vma=False)
```

```python
import functools

import jax
import jax.numpy as jnp
from jax import lax
from jax.experimental import pallas as pl
from jax.experimental.pallas import tpu as pltpu
from jax.sharding import PartitionSpec as P

TILE = 512
HALF = 256
ROWS = 16
COLUMNS = 256
SAMPLE = 256
VMEM_BYTES = 16 << 20
RATIO = 0.1 / 0.05**0.5


def f32dot(a, b):
    return jnp.dot(a, b, preferred_element_type=jnp.float32)


def swapped(value, n, mask):
    return lax.ppermute(value, "dp", [(d ^ mask, d) for d in range(n)])


def ring(n):
    chips = n // 2
    return [*range(0, chips, 2), *range(chips - 1 - chips % 2, 0, -2)]


def along_ring(value, n, way):
    order = ring(n)
    pairs = []
    for i, chip in enumerate(order):
        source = order[(i - way) % len(order)]
        pairs += [(2 * source + core, 2 * chip + core) for core in (0, 1)]
    return lax.ppermute(value, "dp", pairs)


def gather(tokens, n, errands):
    parts = {(0, 0): tokens}
    chips = n // 2
    done = []
    token = None
    for hop in range(1, chips // 2 + 1):
        for way in (1, -1):
            if 2 * hop == chips and way == -1:
                continue
            here = parts[way * (hop - 1), 0]
            if token is not None:
                here = lax.optimization_barrier((here, token))[0]
            parts[way * hop, 0] = along_ring(here, n, way)
        token = None
        if errands[len(done) :]:
            after = parts[hop - 1, 0]
            result, token = errands[len(done)](in_hbm(after) if hop == 1 else after)
            done.append(result)
    for back, core in list(parts):
        parts[back, 1] = swapped(parts[back, core], n, 1)
    return parts, done


def owners(n, steps):
    order = ring(n)
    me = lax.axis_index("dp")
    chip, core = me // 2, lax.rem(me, 2)
    at = jnp.where(lax.rem(chip, 2) == 0, chip // 2, n // 2 - 1 - chip // 2)
    places = []
    for back, other in steps:
        there = lax.rem(at - back + len(order), len(order))
        up = len(order) // 2
        source = jnp.where(there < up, 2 * there, 2 * (len(order) - 1 - there) + 1)
        places.append(2 * source + lax.rem(core + other, 2))
    return places


def all_sum(value, n):
    total = value
    for mask in range(4, n, 4):
        total = total + swapped(value, n, mask)
    return [total] + [swapped(total, n, mask) for mask in (1, 2, 3)]


def over_columns(row):
    return jnp.transpose(jnp.broadcast_to(row, (8, row.shape[1])))[:, :1]


def over_lanes(x):
    x = sum(x[:, i : i + 128] for i in range(0, x.shape[1], 128))
    return jnp.sum(jnp.transpose(x), axis=0, keepdims=True)


def fold(x):
    return jnp.sum(x.reshape(x.shape[0] // 8, 8, x.shape[1]), axis=0)


def update(grad, one, two):
    first = one + grad
    second = 19.0 * two.astype(jnp.float32) + grad * grad
    over = lax.rsqrt(second)
    inv = pltpu.reciprocal(second * over + 1e-08 / 0.05**0.5, approx=True)
    return over, inv, first * inv


def fetch_kernel(factor, far, after, near, token, raw, sem):
    target = near if factor is None else raw
    tiles = far.shape[0] // TILE

    def copy(i):
        at = pl.ds(pl.multiple_of(i * TILE, TILE), TILE)
        return pltpu.make_async_copy(far.at[at, :], target.at[at, :], sem.at[i])

    for i in range(tiles):
        copy(i).start()
    token[...] = jnp.zeros_like(token)

    def widen(i, _):
        copy(i).wait()
        if factor is not None:
            at = pl.ds(pl.multiple_of(i * TILE, TILE), TILE)
            near[at, :] = factor * raw[at, :].astype(jnp.float32)
        return 0

    lax.fori_loop(0, tiles, widen, 0)


def fetch(x, after, factor=None):
    dtype = x.dtype if factor is None else jnp.float32
    raw = (8, 128) if factor is None else x.shape
    return pl.pallas_call(
        functools.partial(fetch_kernel, factor),
        in_specs=[pl.BlockSpec(memory_space=pl.ANY)] * 2,
        out_specs=[pl.BlockSpec(memory_space=pltpu.VMEM)] * 2,
        out_shape=[pltpu.VMEM(x.shape, dtype), jax.ShapeDtypeStruct((8, 128), jnp.float32)],
        scratch_shapes=[pltpu.VMEM(raw, x.dtype), pltpu.SemaphoreType.DMA((x.shape[0] // TILE,))],
        compiler_params=pltpu.CompilerParams(vmem_limit_bytes=VMEM_BYTES),
        cost_estimate=pl.CostEstimate(flops=0, bytes_accessed=8 << 20, transcendentals=0),
        name="fetch",
    )(in_hbm(x), after)


def replay_kernel(steps, *refs):
    n = len(steps)
    parts, far, (weight, one) = refs[:n], refs[n : n + 4], refs[n + 4 : n + 6]
    (adjoint, turned, along, across, bend, stats) = refs[n + 6 : n + 12]
    (tokens, scaled, score, g0, g1, a0, a1, b0, b1, sums) = refs[n + 12 : n + 22]
    (two, cot, token_weight, part_sem, tile_sem) = refs[n + 22 :]
    grads, firsts, seconds = (g0, g1), (a0, a1), (b0, b1)
    height, depth = parts[0].shape
    count, width = cot.shape
    tiles = depth // TILE

    def span(i):
        return pl.ds(pl.multiple_of(i * TILE, TILE), TILE)

    places = owners(n, steps)

    def part_copy(part):
        at = pl.multiple_of(places[part] * height, height)
        return pltpu.make_async_copy(parts[part], tokens.at[pl.ds(at, height), :], part_sem.at[part])

    small = [
        pltpu.make_async_copy(far[k], ref, part_sem.at[n + k]) for k, ref in enumerate((cot, token_weight))
    ]

    near = (two, adjoint)

    def tile_copy(which, i):
        return pltpu.make_async_copy(far[2 + which].at[span(i), :], near[which].at[span(i), :], tile_sem.at[which, i])

    for part in range(n):
        part_copy(part).start()
    for copy in small:
        copy.start()
    for part in range(n):
        part_copy(part).wait()

    along[...] = jnp.zeros_like(along)
    across[...] = jnp.zeros_like(across)

    def gate_step(i, _):
        tile_copy(0, i).start()
        tile_copy(1, i).start()
        here = tokens[:, span(i)]
        along[...] += f32dot(here, weight[span(i), :])
        turned[span(i), :] = here.T
        return 0

    lax.fori_loop(0, tiles, gate_step, 0)

    gate = along[...]
    for copy in small:
        copy.wait()
    weights = over_columns(token_weight[...])
    cot_f = cot[...].astype(jnp.float32)
    sig = 1.0 / (1.0 + jnp.exp(-gate))
    slope = sig * (1.0 + gate * (1.0 - sig))
    curve = sig * (1.0 - sig) * (2.0 + gate * (1.0 - 2.0 * sig))
    scaled[...] = (weights * cot_f * slope).astype(jnp.bfloat16)
    bend[...] = weights * cot_f * curve
    score[...] = cot_f * slope
    along[...] = jnp.zeros_like(along)

    def grad_rows(i, slot, r):
        at = pl.ds(pl.multiple_of(i * TILE + r, HALF), HALF)
        grads[slot][r : r + HALF, :] = f32dot(turned[at, :], scaled[...])

    def probe(i, slot, target, terms):
        target[...] += f32dot(tokens[:, span(i)], terms[slot][...])

    def arrive(i):
        tile_copy(0, i).wait()
        tile_copy(1, i).wait()

    def pieces(i, slot, first, last):
        for r in range(first, last, ROWS):
            at = pl.ds(pl.multiple_of(i * TILE + r, ROWS), ROWS)
            for c in range(0, width, COLUMNS):
                cols = slice(c, min(c + COLUMNS, width))
                yield r, cols, grads[slot][r : r + ROWS, cols], one[at, cols], two[at, cols], adjoint[at, cols]

    arrive(0)
    grad_rows(0, 0, 0)
    grad_rows(0, 0, HALF)
    sq, cross = {}, {}
    for r, cols, g, m1, m2, adj in pieces(0, 0, 0, SAMPLE):
        _, _, upd = update(g, m1, m2)
        sq[cols.start] = sq.get(cols.start, 0.0) + fold(upd * upd)
        cross[cols.start] = cross.get(cols.start, 0.0) + fold(adj * upd)
    sq = jnp.sum(sum(sq.values()), keepdims=True)
    cross = jnp.sum(sum(cross.values()), keepdims=True)
    clipped = sq * RATIO**2 > float(SAMPLE * width)
    guess = jnp.where(clipped, cross / jnp.maximum(sq, 1.0), 0.0)

    sums[...] = jnp.zeros_like(sums)

    def update_rows(i, slot, first):
        sq, cross = {}, {}
        for r, cols, g, m1, m2, adj in pieces(i, slot, first, first + HALF):
            over, inv, upd = update(g, m1, m2)
            sq[cols.start] = sq.get(cols.start, 0.0) + fold(upd * upd)
            cross[cols.start] = cross.get(cols.start, 0.0) + fold(adj * upd)
            pull = inv * (1.0 - g * (upd * over))
            firsts[slot][r : r + ROWS, cols] = ((adj - guess * upd) * pull).astype(jnp.bfloat16)
            seconds[slot][r : r + ROWS, cols] = (upd * pull).astype(jnp.bfloat16)
        sums[0] += sum(sq.values())
        sums[1] += sum(cross.values())

    def body(i, slot, ahead=True, behind=True):
        if ahead:
            arrive(i + 1)
        for r, target, terms in ((0, along, firsts), (HALF, across, seconds)):
            if ahead:
                grad_rows(i + 1, 1 - slot, r)
            update_rows(i, slot, r)
            if behind:
                probe(i - 1, 1 - slot, target, terms)

    body(0, 0, behind=False)

    def pair(k, _):
        body(2 * k + 1, 1)
        body(2 * k + 2, 0)
        return 0

    lax.fori_loop(0, tiles // 2 - 1, pair, 0)
    body(tiles - 1, 1, ahead=False)
    probe(tiles - 1, 1, along, firsts)
    probe(tiles - 1, 1, across, seconds)

    b = score[...] * across[...]
    a = score[...] * along[...] + guess * b
    whole = lambda x: jnp.broadcast_to(jnp.sum(x, keepdims=True), (1, count))
    stats[0:1, :] = RATIO * over_lanes(a)
    stats[1:2, :] = RATIO**2 * over_lanes(b)
    stats[2:3, :] = RATIO**2 * whole(sums[0])
    stats[3:4, :] = RATIO * whole(sums[1])
    stats[4:8, :] = jnp.broadcast_to(guess, (4, count))


def replay_call(parts, cot, token_weight, two, adjoint, weight, one):
    steps = list(parts)
    n = len(steps)
    depth = weight.shape[0]
    count, width = cot.shape
    vmem = pl.BlockSpec(memory_space=pltpu.VMEM)
    far = pl.BlockSpec(memory_space=pl.ANY)
    block = lambda dtype: pltpu.VMEM((TILE, width), dtype)
    return pl.pallas_call(
        functools.partial(replay_kernel, steps),
        in_specs=[far] * (n + 4) + [vmem] * 2,
        out_specs=[vmem] * 6,
        out_shape=[
            pltpu.VMEM((depth, width), jnp.float32),
            pltpu.VMEM((depth, count), jnp.bfloat16),
            pltpu.VMEM((count, width), jnp.float32),
            pltpu.VMEM((count, width), jnp.float32),
            pltpu.VMEM((count, width), jnp.float32),
            pltpu.VMEM((8, count), jnp.float32),
        ],
        scratch_shapes=[
            pltpu.VMEM((count, depth), jnp.bfloat16),
            pltpu.VMEM((count, width), jnp.bfloat16),
            pltpu.VMEM((count, width), jnp.float32),
            block(jnp.float32),
            block(jnp.float32),
            block(jnp.bfloat16),
            block(jnp.bfloat16),
            block(jnp.bfloat16),
            block(jnp.bfloat16),
            pltpu.VMEM((2, 8, min(COLUMNS, width)), jnp.float32),
            pltpu.VMEM((depth, width), jnp.bfloat16),
            pltpu.VMEM((count, width), jnp.bfloat16),
            pltpu.VMEM((1, count), jnp.float32),
            pltpu.SemaphoreType.DMA((n + 2,)),
            pltpu.SemaphoreType.DMA((2, depth // TILE)),
        ],
        compiler_params=pltpu.CompilerParams(vmem_limit_bytes=VMEM_BYTES),
        name="replay",
    )(
        *[in_hbm(x) if step == (0, 0) else x for step, x in parts.items()],
        *[in_hbm(x) for x in (cot, token_weight, two, adjoint)],
        weight,
        one,
    )


def in_hbm(x):
    return pltpu.with_memory_space_constraint(x, pltpu.HBM)


def theta_kernel(n, entries, s0, s1, s2, s3, own, along, across, bend, turned, adjoint, theta, scores, ready, sent):
    total = s0[...] + s1[...] + (s2[...] + s3[...])
    sq, cross = total[2:3, 0:1], total[3:4, 0:1]
    rms = jnp.sqrt(sq / entries)
    scale = 1.0 / jnp.maximum(1.0, rms)
    bind = jnp.where(rms > 1.0, 1.0 / (rms * rms * rms), 0.0)
    lead = -0.01 * scale
    rest = 0.01 * cross * bind / entries
    mine = lead * total[0:8, :] + rest * pltpu.roll(total, 7, 0)
    count = total.shape[1]
    height = count // n
    mine = pltpu.roll(mine, lax.rem(count - lax.axis_index("dp") * height, count), 1)
    scores[...] = mine[0:1, 0:height]
    lead_here = RATIO * lead
    rest_here = RATIO**2 * rest + lead_here * own[4:5, 0:1]
    bent = (bend[...] * (lead_here * along[...] + rest_here * across[...])).astype(jnp.bfloat16)

    def copy(i):
        at = pl.ds(i * TILE, TILE)
        return pltpu.make_async_copy(ready.at[at, :], theta.at[at, :], sent.at[i])

    tiles = theta.shape[0] // TILE
    for i in range(tiles):
        at = pl.ds(i * TILE, TILE)
        ready[at, :] = 0.999 * adjoint[at, :] + f32dot(turned[at, :], bent)
        copy(i).start()
    for i in range(tiles):
        copy(i).wait()


def theta_call(n, entries, sums, own, along, across, bend, turned, adjoint):
    depth, width = adjoint.shape
    count = turned.shape[1]
    vmem = pl.BlockSpec(memory_space=pltpu.VMEM)
    return pl.pallas_call(
        functools.partial(theta_kernel, n, entries),
        in_specs=[vmem] * 10,
        out_specs=[pl.BlockSpec(memory_space=pl.ANY), vmem],
        out_shape=[
            jax.ShapeDtypeStruct((depth, width), jnp.float32),
            jax.ShapeDtypeStruct((1, count // n), jnp.float32),
        ],
        scratch_shapes=[pltpu.VMEM((depth, width), jnp.float32), pltpu.SemaphoreType.DMA((depth // TILE,))],
        compiler_params=pltpu.CompilerParams(vmem_limit_bytes=VMEM_BYTES),
        name="theta",
    )(*sums, own, along, across, bend, turned, adjoint)


def shards(n, tokens, cotangent, token_weight, weight, moment_one, moment_two, adjoint):
    entries = float(adjoint.shape[0] * adjoint.shape[1] * n)
    errands = [
        lambda after: fetch(weight, after),
        lambda after: fetch(moment_one, after, 9.0),
    ]
    parts, (weight_near, one_near) = gather(tokens, n, errands)
    adjoint_near, turned, along, across, bend, stats = replay_call(
        parts, cotangent, token_weight.reshape(1, -1), moment_two, adjoint, weight_near, one_near
    )
    sums = all_sum(stats, n)
    theta_bar, scores = theta_call(n, entries, sums, stats, along, across, bend, turned, adjoint_near)
    return (theta_bar, scores.reshape(-1))


def solution(mesh):
    in_specs = (
        P(("group", "dp"), None),
        P("group", "dp"),
        P("group"),
        P(None, "dp"),
        P(None, "dp"),
        P(None, "dp"),
        P(None, "dp"),
    )
    out_specs = (P("group", "dp"), P(("group", "dp")))
    body = functools.partial(shards, mesh.shape["dp"])
    return jax.shard_map(body, mesh=mesh, in_specs=in_specs, out_specs=out_specs, check_vma=False)
```

```python
import functools

import jax
import jax.numpy as jnp
from jax import lax
from jax.experimental import pallas as pl
from jax.experimental.pallas import tpu as pltpu
from jax.sharding import PartitionSpec as P

TILE = 512
HALF = 256
ROWS = 16
COLUMNS = 256
COST = 4 << 30
SAMPLE = 256
VMEM_BYTES = 12 << 20
RATIO = 0.1 / 0.05**0.5


def f32dot(a, b):
    return jnp.dot(a, b, preferred_element_type=jnp.float32)


def swapped(value, n, mask):
    return lax.ppermute(value, "dp", [(d ^ mask, d) for d in range(n)])


def ring(n):
    chips = n // 2
    return [*range(0, chips, 2), *range(chips - 1 - chips % 2, 0, -2)]


def onward(value, n):
    order = ring(n)
    pairs = []
    for i, chip in enumerate(order):
        pairs.append((2 * order[i - 1], 2 * chip))
        pairs.append((2 * order[(i + 1) % len(order)] + 1, 2 * chip + 1))
    return lax.ppermute(value, "dp", pairs)


def gather(tokens, n, errands):
    hops = n // 4
    done = []
    token = None
    own = jnp.concatenate([tokens, swapped(tokens, n, 1)], axis=0)
    blocks = [own]
    here = own
    for hop in range(1, hops + 1):
        after = in_hbm(tokens) if hop == 1 else here
        if token is not None:
            here = lax.optimization_barrier((here, token))[0]
        here = onward(here, n)
        token = None
        if errands[len(done) :]:
            result, token = errands[len(done)](after)
            done.append(result)
        blocks.append(here)
        if hop < hops:
            blocks.append(swapped(here, n, 1))
    return blocks, done


def owners(n):
    chips = n // 2
    me = lax.axis_index("dp")
    chip, core = me // 2, lax.rem(me, 2)
    at = jnp.where(lax.rem(chip, 2) == 0, chip // 2, chips - 1 - chip // 2)
    way = 2 * core - 1
    blocks = [(0, core)]
    for hop in range(1, chips // 2 + 1):
        blocks.append((way * hop, core))
        if 2 * hop < chips:
            blocks.append((-way * hop, 1 - core))
    places = []
    for step, first in blocks:
        there = lax.rem(at + step + chips, chips)
        source = jnp.where(there < chips // 2, 2 * there, 2 * (chips - 1 - there) + 1)
        places += [2 * source + first, 2 * source + 1 - first]
    return places


def all_sum(value, n):
    total = value
    for mask in range(4, n, 4):
        total = total + swapped(value, n, mask)
    return [total] + [swapped(total, n, mask) for mask in (1, 2, 3)]


def over_columns(row):
    return jnp.transpose(jnp.broadcast_to(row, (8, row.shape[1])))[:, :1]


def fold(x):
    return jnp.sum(x.reshape(x.shape[0] // 8, 8, x.shape[1]), axis=0)


def update(grad, one, two):
    first = 9.0 * one.astype(jnp.float32) + grad
    second = 19.0 * two.astype(jnp.float32) + grad * grad
    over = lax.rsqrt(second)
    inv = pltpu.reciprocal(second * over + 1e-08 / 0.05**0.5, approx=True)
    return over, inv, first * inv


def fetch_kernel(far, after, near, token, sem):
    copy = pltpu.make_async_copy(far, near, sem.at[0])
    copy.start()
    token[...] = jnp.zeros_like(token)
    copy.wait()


def fetch(x, after):
    return pl.pallas_call(
        fetch_kernel,
        in_specs=[pl.BlockSpec(memory_space=pl.ANY)] * 2,
        out_specs=[pl.BlockSpec(memory_space=pltpu.VMEM)] * 2,
        out_shape=[pltpu.VMEM(x.shape, x.dtype), jax.ShapeDtypeStruct((8, 128), jnp.float32)],
        scratch_shapes=[pltpu.SemaphoreType.DMA((1,))],
        compiler_params=pltpu.CompilerParams(vmem_limit_bytes=1 << 20),
        cost_estimate=pl.CostEstimate(flops=COST, bytes_accessed=8 << 20, transcendentals=0),
        name="fetch",
    )(in_hbm(x), after)


def span(i):
    return pl.ds(pl.multiple_of(i * TILE, TILE), TILE)


def gate_rows(blocks, first, sems, weight, tokens, turned, gate):
    height, depth = blocks[0].shape
    count = len(blocks) * height
    rows = slice(first, first + count)
    copies = [
        pltpu.make_async_copy(ref, tokens.at[pl.ds(first + k * height, height), :], sems.at[k])
        for k, ref in enumerate(blocks)
    ]
    for copy in copies:
        copy.start()
    gate[rows, :] = jnp.zeros((count, gate.shape[1]), jnp.float32)
    for copy in copies:
        copy.wait()

    def step(i, _):
        here = tokens[rows, span(i)]
        gate[rows, :] += f32dot(here, weight[span(i), :])
        turned[span(i), rows] = here.T
        return 0

    lax.fori_loop(0, depth // TILE, step, 0)


def early_kernel(n, half, *refs):
    blocks, (far_cot, far_weight, far_adjoint, weight, _) = refs[:half], refs[half : half + 5]
    (tokens, turned, gate, cot, weights, adjoint) = refs[half + 5 : half + 11]
    (token_weight, upright, sems, cot_sems, far_sems) = refs[half + 11 :]
    height = cot.shape[0] // n
    places = owners(n)
    adjoint_copy = pltpu.make_async_copy(far_adjoint, adjoint, far_sems.at[0])
    weight_copy = pltpu.make_async_copy(far_weight, token_weight, far_sems.at[1])
    cot_copies = [
        pltpu.make_async_copy(
            far_cot.at[pl.ds(pl.multiple_of(place * height, height), height), :],
            cot.at[pl.ds(k * height, height), :],
            cot_sems.at[k],
        )
        for k, place in enumerate(places)
    ]
    weight_copy.start()
    for copy in cot_copies:
        copy.start()
    gate_rows(blocks, 0, sems, weight, tokens, turned, gate)
    adjoint_copy.start()
    weight_copy.wait()
    upright[...] = jnp.broadcast_to(over_columns(token_weight[...]), upright.shape)
    for k, place in enumerate(places):
        weights[k * height : (k + 1) * height, :] = upright[pl.ds(pl.multiple_of(place * height, height), height), :]
    for copy in cot_copies:
        copy.wait()
    adjoint_copy.wait()


def early_call(n, blocks, cot, token_weight, adjoint, weight, token):
    half = len(blocks)
    count, width = cot.shape
    depth = weight.shape[0]
    far = pl.BlockSpec(memory_space=pl.ANY)
    vmem = pl.BlockSpec(memory_space=pltpu.VMEM)
    return pl.pallas_call(
        functools.partial(early_kernel, n, half),
        in_specs=[far] * (half + 3) + [vmem, far],
        out_specs=[vmem] * 6,
        out_shape=[
            pltpu.VMEM((count, depth), jnp.bfloat16),
            pltpu.VMEM((depth, count), jnp.bfloat16),
            pltpu.VMEM((count, width), jnp.float32),
            pltpu.VMEM((count, width), jnp.bfloat16),
            pltpu.VMEM((count, 128), jnp.float32),
            pltpu.VMEM((depth, width), jnp.float32),
        ],
        scratch_shapes=[
            pltpu.VMEM((1, count), jnp.float32),
            pltpu.VMEM((count, 128), jnp.float32),
            pltpu.SemaphoreType.DMA((half,)),
            pltpu.SemaphoreType.DMA((n,)),
            pltpu.SemaphoreType.DMA((2,)),
        ],
        compiler_params=pltpu.CompilerParams(vmem_limit_bytes=VMEM_BYTES),
        cost_estimate=pl.CostEstimate(flops=COST, bytes_accessed=12 << 20, transcendentals=0),
        name="early",
    )(*blocks, *[in_hbm(x) for x in (cot, token_weight, adjoint)], weight, token)


def late_kernel(half, *refs):
    blocks, (weight, cot, weights) = refs[:half], refs[half : half + 3]
    (tokens, turned, gate, scaled, bend, score, sems) = refs[half + 6 :]
    count, width = cot.shape
    gate_rows(blocks, count // 2, sems, weight, tokens, turned, gate)
    for r in range(0, count, 64):
        at = slice(r, r + 64)
        x = gate[at, :]
        token_weight = weights[at, 0:1]
        cot_f = cot[at, :].astype(jnp.float32)
        sig = 1.0 / (1.0 + jnp.exp(-x))
        slope = sig * (1.0 + x * (1.0 - sig))
        curve = sig * (1.0 - sig) * (2.0 + x * (1.0 - 2.0 * sig))
        scaled[at, :] = (token_weight * cot_f * slope).astype(jnp.bfloat16)
        bend[at, :] = token_weight * cot_f * curve
        score[at, :] = cot_f * slope


def late_call(blocks, weight, cot, weights, tokens, turned, gate):
    half = len(blocks)
    count, width = cot.shape
    far = pl.BlockSpec(memory_space=pl.ANY)
    vmem = pl.BlockSpec(memory_space=pltpu.VMEM)
    like = lambda x: pltpu.VMEM(x.shape, x.dtype)
    return pl.pallas_call(
        functools.partial(late_kernel, half),
        in_specs=[far] * half + [vmem] * 6,
        out_specs=[vmem] * 6,
        out_shape=[
            like(tokens),
            like(turned),
            like(gate),
            pltpu.VMEM((count, width), jnp.bfloat16),
            pltpu.VMEM((count, width), jnp.float32),
            pltpu.VMEM((count, width), jnp.float32),
        ],
        scratch_shapes=[pltpu.SemaphoreType.DMA((half,))],
        input_output_aliases={half + 3: 0, half + 4: 1, half + 5: 2},
        compiler_params=pltpu.CompilerParams(vmem_limit_bytes=VMEM_BYTES),
        name="late",
    )(*blocks, weight, cot, weights, tokens, turned, gate)


def step_kernel(n, tokens, turned, scaled, score, one, two, adjoint, along, across, stats, *scratch):
    (g0, g1, a0, a1, b0, b1, sums, upright) = scratch
    grads, firsts, seconds = (g0, g1), (a0, a1), (b0, b1)
    depth = one.shape[0]
    count, width = scaled.shape
    tiles = depth // TILE
    along[...] = jnp.zeros_like(along)
    across[...] = jnp.zeros_like(across)

    def grad_rows(i, slot, r):
        at = pl.ds(pl.multiple_of(i * TILE + r, HALF), HALF)
        grads[slot][r : r + HALF, :] = f32dot(turned[at, :], scaled[...])

    def probe(i, slot, target, terms):
        target[...] += f32dot(tokens[:, span(i)], terms[slot][...])

    def pieces(i, slot, first, last):
        for r in range(first, last, ROWS):
            at = pl.ds(pl.multiple_of(i * TILE + r, ROWS), ROWS)
            for c in range(0, width, COLUMNS):
                cols = slice(c, min(c + COLUMNS, width))
                yield r, cols, grads[slot][r : r + ROWS, cols], one[at, cols], two[at, cols], adjoint[at, cols]

    grad_rows(0, 0, 0)
    grad_rows(0, 0, HALF)
    sq, cross = {}, {}
    for r, cols, g, m1, m2, adj in pieces(0, 0, 0, SAMPLE):
        _, _, upd = update(g, m1, m2)
        sq[cols.start] = sq.get(cols.start, 0.0) + fold(upd * upd)
        cross[cols.start] = cross.get(cols.start, 0.0) + fold(adj * upd)
    sq = jnp.sum(sum(sq.values()), keepdims=True)
    cross = jnp.sum(sum(cross.values()), keepdims=True)
    clipped = sq * RATIO**2 > float(SAMPLE * width)
    guess = jnp.where(clipped, cross / jnp.maximum(sq, 1.0), 0.0)

    sums[...] = jnp.zeros_like(sums)

    def update_rows(i, slot, first):
        sq, cross = {}, {}
        for r, cols, g, m1, m2, adj in pieces(i, slot, first, first + HALF):
            over, inv, upd = update(g, m1, m2)
            sq[cols.start] = sq.get(cols.start, 0.0) + fold(upd * upd)
            cross[cols.start] = cross.get(cols.start, 0.0) + fold(adj * upd)
            pull = inv * (1.0 - g * (upd * over))
            firsts[slot][r : r + ROWS, cols] = ((adj - guess * upd) * pull).astype(jnp.bfloat16)
            seconds[slot][r : r + ROWS, cols] = (upd * pull).astype(jnp.bfloat16)
        sums[0] += sum(sq.values())
        sums[1] += sum(cross.values())

    def body(i, slot, ahead=True, behind=True):
        for r, target, terms in ((0, along, firsts), (HALF, across, seconds)):
            if ahead:
                grad_rows(i + 1, 1 - slot, r)
            update_rows(i, slot, r)
            if behind:
                probe(i - 1, 1 - slot, target, terms)

    body(0, 0, behind=False)

    def pair(k, _):
        body(2 * k + 1, 1)
        body(2 * k + 2, 0)
        return 0

    lax.fori_loop(0, tiles // 2 - 1, pair, 0)
    body(tiles - 1, 1, ahead=False)
    probe(tiles - 1, 1, along, firsts)
    probe(tiles - 1, 1, across, seconds)

    height = count // n
    places = owners(n)

    def spread(x):
        x = sum(x[:, i : i + 128] for i in range(0, width, 128))
        for k, place in enumerate(places):
            upright[pl.ds(pl.multiple_of(place * height, height), height), :] = x[k * height : (k + 1) * height, :]
        return jnp.sum(jnp.transpose(upright[...]), axis=0, keepdims=True)

    b = score[...] * across[...]
    a = score[...] * along[...] + guess * b
    whole = lambda x: jnp.broadcast_to(jnp.sum(x, keepdims=True), (1, count))
    stats[0:1, :] = RATIO * spread(a)
    stats[1:2, :] = RATIO**2 * spread(b)
    stats[2:3, :] = RATIO**2 * whole(sums[0])
    stats[3:4, :] = RATIO * whole(sums[1])
    stats[4:8, :] = jnp.broadcast_to(guess, (4, count))


def step_call(n, tokens, turned, scaled, score, one, two, adjoint):
    count, width = scaled.shape
    vmem = pl.BlockSpec(memory_space=pltpu.VMEM)
    block = lambda dtype: pltpu.VMEM((TILE, width), dtype)
    return pl.pallas_call(
        functools.partial(step_kernel, n),
        in_specs=[vmem] * 7,
        out_specs=[vmem] * 3,
        out_shape=[
            pltpu.VMEM((count, width), jnp.float32),
            pltpu.VMEM((count, width), jnp.float32),
            pltpu.VMEM((8, count), jnp.float32),
        ],
        scratch_shapes=[
            block(jnp.float32),
            block(jnp.float32),
            block(jnp.bfloat16),
            block(jnp.bfloat16),
            block(jnp.bfloat16),
            block(jnp.bfloat16),
            pltpu.VMEM((2, 8, min(COLUMNS, width)), jnp.float32),
            pltpu.VMEM((count, 128), jnp.float32),
        ],
        compiler_params=pltpu.CompilerParams(vmem_limit_bytes=VMEM_BYTES),
        name="step",
    )(tokens, turned, scaled, score, one, two, adjoint)


def in_hbm(x):
    return pltpu.with_memory_space_constraint(x, pltpu.HBM)


def theta_kernel(n, entries, s0, s1, s2, s3, own, along, across, bend, turned, adjoint, theta, scores, ready, sent):
    total = s0[...] + s1[...] + (s2[...] + s3[...])
    sq, cross = total[2:3, 0:1], total[3:4, 0:1]
    rms = jnp.sqrt(sq / entries)
    scale = 1.0 / jnp.maximum(1.0, rms)
    bind = jnp.where(rms > 1.0, 1.0 / (rms * rms * rms), 0.0)
    lead = -0.01 * scale
    rest = 0.01 * cross * bind / entries
    mine = lead * total[0:8, :] + rest * pltpu.roll(total, 7, 0)
    count = total.shape[1]
    height = count // n
    mine = pltpu.roll(mine, lax.rem(count - lax.axis_index("dp") * height, count), 1)
    scores[...] = mine[0:1, 0:height]
    lead_here = RATIO * lead
    rest_here = RATIO**2 * rest + lead_here * own[4:5, 0:1]
    bent = (bend[...] * (lead_here * along[...] + rest_here * across[...])).astype(jnp.bfloat16)

    def copy(i):
        at = pl.ds(i * TILE, TILE)
        return pltpu.make_async_copy(ready.at[at, :], theta.at[at, :], sent.at[i])

    tiles = theta.shape[0] // TILE
    for i in range(tiles):
        at = pl.ds(i * TILE, TILE)
        ready[at, :] = 0.999 * adjoint[at, :] + f32dot(turned[at, :], bent)
        copy(i).start()
    for i in range(tiles):
        copy(i).wait()


def theta_call(n, entries, sums, own, along, across, bend, turned, adjoint):
    depth, width = adjoint.shape
    count = turned.shape[1]
    vmem = pl.BlockSpec(memory_space=pltpu.VMEM)
    return pl.pallas_call(
        functools.partial(theta_kernel, n, entries),
        in_specs=[vmem] * 10,
        out_specs=[pl.BlockSpec(memory_space=pl.ANY), vmem],
        out_shape=[
            jax.ShapeDtypeStruct((depth, width), jnp.float32),
            jax.ShapeDtypeStruct((1, count // n), jnp.float32),
        ],
        scratch_shapes=[pltpu.VMEM((depth, width), jnp.float32), pltpu.SemaphoreType.DMA((depth // TILE,))],
        compiler_params=pltpu.CompilerParams(vmem_limit_bytes=VMEM_BYTES),
        name="theta",
    )(*sums, own, along, across, bend, turned, adjoint)


def shards(n, tokens, cotangent, token_weight, weight, moment_one, moment_two, adjoint):
    entries = float(adjoint.shape[0] * adjoint.shape[1] * n)
    errands = [
        lambda after: fetch(weight, after),
        lambda after: fetch(moment_one, after),
        lambda after: fetch(moment_two, after),
    ]
    blocks, (weight_near, one, two) = gather(tokens, n, errands)
    half = len(blocks) // 2
    rows, turned, gate, cot, weights, adjoint_near = early_call(
        n, blocks[:half], cotangent, token_weight.reshape(1, -1), adjoint, weight_near, two
    )
    rows, turned, gate, scaled, bend, score = late_call(blocks[half:], weight_near, cot, weights, rows, turned, gate)
    along, across, stats = step_call(n, rows, turned, scaled, score, one, two, adjoint_near)
    sums = all_sum(stats, n)
    theta_bar, scores = theta_call(n, entries, sums, stats, along, across, bend, turned, adjoint_near)
    return (theta_bar, scores.reshape(-1))


def solution(mesh):
    in_specs = (
        P(("group", "dp"), None),
        P("group", "dp"),
        P("group"),
        P(None, "dp"),
        P(None, "dp"),
        P(None, "dp"),
        P(None, "dp"),
    )
    out_specs = (P("group", "dp"), P(("group", "dp")))
    body = functools.partial(shards, mesh.shape["dp"])
    return jax.shard_map(body, mesh=mesh, in_specs=in_specs, out_specs=out_specs, check_vma=False)
```

```python
import functools

import jax
import jax.numpy as jnp
from jax import lax
from jax.experimental import pallas as pl
from jax.experimental.pallas import tpu as pltpu
from jax.sharding import PartitionSpec as P

TILE = 512
HALF = 256
ROWS = 16
COLUMNS = 256
COST = 4 << 30
SAMPLE = 256
VMEM_BYTES = 12 << 20
RATIO = 0.1 / 0.05**0.5


def f32dot(a, b):
    return jnp.dot(a, b, preferred_element_type=jnp.float32)


def swapped(value, n, mask):
    return lax.ppermute(value, "dp", [(d ^ mask, d) for d in range(n)])


def ring(n):
    chips = n // 2
    return [*range(0, chips, 2), *range(chips - 1 - chips % 2, 0, -2)]


def onward(value, n):
    order = ring(n)
    pairs = []
    for i, chip in enumerate(order):
        pairs.append((2 * order[i - 1], 2 * chip))
        pairs.append((2 * order[(i + 1) % len(order)] + 1, 2 * chip + 1))
    return lax.ppermute(value, "dp", pairs)


def gather(tokens, n, errands):
    hops = n // 4
    done = []
    here = [tokens, swapped(tokens, n, 1)]
    parts = list(here)
    for hop in range(1, hops + 1):
        after = in_hbm(tokens) if hop == 1 else here[0]
        here = [onward(x, n) for x in here]
        if errands[len(done) :]:
            done.append(errands[len(done)](after))
        parts += here
        if hop < hops:
            parts += [swapped(x, n, 1) for x in here]
    return parts, done


def owners(n):
    chips = n // 2
    me = lax.axis_index("dp")
    chip, core = me // 2, lax.rem(me, 2)
    at = jnp.where(lax.rem(chip, 2) == 0, chip // 2, chips - 1 - chip // 2)
    way = 2 * core - 1
    blocks = [(0, core)]
    for hop in range(1, chips // 2 + 1):
        blocks.append((way * hop, core))
        if 2 * hop < chips:
            blocks.append((-way * hop, 1 - core))
    places = []
    for step, first in blocks:
        there = lax.rem(at + step + chips, chips)
        source = jnp.where(there < chips // 2, 2 * there, 2 * (chips - 1 - there) + 1)
        places += [2 * source + first, 2 * source + 1 - first]
    return places


def all_sum(value, n):
    total = value
    for mask in range(4, n, 4):
        total = total + swapped(value, n, mask)
    return [total] + [swapped(total, n, mask) for mask in (1, 2, 3)]


def over_columns(row):
    return jnp.transpose(jnp.broadcast_to(row, (8, row.shape[1])))[:, :1]


def fold(x):
    return jnp.sum(x.reshape(x.shape[0] // 8, 8, x.shape[1]), axis=0)


def update(grad, one, two):
    first = 9.0 * one.astype(jnp.float32) + grad
    second = 19.0 * two.astype(jnp.float32) + grad * grad
    over = lax.rsqrt(second)
    inv = pltpu.reciprocal(second * over + 1e-08 / 0.05**0.5, approx=True)
    return over, inv, first * inv


def fetch_kernel(far, after, near, sem):
    copy = pltpu.make_async_copy(far, near, sem.at[0])
    copy.start()
    copy.wait()


def fetch(x, after):
    return pl.pallas_call(
        fetch_kernel,
        in_specs=[pl.BlockSpec(memory_space=pl.ANY)] * 2,
        out_specs=pl.BlockSpec(memory_space=pltpu.VMEM),
        out_shape=pltpu.VMEM(x.shape, x.dtype),
        scratch_shapes=[pltpu.SemaphoreType.DMA((1,))],
        compiler_params=pltpu.CompilerParams(vmem_limit_bytes=1 << 20),
        cost_estimate=pl.CostEstimate(flops=COST, bytes_accessed=8 << 20, transcendentals=0),
        name="fetch",
    )(in_hbm(x), after)


def span(i):
    return pl.ds(pl.multiple_of(i * TILE, TILE), TILE)


def gate_rows(blocks, first, sems, weight, tokens, turned, gate, beside):
    height, depth = blocks[0].shape
    count = len(blocks) * height
    rows = slice(first, first + count)
    copies = [
        pltpu.make_async_copy(ref, tokens.at[pl.ds(first + k * height, height), :], sems.at[k])
        for k, ref in enumerate(blocks)
    ]
    for copy in copies:
        copy.start()
    gate[rows, :] = jnp.zeros((count, gate.shape[1]), jnp.float32)
    for copy in copies:
        copy.wait()

    def step(i, _):
        beside(i)
        here = tokens[rows, span(i)]
        gate[rows, :] += f32dot(here, weight[span(i), :])
        turned[span(i), rows] = here.T
        return 0

    lax.fori_loop(0, depth // TILE, step, 0)


def early_kernel(n, half, *refs):
    blocks, (far_cot, far_weight, weight) = refs[:half], refs[half : half + 3]
    (tokens, turned, gate, cot, weights) = refs[half + 3 : half + 8]
    (token_weight, upright, sems, cot_sems, far_sems) = refs[half + 8 :]
    height = cot.shape[0] // n
    places = owners(n)
    weight_copy = pltpu.make_async_copy(far_weight, token_weight, far_sems.at[0])
    cot_copies = [
        pltpu.make_async_copy(
            far_cot.at[pl.ds(pl.multiple_of(place * height, height), height), :],
            cot.at[pl.ds(k * height, height), :],
            cot_sems.at[k],
        )
        for k, place in enumerate(places)
    ]
    weight_copy.start()
    for copy in cot_copies:
        copy.start()
    gate_rows(blocks, 0, sems, weight, tokens, turned, gate, lambda i: None)
    weight_copy.wait()
    upright[...] = jnp.broadcast_to(over_columns(token_weight[...]), upright.shape)
    for k, place in enumerate(places):
        weights[k * height : (k + 1) * height, :] = upright[pl.ds(pl.multiple_of(place * height, height), height), :]
    for copy in cot_copies:
        copy.wait()


def early_call(n, blocks, cot, token_weight, weight):
    half = len(blocks)
    count, width = cot.shape
    depth = weight.shape[0]
    far = pl.BlockSpec(memory_space=pl.ANY)
    vmem = pl.BlockSpec(memory_space=pltpu.VMEM)
    return pl.pallas_call(
        functools.partial(early_kernel, n, half),
        in_specs=[far] * (half + 2) + [vmem],
        out_specs=[vmem] * 5,
        out_shape=[
            pltpu.VMEM((count, depth), jnp.bfloat16),
            pltpu.VMEM((depth, count), jnp.bfloat16),
            pltpu.VMEM((count, width), jnp.float32),
            pltpu.VMEM((count, width), jnp.bfloat16),
            pltpu.VMEM((count, 128), jnp.float32),
        ],
        scratch_shapes=[
            pltpu.VMEM((1, count), jnp.float32),
            pltpu.VMEM((count, 128), jnp.float32),
            pltpu.SemaphoreType.DMA((half,)),
            pltpu.SemaphoreType.DMA((n,)),
            pltpu.SemaphoreType.DMA((1,)),
        ],
        compiler_params=pltpu.CompilerParams(vmem_limit_bytes=VMEM_BYTES),
        cost_estimate=pl.CostEstimate(flops=COST, bytes_accessed=12 << 20, transcendentals=0),
        name="early",
    )(*blocks, *[in_hbm(x) for x in (cot, token_weight)], weight)


def replay_kernel(n, half, *refs):
    blocks, far = refs[:half], refs[half : half + 2]
    (weight, cot, weights, one) = refs[half + 2 : half + 6]
    (tokens, turned, gate, adjoint, along, across, bend, stats) = refs[half + 9 : half + 17]
    (scaled, score, two, g0, g1, a0, a1, b0, b1, sums, upright, sems, tile_sems) = refs[half + 17 :]
    grads, firsts, seconds = (g0, g1), (a0, a1), (b0, b1)
    near = (two, adjoint)
    depth = one.shape[0]
    count, width = scaled.shape
    tiles = depth // TILE

    def tile_copy(which, i):
        return pltpu.make_async_copy(far[which].at[span(i), :], near[which].at[span(i), :], tile_sems.at[which, i])

    def start(i):
        tile_copy(0, i).start()
        tile_copy(1, i).start()

    def arrive(i):
        tile_copy(0, i).wait()
        tile_copy(1, i).wait()

    gate_rows(blocks, count // 2, sems, weight, tokens, turned, gate, start)
    for r in range(0, count, 64):
        at = slice(r, r + 64)
        x = gate[at, :]
        token_weight = weights[at, 0:1]
        cot_f = cot[at, :].astype(jnp.float32)
        sig = 1.0 / (1.0 + jnp.exp(-x))
        slope = sig * (1.0 + x * (1.0 - sig))
        curve = sig * (1.0 - sig) * (2.0 + x * (1.0 - 2.0 * sig))
        scaled[at, :] = (token_weight * cot_f * slope).astype(jnp.bfloat16)
        bend[at, :] = token_weight * cot_f * curve
        score[at, :] = cot_f * slope

    along[...] = jnp.zeros_like(along)
    across[...] = jnp.zeros_like(across)

    def grad_rows(i, slot, r):
        at = pl.ds(pl.multiple_of(i * TILE + r, HALF), HALF)
        grads[slot][r : r + HALF, :] = f32dot(turned[at, :], scaled[...])

    def probe(i, slot, target, terms):
        target[...] += f32dot(tokens[:, span(i)], terms[slot][...])

    def pieces(i, slot, first, last):
        for r in range(first, last, ROWS):
            at = pl.ds(pl.multiple_of(i * TILE + r, ROWS), ROWS)
            for c in range(0, width, COLUMNS):
                cols = slice(c, min(c + COLUMNS, width))
                yield r, cols, grads[slot][r : r + ROWS, cols], one[at, cols], two[at, cols], adjoint[at, cols]

    arrive(0)
    grad_rows(0, 0, 0)
    grad_rows(0, 0, HALF)
    sq, cross = {}, {}
    for r, cols, g, m1, m2, adj in pieces(0, 0, 0, SAMPLE):
        _, _, upd = update(g, m1, m2)
        sq[cols.start] = sq.get(cols.start, 0.0) + fold(upd * upd)
        cross[cols.start] = cross.get(cols.start, 0.0) + fold(adj * upd)
    sq = jnp.sum(sum(sq.values()), keepdims=True)
    cross = jnp.sum(sum(cross.values()), keepdims=True)
    clipped = sq * RATIO**2 > float(SAMPLE * width)
    guess = jnp.where(clipped, cross / jnp.maximum(sq, 1.0), 0.0)

    sums[...] = jnp.zeros_like(sums)

    def update_rows(i, slot, first):
        sq, cross = {}, {}
        for r, cols, g, m1, m2, adj in pieces(i, slot, first, first + HALF):
            over, inv, upd = update(g, m1, m2)
            sq[cols.start] = sq.get(cols.start, 0.0) + fold(upd * upd)
            cross[cols.start] = cross.get(cols.start, 0.0) + fold(adj * upd)
            pull = inv * (1.0 - g * (upd * over))
            firsts[slot][r : r + ROWS, cols] = ((adj - guess * upd) * pull).astype(jnp.bfloat16)
            seconds[slot][r : r + ROWS, cols] = (upd * pull).astype(jnp.bfloat16)
        sums[0] += sum(sq.values())
        sums[1] += sum(cross.values())

    def body(i, slot, ahead=True, behind=True):
        if ahead:
            arrive(i + 1)
        for r, target, terms in ((0, along, firsts), (HALF, across, seconds)):
            if ahead:
                grad_rows(i + 1, 1 - slot, r)
            update_rows(i, slot, r)
            if behind:
                probe(i - 1, 1 - slot, target, terms)

    body(0, 0, behind=False)

    def pair(k, _):
        body(2 * k + 1, 1)
        body(2 * k + 2, 0)
        return 0

    lax.fori_loop(0, tiles // 2 - 1, pair, 0)
    body(tiles - 1, 1, ahead=False)
    probe(tiles - 1, 1, along, firsts)
    probe(tiles - 1, 1, across, seconds)

    height = count // n
    places = owners(n)

    def spread(x):
        x = sum(x[:, i : i + 128] for i in range(0, width, 128))
        for k, place in enumerate(places):
            upright[pl.ds(pl.multiple_of(place * height, height), height), :] = x[k * height : (k + 1) * height, :]
        return jnp.sum(jnp.transpose(upright[...]), axis=0, keepdims=True)

    b = score[...] * across[...]
    a = score[...] * along[...] + guess * b
    whole = lambda x: jnp.broadcast_to(jnp.sum(x, keepdims=True), (1, count))
    stats[0:1, :] = RATIO * spread(a)
    stats[1:2, :] = RATIO**2 * spread(b)
    stats[2:3, :] = RATIO**2 * whole(sums[0])
    stats[3:4, :] = RATIO * whole(sums[1])
    stats[4:8, :] = jnp.broadcast_to(guess, (4, count))


def replay_call(n, blocks, two, adjoint, weight, cot, weights, one, tokens, turned, gate):
    half = len(blocks)
    depth = one.shape[0]
    count, width = cot.shape
    far = pl.BlockSpec(memory_space=pl.ANY)
    vmem = pl.BlockSpec(memory_space=pltpu.VMEM)
    like = lambda x: pltpu.VMEM(x.shape, x.dtype)
    block = lambda dtype: pltpu.VMEM((TILE, width), dtype)
    return pl.pallas_call(
        functools.partial(replay_kernel, n, half),
        in_specs=[far] * (half + 2) + [vmem] * 7,
        out_specs=[vmem] * 8,
        out_shape=[
            like(tokens),
            like(turned),
            like(gate),
            pltpu.VMEM((depth, width), jnp.float32),
            pltpu.VMEM((count, width), jnp.float32),
            pltpu.VMEM((count, width), jnp.float32),
            pltpu.VMEM((count, width), jnp.float32),
            pltpu.VMEM((8, count), jnp.float32),
        ],
        scratch_shapes=[
            pltpu.VMEM((count, width), jnp.bfloat16),
            pltpu.VMEM((count, width), jnp.float32),
            pltpu.VMEM((depth, width), jnp.bfloat16),
            block(jnp.float32),
            block(jnp.float32),
            block(jnp.bfloat16),
            block(jnp.bfloat16),
            block(jnp.bfloat16),
            block(jnp.bfloat16),
            pltpu.VMEM((2, 8, min(COLUMNS, width)), jnp.float32),
            pltpu.VMEM((count, 128), jnp.float32),
            pltpu.SemaphoreType.DMA((half,)),
            pltpu.SemaphoreType.DMA((2, depth // TILE)),
        ],
        input_output_aliases={half + 6: 0, half + 7: 1, half + 8: 2},
        compiler_params=pltpu.CompilerParams(vmem_limit_bytes=VMEM_BYTES),
        name="replay",
    )(*blocks, in_hbm(two), in_hbm(adjoint), weight, cot, weights, one, tokens, turned, gate)


def in_hbm(x):
    return pltpu.with_memory_space_constraint(x, pltpu.HBM)


def theta_kernel(n, entries, s0, s1, s2, s3, own, along, across, bend, turned, adjoint, theta, scores, ready, sent):
    total = s0[...] + s1[...] + (s2[...] + s3[...])
    sq, cross = total[2:3, 0:1], total[3:4, 0:1]
    rms = jnp.sqrt(sq / entries)
    scale = 1.0 / jnp.maximum(1.0, rms)
    bind = jnp.where(rms > 1.0, 1.0 / (rms * rms * rms), 0.0)
    lead = -0.01 * scale
    rest = 0.01 * cross * bind / entries
    mine = lead * total[0:8, :] + rest * pltpu.roll(total, 7, 0)
    count = total.shape[1]
    height = count // n
    mine = pltpu.roll(mine, lax.rem(count - lax.axis_index("dp") * height, count), 1)
    scores[...] = mine[0:1, 0:height]
    lead_here = RATIO * lead
    rest_here = RATIO**2 * rest + lead_here * own[4:5, 0:1]
    bent = (bend[...] * (lead_here * along[...] + rest_here * across[...])).astype(jnp.bfloat16)

    def copy(i):
        at = pl.ds(i * TILE, TILE)
        return pltpu.make_async_copy(ready.at[at, :], theta.at[at, :], sent.at[i])

    tiles = theta.shape[0] // TILE
    for i in range(tiles):
        at = pl.ds(i * TILE, TILE)
        ready[at, :] = 0.999 * adjoint[at, :] + f32dot(turned[at, :], bent)
        copy(i).start()
    for i in range(tiles):
        copy(i).wait()


def theta_call(n, entries, sums, own, along, across, bend, turned, adjoint):
    depth, width = adjoint.shape
    count = turned.shape[1]
    vmem = pl.BlockSpec(memory_space=pltpu.VMEM)
    return pl.pallas_call(
        functools.partial(theta_kernel, n, entries),
        in_specs=[vmem] * 10,
        out_specs=[pl.BlockSpec(memory_space=pl.ANY), vmem],
        out_shape=[
            jax.ShapeDtypeStruct((depth, width), jnp.float32),
            jax.ShapeDtypeStruct((1, count // n), jnp.float32),
        ],
        scratch_shapes=[pltpu.VMEM((depth, width), jnp.float32), pltpu.SemaphoreType.DMA((depth // TILE,))],
        compiler_params=pltpu.CompilerParams(vmem_limit_bytes=VMEM_BYTES),
        name="theta",
    )(*sums, own, along, across, bend, turned, adjoint)


def shards(n, tokens, cotangent, token_weight, weight, moment_one, moment_two, adjoint):
    entries = float(adjoint.shape[0] * adjoint.shape[1] * n)
    errands = [lambda after: fetch(weight, after), lambda after: fetch(moment_one, after)]
    blocks, (weight_near, one) = gather(tokens, n, errands)
    half = len(blocks) // 2
    rows, turned, gate, cot, weights = early_call(n, blocks[:half], cotangent, token_weight.reshape(1, -1), weight_near)
    _, turned, _, adjoint_near, along, across, bend, stats = replay_call(
        n, blocks[half:], moment_two, adjoint, weight_near, cot, weights, one, rows, turned, gate
    )
    sums = all_sum(stats, n)
    theta_bar, scores = theta_call(n, entries, sums, stats, along, across, bend, turned, adjoint_near)
    return (theta_bar, scores.reshape(-1))


def solution(mesh):
    in_specs = (
        P(("group", "dp"), None),
        P("group", "dp"),
        P("group"),
        P(None, "dp"),
        P(None, "dp"),
        P(None, "dp"),
        P(None, "dp"),
    )
    out_specs = (P("group", "dp"), P(("group", "dp")))
    body = functools.partial(shards, mesh.shape["dp"])
    return jax.shard_map(body, mesh=mesh, in_specs=in_specs, out_specs=out_specs, check_vma=False)
```

```python
import functools

import jax
import jax.numpy as jnp
from jax import lax
from jax.experimental import pallas as pl
from jax.experimental.pallas import tpu as pltpu
from jax.sharding import PartitionSpec as P

TILE = 512
HALF = 256
ROWS = 16
COLUMNS = 256
COST = 4 << 30
SAMPLE = 256
VMEM_BYTES = 12 << 20
RATIO = 0.1 / 0.05**0.5


def f32dot(a, b):
    return jnp.dot(a, b, preferred_element_type=jnp.float32)


def swapped(value, n, mask):
    return lax.ppermute(value, "dp", [(d ^ mask, d) for d in range(n)])


def ring(n):
    chips = n // 2
    return [*range(0, chips, 2), *range(chips - 1 - chips % 2, 0, -2)]


def onward(value, n):
    order = ring(n)
    pairs = []
    for i, chip in enumerate(order):
        pairs.append((2 * order[i - 1], 2 * chip))
        pairs.append((2 * order[(i + 1) % len(order)] + 1, 2 * chip + 1))
    return lax.ppermute(value, "dp", pairs)


def gather(tokens, n, errands):
    hops = n // 4
    done = []
    here = [tokens, swapped(tokens, n, 1)]
    parts = list(here)
    for hop in range(1, hops + 1):
        after = in_hbm(tokens) if hop == 1 else here[0]
        here = [onward(x, n) for x in here]
        if errands[len(done) :]:
            done.append(errands[len(done)](after))
        parts += here
        if hop < hops:
            parts += [swapped(x, n, 1) for x in here]
    return parts, done


def owners(n):
    chips = n // 2
    me = lax.axis_index("dp")
    chip, core = me >> 1, me & 1
    at = jnp.where(chip & 1 == 0, chip >> 1, chips - 1 - (chip >> 1))
    way = 2 * core - 1
    blocks = [(0, core)]
    for hop in range(1, chips // 2 + 1):
        blocks.append((way * hop, core))
        if 2 * hop < chips:
            blocks.append((-way * hop, 1 - core))
    places = []
    for step, first in blocks:
        there = at + step
        there = jnp.where(there < 0, there + chips, jnp.where(there >= chips, there - chips, there))
        source = jnp.where(there < chips // 2, 2 * there, 2 * (chips - 1 - there) + 1)
        places += [2 * source + first, 2 * source + 1 - first]
    return places


def all_sum(value, n):
    total = value
    for mask in range(4, n, 4):
        total = total + swapped(value, n, mask)
    return [total] + [swapped(total, n, mask) for mask in (1, 2, 3)]


def over_columns(row):
    return jnp.transpose(jnp.broadcast_to(row, (8, row.shape[1])))[:, :1]


def fold(x):
    return jnp.sum(x.reshape(x.shape[0] // 8, 8, x.shape[1]), axis=0)


def update(grad, one, two):
    first = one + grad
    second = two + grad * grad
    over = lax.rsqrt(second)
    inv = pltpu.reciprocal(second * over + 1e-08 / 0.05**0.5, approx=True)
    return over, inv, first * inv


def fetch_params():
    return {
        "compiler_params": pltpu.CompilerParams(vmem_limit_bytes=6 << 20),
        "cost_estimate": pl.CostEstimate(flops=COST, bytes_accessed=8 << 20, transcendentals=0),
    }


def widen_kernel(factor, far, after, near, raw, sems):
    tiles = far.shape[0] // TILE

    def copy(i):
        return pltpu.make_async_copy(far.at[span(i), :], raw.at[span(i), :], sems.at[i])

    for i in range(tiles):
        copy(i).start()

    def step(i, _):
        copy(i).wait()
        near[span(i), :] = factor * raw[span(i), :].astype(jnp.float32)
        return 0

    lax.fori_loop(0, tiles, step, 0)


def fetch_wide(x, factor, after):
    return pl.pallas_call(
        functools.partial(widen_kernel, factor),
        in_specs=[pl.BlockSpec(memory_space=pl.ANY)] * 2,
        out_specs=pl.BlockSpec(memory_space=pltpu.VMEM),
        out_shape=pltpu.VMEM(x.shape, jnp.float32),
        scratch_shapes=[pltpu.VMEM(x.shape, x.dtype), pltpu.SemaphoreType.DMA((x.shape[0] // TILE,))],
        name="widen",
        **fetch_params(),
    )(in_hbm(x), after)


def fetch_kernel(n, far, far_cot, far_weight, after, near, cot, weights, token_weight, upright, sems, cot_sems):
    height = cot.shape[0] // n
    copy = pltpu.make_async_copy(far, near, sems.at[0])
    weight_copy = pltpu.make_async_copy(far_weight, token_weight, sems.at[1])
    weight_copy.start()
    copy.start()
    places = [pl.multiple_of(place * height, height) for place in owners(n)]
    cot_copies = [
        pltpu.make_async_copy(
            far_cot.at[pl.ds(place, height), :], cot.at[pl.ds(k * height, height), :], cot_sems.at[k]
        )
        for k, place in enumerate(places)
    ]
    for cot_copy in cot_copies:
        cot_copy.start()
    weight_copy.wait()
    upright[...] = jnp.broadcast_to(over_columns(token_weight[...]), upright.shape)
    for k, place in enumerate(places):
        weights[k * height : (k + 1) * height, :] = upright[pl.ds(place, height), :]
    for cot_copy in cot_copies:
        cot_copy.wait()
    copy.wait()


def fetch(n, weight, cot, token_weight, after):
    count = cot.shape[0]
    vmem = pl.BlockSpec(memory_space=pltpu.VMEM)
    return pl.pallas_call(
        functools.partial(fetch_kernel, n),
        in_specs=[pl.BlockSpec(memory_space=pl.ANY)] * 4,
        out_specs=[vmem] * 3,
        out_shape=[
            pltpu.VMEM(weight.shape, weight.dtype),
            pltpu.VMEM(cot.shape, cot.dtype),
            pltpu.VMEM((count, 128), jnp.float32),
        ],
        scratch_shapes=[
            pltpu.VMEM((1, count), jnp.float32),
            pltpu.VMEM((count, 128), jnp.float32),
            pltpu.SemaphoreType.DMA((2,)),
            pltpu.SemaphoreType.DMA((n,)),
        ],
        name="fetch",
        **fetch_params(),
    )(in_hbm(weight), in_hbm(cot), in_hbm(token_weight), after)


def span(i):
    return pl.ds(pl.multiple_of(i * TILE, TILE), TILE)


def gate_rows(blocks, first, sems, weight, tokens, turned, gate, beside):
    height, depth = blocks[0].shape
    count = len(blocks) * height
    rows = slice(first, first + count)
    copies = [
        pltpu.make_async_copy(ref, tokens.at[pl.ds(first + k * height, height), :], sems.at[k])
        for k, ref in enumerate(blocks)
    ]
    for copy in copies:
        copy.start()
    gate[rows, :] = jnp.zeros((count, gate.shape[1]), jnp.float32)
    for copy in copies:
        copy.wait()

    def step(i, _):
        beside(i)
        here = tokens[rows, span(i)]
        gate[rows, :] += f32dot(here, weight[span(i), :])
        turned[span(i), rows] = here.T
        return 0

    lax.fori_loop(0, depth // TILE, step, 0)


def early_kernel(half, *refs):
    blocks, weight, (tokens, turned, gate, sems) = refs[:half], refs[half], refs[half + 1 :]
    gate_rows(blocks, 0, sems, weight, tokens, turned, gate, lambda i: None)


def early_call(blocks, weight, count):
    half = len(blocks)
    depth, width = weight.shape
    vmem = pl.BlockSpec(memory_space=pltpu.VMEM)
    return pl.pallas_call(
        functools.partial(early_kernel, half),
        in_specs=[pl.BlockSpec(memory_space=pl.ANY)] * half + [vmem],
        out_specs=[vmem] * 3,
        out_shape=[
            pltpu.VMEM((count, depth), jnp.bfloat16),
            pltpu.VMEM((depth, count), jnp.bfloat16),
            pltpu.VMEM((count, width), jnp.float32),
        ],
        scratch_shapes=[pltpu.SemaphoreType.DMA((half,))],
        compiler_params=pltpu.CompilerParams(vmem_limit_bytes=4 << 20),
        cost_estimate=pl.CostEstimate(flops=COST, bytes_accessed=12 << 20, transcendentals=0),
        name="early",
    )(*blocks, weight)


def replay_kernel(n, half, *refs):
    blocks, (far, weight, cot, weights, one, two) = refs[:half], refs[half : half + 6]
    (tokens, turned, gate, adjoint, along, across, bend, stats) = refs[half + 9 : half + 17]
    (scaled, score, g0, g1, a0, a1, b0, b1, sums, upright, sems, tile_sems) = refs[half + 17 :]
    grads, firsts, seconds = (g0, g1), (a0, a1), (b0, b1)
    depth = one.shape[0]
    count, width = scaled.shape
    tiles = depth // TILE

    def tile_copy(i):
        return pltpu.make_async_copy(far.at[span(i), :], adjoint.at[span(i), :], tile_sems.at[i])

    gate_rows(blocks, count // 2, sems, weight, tokens, turned, gate, lambda i: tile_copy(i).start())
    for r in range(0, count, 64):
        at = slice(r, r + 64)
        x = gate[at, :]
        token_weight = weights[at, 0:1]
        cot_f = cot[at, :].astype(jnp.float32)
        sig = 1.0 / (1.0 + jnp.exp(-x))
        slope = sig * (1.0 + x * (1.0 - sig))
        curve = sig * (1.0 - sig) * (2.0 + x * (1.0 - 2.0 * sig))
        scaled[at, :] = (token_weight * cot_f * slope).astype(jnp.bfloat16)
        bend[at, :] = token_weight * cot_f * curve
        score[at, :] = cot_f * slope

    along[...] = jnp.zeros_like(along)
    across[...] = jnp.zeros_like(across)

    def grad_rows(i, slot, r):
        at = pl.ds(pl.multiple_of(i * TILE + r, HALF), HALF)
        grads[slot][r : r + HALF, :] = f32dot(turned[at, :], scaled[...])

    def probe(i, slot, target, terms):
        target[...] += f32dot(tokens[:, span(i)], terms[slot][...])

    def pieces(i, slot, first, last):
        for r in range(first, last, ROWS):
            at = pl.ds(pl.multiple_of(i * TILE + r, ROWS), ROWS)
            for c in range(0, width, COLUMNS):
                cols = slice(c, min(c + COLUMNS, width))
                yield r, cols, grads[slot][r : r + ROWS, cols], one[at, cols], two[at, cols], adjoint[at, cols]

    for i in range(2):
        tile_copy(i).wait()
    grad_rows(0, 0, 0)
    grad_rows(0, 0, HALF)
    sq, cross = {}, {}
    for r, cols, g, m1, m2, adj in pieces(0, 0, 0, SAMPLE):
        _, _, upd = update(g, m1, m2)
        sq[cols.start] = sq.get(cols.start, 0.0) + fold(upd * upd)
        cross[cols.start] = cross.get(cols.start, 0.0) + fold(adj * upd)
    sq = jnp.sum(sum(sq.values()), keepdims=True)
    cross = jnp.sum(sum(cross.values()), keepdims=True)
    clipped = sq * RATIO**2 > float(SAMPLE * width)
    guess = jnp.where(clipped, cross / jnp.maximum(sq, 1.0), 0.0)

    sums[...] = jnp.zeros_like(sums)

    def update_rows(i, slot, first):
        sq, cross = {}, {}
        for r, cols, g, m1, m2, adj in pieces(i, slot, first, first + HALF):
            over, inv, upd = update(g, m1, m2)
            sq[cols.start] = sq.get(cols.start, 0.0) + fold(upd * upd)
            cross[cols.start] = cross.get(cols.start, 0.0) + fold(adj * upd)
            pull = inv * (1.0 - g * (upd * over))
            firsts[slot][r : r + ROWS, cols] = ((adj - guess * upd) * pull).astype(jnp.bfloat16)
            seconds[slot][r : r + ROWS, cols] = (upd * pull).astype(jnp.bfloat16)
        sums[0] += sum(sq.values())
        sums[1] += sum(cross.values())

    def body(i, slot, ahead=True, behind=True):
        for r, target, terms in ((0, along, firsts), (HALF, across, seconds)):
            if ahead:
                grad_rows(i + 1, 1 - slot, r)
            update_rows(i, slot, r)
            if behind:
                probe(i - 1, 1 - slot, target, terms)

    body(0, 0, behind=False)

    def pair(k, _):
        tile_copy(2 * k + 2).wait()
        tile_copy(2 * k + 3).wait()
        body(2 * k + 1, 1)
        body(2 * k + 2, 0)
        return 0

    lax.fori_loop(0, tiles // 2 - 1, pair, 0)
    body(tiles - 1, 1, ahead=False)
    probe(tiles - 1, 1, along, firsts)
    probe(tiles - 1, 1, across, seconds)

    height = count // n
    places = owners(n)

    def spread(x):
        x = sum(x[:, i : i + 128] for i in range(0, width, 128))
        for k, place in enumerate(places):
            upright[pl.ds(pl.multiple_of(place * height, height), height), :] = x[k * height : (k + 1) * height, :]
        return jnp.sum(jnp.transpose(upright[...]), axis=0, keepdims=True)

    b = score[...] * across[...]
    a = score[...] * along[...] + guess * b
    whole = lambda x: jnp.broadcast_to(jnp.sum(x, keepdims=True), (1, count))
    stats[0:1, :] = RATIO * spread(a)
    stats[1:2, :] = RATIO**2 * spread(b)
    stats[2:3, :] = RATIO**2 * whole(sums[0])
    stats[3:4, :] = RATIO * whole(sums[1])
    stats[4:8, :] = jnp.broadcast_to(guess, (4, count))


def replay_call(n, blocks, adjoint, weight, cot, weights, one, two, tokens, turned, gate):
    half = len(blocks)
    depth = one.shape[0]
    count, width = cot.shape
    far = pl.BlockSpec(memory_space=pl.ANY)
    vmem = pl.BlockSpec(memory_space=pltpu.VMEM)
    like = lambda x: pltpu.VMEM(x.shape, x.dtype)
    block = lambda dtype: pltpu.VMEM((TILE, width), dtype)
    return pl.pallas_call(
        functools.partial(replay_kernel, n, half),
        in_specs=[far] * (half + 1) + [vmem] * 8,
        out_specs=[vmem] * 8,
        out_shape=[
            like(tokens),
            like(turned),
            like(gate),
            pltpu.VMEM((depth, width), jnp.float32),
            pltpu.VMEM((count, width), jnp.float32),
            pltpu.VMEM((count, width), jnp.float32),
            pltpu.VMEM((count, width), jnp.float32),
            pltpu.VMEM((8, count), jnp.float32),
        ],
        scratch_shapes=[
            pltpu.VMEM((count, width), jnp.bfloat16),
            pltpu.VMEM((count, width), jnp.float32),
            block(jnp.float32),
            block(jnp.float32),
            block(jnp.bfloat16),
            block(jnp.bfloat16),
            block(jnp.bfloat16),
            block(jnp.bfloat16),
            pltpu.VMEM((2, 8, min(COLUMNS, width)), jnp.float32),
            pltpu.VMEM((count, 128), jnp.float32),
            pltpu.SemaphoreType.DMA((half,)),
            pltpu.SemaphoreType.DMA((depth // TILE,)),
        ],
        input_output_aliases={half + 6: 0, half + 7: 1, half + 8: 2},
        compiler_params=pltpu.CompilerParams(vmem_limit_bytes=VMEM_BYTES),
        name="replay",
    )(*blocks, in_hbm(adjoint), weight, cot, weights, one, two, tokens, turned, gate)


def in_hbm(x):
    return pltpu.with_memory_space_constraint(x, pltpu.HBM)


def theta_kernel(n, entries, s0, s1, s2, s3, own, along, across, bend, turned, adjoint, theta, scores, ready, sent):
    total = s0[...] + s1[...] + (s2[...] + s3[...])
    sq, cross = total[2:3, 0:1], total[3:4, 0:1]
    rms = jnp.sqrt(sq / entries)
    scale = 1.0 / jnp.maximum(1.0, rms)
    bind = jnp.where(rms > 1.0, 1.0 / (rms * rms * rms), 0.0)
    lead = -0.01 * scale
    rest = 0.01 * cross * bind / entries
    mine = lead * total[0:8, :] + rest * pltpu.roll(total, 7, 0)
    count = total.shape[1]
    height = count // n
    mine = pltpu.roll(mine, lax.rem(count - lax.axis_index("dp") * height, count), 1)
    scores[...] = mine[0:1, 0:height]
    lead_here = RATIO * lead
    rest_here = RATIO**2 * rest + lead_here * own[4:5, 0:1]
    bent = (bend[...] * (lead_here * along[...] + rest_here * across[...])).astype(jnp.bfloat16)

    def copy(i):
        at = pl.ds(i * TILE, TILE)
        return pltpu.make_async_copy(ready.at[at, :], theta.at[at, :], sent.at[i])

    tiles = theta.shape[0] // TILE
    for i in range(tiles):
        at = pl.ds(i * TILE, TILE)
        ready[at, :] = 0.999 * adjoint[at, :] + f32dot(turned[at, :], bent)
        copy(i).start()
    for i in range(tiles):
        copy(i).wait()


def theta_call(n, entries, sums, own, along, across, bend, turned, adjoint):
    depth, width = adjoint.shape
    count = turned.shape[1]
    vmem = pl.BlockSpec(memory_space=pltpu.VMEM)
    return pl.pallas_call(
        functools.partial(theta_kernel, n, entries),
        in_specs=[vmem] * 10,
        out_specs=[pl.BlockSpec(memory_space=pl.ANY), vmem],
        out_shape=[
            jax.ShapeDtypeStruct((depth, width), jnp.float32),
            jax.ShapeDtypeStruct((1, count // n), jnp.float32),
        ],
        scratch_shapes=[pltpu.VMEM((depth, width), jnp.float32), pltpu.SemaphoreType.DMA((depth // TILE,))],
        compiler_params=pltpu.CompilerParams(vmem_limit_bytes=VMEM_BYTES),
        name="theta",
    )(*sums, own, along, across, bend, turned, adjoint)


def shards(n, tokens, cotangent, token_weight, weight, moment_one, moment_two, adjoint):
    entries = float(adjoint.shape[0] * adjoint.shape[1] * n)
    errands = [
        lambda after: fetch(n, weight, cotangent, token_weight.reshape(1, -1), after),
        lambda after: fetch_wide(moment_one, 9.0, after),
        lambda after: fetch_wide(moment_two, 19.0, after),
    ]
    blocks, ((weight_near, cot, weights), one, two) = gather(tokens, n, errands)
    half = len(blocks) // 2
    rows, turned, gate = early_call(blocks[:half], weight_near, cot.shape[0])
    _, turned, _, adjoint_near, along, across, bend, stats = replay_call(
        n, blocks[half:], adjoint, weight_near, cot, weights, one, two, rows, turned, gate
    )
    sums = all_sum(stats, n)
    theta_bar, scores = theta_call(n, entries, sums, stats, along, across, bend, turned, adjoint_near)
    return (theta_bar, scores.reshape(-1))


def solution(mesh):
    in_specs = (
        P(("group", "dp"), None),
        P("group", "dp"),
        P("group"),
        P(None, "dp"),
        P(None, "dp"),
        P(None, "dp"),
        P(None, "dp"),
    )
    out_specs = (P("group", "dp"), P(("group", "dp")))
    body = functools.partial(shards, mesh.shape["dp"])
    return jax.shard_map(body, mesh=mesh, in_specs=in_specs, out_specs=out_specs, check_vma=False)
```

```python
import functools

import jax
import jax.numpy as jnp
from jax import lax
from jax.experimental import pallas as pl
from jax.experimental.pallas import tpu as pltpu
from jax.sharding import PartitionSpec as P

TILE = 512
QUARTER = 128
ROWS = 16
COLUMNS = 256
COST = 4 << 30
SAMPLE = 256
VMEM_BYTES = 12 << 20
RATIO = 0.1 / 0.05**0.5


def f32dot(a, b):
    return jnp.dot(a, b, preferred_element_type=jnp.float32)


def swapped(value, n, mask):
    return lax.ppermute(value, "dp", [(d ^ mask, d) for d in range(n)])


def ring(n):
    chips = n // 2
    return [*range(0, chips, 2), *range(chips - 1 - chips % 2, 0, -2)]


def onward(value, n):
    order = ring(n)
    pairs = []
    for i, chip in enumerate(order):
        pairs.append((2 * order[i - 1], 2 * chip))
        pairs.append((2 * order[(i + 1) % len(order)] + 1, 2 * chip + 1))
    return lax.ppermute(value, "dp", pairs)


def gather(tokens, n, errands):
    hops = n // 4
    done = []
    here = [tokens, swapped(tokens, n, 1)]
    parts = list(here)
    for hop in range(1, hops + 1):
        after = in_hbm(tokens) if hop == 1 else here[0]
        here = [onward(x, n) for x in here]
        if errands[len(done) :]:
            done.append(errands[len(done)](after))
        parts += here
        if hop < hops:
            parts += [swapped(x, n, 1) for x in here]
    return parts, done


def owners(n):
    chips = n // 2
    me = lax.axis_index("dp")
    chip, core = me >> 1, me & 1
    at = jnp.where(chip & 1 == 0, chip >> 1, chips - 1 - (chip >> 1))
    way = 2 * core - 1
    blocks = [(0, core)]
    for hop in range(1, chips // 2 + 1):
        blocks.append((way * hop, core))
        if 2 * hop < chips:
            blocks.append((-way * hop, 1 - core))
    places = []
    for step, first in blocks:
        there = at + step
        there = jnp.where(there < 0, there + chips, jnp.where(there >= chips, there - chips, there))
        source = jnp.where(there < chips // 2, 2 * there, 2 * (chips - 1 - there) + 1)
        places += [2 * source + first, 2 * source + 1 - first]
    return places


def all_sum(value, n):
    total = value
    for mask in range(4, n, 4):
        total = total + swapped(value, n, mask)
    return [total] + [swapped(total, n, mask) for mask in (1, 2, 3)]


def over_columns(row):
    return jnp.transpose(jnp.broadcast_to(row, (8, row.shape[1])))[:, :1]


def fold(x):
    return jnp.sum(x.reshape(x.shape[0] // 8, 8, x.shape[1]), axis=0)


def update(grad, one, two):
    first = one + grad
    second = two + grad * grad
    over = lax.rsqrt(second)
    inv = pltpu.reciprocal(second * over + 1e-08 / 0.05**0.5, approx=True)
    return over, inv, first * inv


def fetch_params():
    return {
        "compiler_params": pltpu.CompilerParams(vmem_limit_bytes=6 << 20),
        "cost_estimate": pl.CostEstimate(flops=COST, bytes_accessed=8 << 20, transcendentals=0),
    }


def widen_kernel(factor, far, after, near, raw, sems):
    tiles = far.shape[0] // TILE

    def copy(i):
        return pltpu.make_async_copy(far.at[span(i), :], raw.at[span(i), :], sems.at[i])

    for i in range(tiles):
        copy(i).start()

    def step(i, _):
        copy(i).wait()
        near[span(i), :] = factor * raw[span(i), :].astype(jnp.float32)
        return 0

    lax.fori_loop(0, tiles, step, 0)


def fetch_wide(x, factor, after):
    return pl.pallas_call(
        functools.partial(widen_kernel, factor),
        in_specs=[pl.BlockSpec(memory_space=pl.ANY)] * 2,
        out_specs=pl.BlockSpec(memory_space=pltpu.VMEM),
        out_shape=pltpu.VMEM(x.shape, jnp.float32),
        scratch_shapes=[pltpu.VMEM(x.shape, x.dtype), pltpu.SemaphoreType.DMA((x.shape[0] // TILE,))],
        name="widen",
        **fetch_params(),
    )(in_hbm(x), after)


def fetch_kernel(n, far, far_cot, far_weight, after, near, cot, weights, token_weight, upright, sems, cot_sems):
    height = cot.shape[0] // n
    copy = pltpu.make_async_copy(far, near, sems.at[0])
    weight_copy = pltpu.make_async_copy(far_weight, token_weight, sems.at[1])
    weight_copy.start()
    copy.start()
    places = [pl.multiple_of(place * height, height) for place in owners(n)]
    cot_copies = [
        pltpu.make_async_copy(
            far_cot.at[pl.ds(place, height), :], cot.at[pl.ds(k * height, height), :], cot_sems.at[k]
        )
        for k, place in enumerate(places)
    ]
    for cot_copy in cot_copies:
        cot_copy.start()
    weight_copy.wait()
    upright[...] = jnp.broadcast_to(over_columns(token_weight[...]), upright.shape)
    for k, place in enumerate(places):
        weights[k * height : (k + 1) * height, :] = upright[pl.ds(place, height), :]
    for cot_copy in cot_copies:
        cot_copy.wait()
    copy.wait()


def fetch(n, weight, cot, token_weight, after):
    count = cot.shape[0]
    vmem = pl.BlockSpec(memory_space=pltpu.VMEM)
    return pl.pallas_call(
        functools.partial(fetch_kernel, n),
        in_specs=[pl.BlockSpec(memory_space=pl.ANY)] * 4,
        out_specs=[vmem] * 3,
        out_shape=[
            pltpu.VMEM(weight.shape, weight.dtype),
            pltpu.VMEM(cot.shape, cot.dtype),
            pltpu.VMEM((count, 128), jnp.float32),
        ],
        scratch_shapes=[
            pltpu.VMEM((1, count), jnp.float32),
            pltpu.VMEM((count, 128), jnp.float32),
            pltpu.SemaphoreType.DMA((2,)),
            pltpu.SemaphoreType.DMA((n,)),
        ],
        name="fetch",
        **fetch_params(),
    )(in_hbm(weight), in_hbm(cot), in_hbm(token_weight), after)


def span(i):
    return pl.ds(pl.multiple_of(i * TILE, TILE), TILE)


def gate_rows(blocks, first, sems, weight, tokens, turned, gate, beside):
    height, depth = blocks[0].shape
    count = len(blocks) * height
    rows = slice(first, first + count)
    copies = [
        pltpu.make_async_copy(ref, tokens.at[pl.ds(first + k * height, height), :], sems.at[k])
        for k, ref in enumerate(blocks)
    ]
    for copy in copies:
        copy.start()
    gate[rows, :] = jnp.zeros((count, gate.shape[1]), jnp.float32)
    for copy in copies:
        copy.wait()

    def step(i, _):
        beside(i)
        here = tokens[rows, span(i)]
        gate[rows, :] += f32dot(here, weight[span(i), :])
        turned[span(i), rows] = here.T
        return 0

    lax.fori_loop(0, depth // TILE, step, 0)


def early_kernel(half, *refs):
    blocks, weight, (tokens, turned, gate, sems) = refs[:half], refs[half], refs[half + 1 :]
    gate_rows(blocks, 0, sems, weight, tokens, turned, gate, lambda i: None)


def early_call(blocks, weight, count):
    half = len(blocks)
    depth, width = weight.shape
    vmem = pl.BlockSpec(memory_space=pltpu.VMEM)
    return pl.pallas_call(
        functools.partial(early_kernel, half),
        in_specs=[pl.BlockSpec(memory_space=pl.ANY)] * half + [vmem],
        out_specs=[vmem] * 3,
        out_shape=[
            pltpu.VMEM((count, depth), jnp.bfloat16),
            pltpu.VMEM((depth, count), jnp.bfloat16),
            pltpu.VMEM((count, width), jnp.float32),
        ],
        scratch_shapes=[pltpu.SemaphoreType.DMA((half,))],
        compiler_params=pltpu.CompilerParams(vmem_limit_bytes=4 << 20),
        cost_estimate=pl.CostEstimate(flops=COST, bytes_accessed=12 << 20, transcendentals=0),
        name="early",
    )(*blocks, weight)


def replay_kernel(n, half, *refs):
    blocks, (far, weight, cot, weights, one, two) = refs[:half], refs[half : half + 6]
    (tokens, turned, gate, adjoint, along, across, bend, stats) = refs[half + 9 : half + 17]
    (scaled, score, g0, g1, a0, a1, b0, b1, sums, upright, sems, tile_sems) = refs[half + 17 :]
    grads, firsts, seconds = (g0, g1), (a0, a1), (b0, b1)
    depth = one.shape[0]
    count, width = scaled.shape
    tiles = depth // TILE

    def tile_copy(i):
        return pltpu.make_async_copy(far.at[span(i), :], adjoint.at[span(i), :], tile_sems.at[i])

    gate_rows(blocks, count // 2, sems, weight, tokens, turned, gate, lambda i: tile_copy(i).start())
    for r in range(0, count, 64):
        at = slice(r, r + 64)
        x = gate[at, :]
        token_weight = weights[at, 0:1]
        cot_f = cot[at, :].astype(jnp.float32)
        sig = 1.0 / (1.0 + jnp.exp(-x))
        slope = sig * (1.0 + x * (1.0 - sig))
        curve = sig * (1.0 - sig) * (2.0 + x * (1.0 - 2.0 * sig))
        scaled[at, :] = (token_weight * cot_f * slope).astype(jnp.bfloat16)
        bend[at, :] = token_weight * cot_f * curve
        score[at, :] = cot_f * slope

    along[...] = jnp.zeros_like(along)
    across[...] = jnp.zeros_like(across)

    def grad_rows(i, slot, r):
        at = pl.ds(pl.multiple_of(i * TILE + r, QUARTER), QUARTER)
        grads[slot][r : r + QUARTER, :] = f32dot(turned[at, :], scaled[...])

    units = [
        (target, terms, slice(c, min(c + COLUMNS, width)))
        for target, terms in ((along, firsts), (across, seconds))
        for c in range(0, width, COLUMNS)
    ]

    def probe(i, slot, unit):
        target, terms, cols = unit
        target[:, cols] += f32dot(tokens[:, span(i)], terms[slot][:, cols])

    def pieces(i, slot, first, last):
        for r in range(first, last, ROWS):
            at = pl.ds(pl.multiple_of(i * TILE + r, ROWS), ROWS)
            for c in range(0, width, COLUMNS):
                cols = slice(c, min(c + COLUMNS, width))
                yield r, cols, grads[slot][r : r + ROWS, cols], one[at, cols], two[at, cols], adjoint[at, cols]

    for i in range(2):
        tile_copy(i).wait()
    for r in range(0, TILE, QUARTER):
        grad_rows(0, 0, r)
    sq, cross = {}, {}
    for r, cols, g, m1, m2, adj in pieces(0, 0, 0, SAMPLE):
        _, _, upd = update(g, m1, m2)
        sq[cols.start] = sq.get(cols.start, 0.0) + fold(upd * upd)
        cross[cols.start] = cross.get(cols.start, 0.0) + fold(adj * upd)
    sq = jnp.sum(sum(sq.values()), keepdims=True)
    cross = jnp.sum(sum(cross.values()), keepdims=True)
    clipped = sq * RATIO**2 > float(SAMPLE * width)
    guess = jnp.where(clipped, cross / jnp.maximum(sq, 1.0), 0.0)

    sums[...] = jnp.zeros_like(sums)

    def update_rows(i, slot, first, last):
        sq, cross = {}, {}
        for r, cols, g, m1, m2, adj in pieces(i, slot, first, last):
            over, inv, upd = update(g, m1, m2)
            sq[cols.start] = sq.get(cols.start, 0.0) + fold(upd * upd)
            cross[cols.start] = cross.get(cols.start, 0.0) + fold(adj * upd)
            pull = inv * (1.0 - g * (upd * over))
            firsts[slot][r : r + ROWS, cols] = ((adj - guess * upd) * pull).astype(jnp.bfloat16)
            seconds[slot][r : r + ROWS, cols] = (upd * pull).astype(jnp.bfloat16)
        sums[0] += sum(sq.values())
        sums[1] += sum(cross.values())

    def body(i, slot, ahead=True, behind=True):
        quarters = TILE // QUARTER
        for q in range(quarters):
            r = q * QUARTER
            if ahead:
                grad_rows(i + 1, 1 - slot, r)
            update_rows(i, slot, r, r + QUARTER // 2)
            if behind:
                for unit in units[q::quarters]:
                    probe(i - 1, 1 - slot, unit)
            update_rows(i, slot, r + QUARTER // 2, r + QUARTER)

    body(0, 0, behind=False)

    def pair(k, _):
        tile_copy(2 * k + 2).wait()
        tile_copy(2 * k + 3).wait()
        body(2 * k + 1, 1)
        body(2 * k + 2, 0)
        return 0

    lax.fori_loop(0, tiles // 2 - 1, pair, 0)
    body(tiles - 1, 1, ahead=False)
    for unit in units:
        probe(tiles - 1, 1, unit)

    height = count // n
    places = owners(n)

    def spread(x):
        x = sum(x[:, i : i + 128] for i in range(0, width, 128))
        for k, place in enumerate(places):
            upright[pl.ds(pl.multiple_of(place * height, height), height), :] = x[k * height : (k + 1) * height, :]
        return jnp.sum(jnp.transpose(upright[...]), axis=0, keepdims=True)

    b = score[...] * across[...]
    a = score[...] * along[...] + guess * b
    whole = lambda x: jnp.broadcast_to(jnp.sum(x, keepdims=True), (1, count))
    stats[0:1, :] = RATIO * spread(a)
    stats[1:2, :] = RATIO**2 * spread(b)
    stats[2:3, :] = RATIO**2 * whole(sums[0])
    stats[3:4, :] = RATIO * whole(sums[1])
    stats[4:8, :] = jnp.broadcast_to(guess, (4, count))


def replay_call(n, blocks, adjoint, weight, cot, weights, one, two, tokens, turned, gate):
    half = len(blocks)
    depth = one.shape[0]
    count, width = cot.shape
    far = pl.BlockSpec(memory_space=pl.ANY)
    vmem = pl.BlockSpec(memory_space=pltpu.VMEM)
    like = lambda x: pltpu.VMEM(x.shape, x.dtype)
    block = lambda dtype: pltpu.VMEM((TILE, width), dtype)
    return pl.pallas_call(
        functools.partial(replay_kernel, n, half),
        in_specs=[far] * (half + 1) + [vmem] * 8,
        out_specs=[vmem] * 8,
        out_shape=[
            like(tokens),
            like(turned),
            like(gate),
            pltpu.VMEM((depth, width), jnp.float32),
            pltpu.VMEM((count, width), jnp.float32),
            pltpu.VMEM((count, width), jnp.float32),
            pltpu.VMEM((count, width), jnp.float32),
            pltpu.VMEM((8, count), jnp.float32),
        ],
        scratch_shapes=[
            pltpu.VMEM((count, width), jnp.bfloat16),
            pltpu.VMEM((count, width), jnp.float32),
            block(jnp.float32),
            block(jnp.float32),
            block(jnp.bfloat16),
            block(jnp.bfloat16),
            block(jnp.bfloat16),
            block(jnp.bfloat16),
            pltpu.VMEM((2, 8, min(COLUMNS, width)), jnp.float32),
            pltpu.VMEM((count, 128), jnp.float32),
            pltpu.SemaphoreType.DMA((half,)),
            pltpu.SemaphoreType.DMA((depth // TILE,)),
        ],
        input_output_aliases={half + 6: 0, half + 7: 1, half + 8: 2},
        compiler_params=pltpu.CompilerParams(vmem_limit_bytes=VMEM_BYTES),
        name="replay",
    )(*blocks, in_hbm(adjoint), weight, cot, weights, one, two, tokens, turned, gate)


def in_hbm(x):
    return pltpu.with_memory_space_constraint(x, pltpu.HBM)


def theta_kernel(n, entries, s0, s1, s2, s3, own, along, across, bend, turned, adjoint, theta, scores, ready, sent):
    total = s0[...] + s1[...] + (s2[...] + s3[...])
    sq, cross = total[2:3, 0:1], total[3:4, 0:1]
    rms = jnp.sqrt(sq / entries)
    scale = 1.0 / jnp.maximum(1.0, rms)
    bind = jnp.where(rms > 1.0, 1.0 / (rms * rms * rms), 0.0)
    lead = -0.01 * scale
    rest = 0.01 * cross * bind / entries
    mine = lead * total[0:8, :] + rest * pltpu.roll(total, 7, 0)
    count = total.shape[1]
    height = count // n
    mine = pltpu.roll(mine, lax.rem(count - lax.axis_index("dp") * height, count), 1)
    scores[...] = mine[0:1, 0:height]
    lead_here = RATIO * lead
    rest_here = RATIO**2 * rest + lead_here * own[4:5, 0:1]
    bent = (bend[...] * (lead_here * along[...] + rest_here * across[...])).astype(jnp.bfloat16)

    def copy(i):
        at = pl.ds(i * SAMPLE, SAMPLE)
        return pltpu.make_async_copy(ready.at[at, :], theta.at[at, :], sent.at[i])

    tiles = theta.shape[0] // SAMPLE
    for i in range(tiles):
        at = pl.ds(i * SAMPLE, SAMPLE)
        ready[at, :] = 0.999 * adjoint[at, :] + f32dot(turned[at, :], bent)
        copy(i).start()
    for i in range(tiles):
        copy(i).wait()


def theta_call(n, entries, sums, own, along, across, bend, turned, adjoint):
    depth, width = adjoint.shape
    count = turned.shape[1]
    vmem = pl.BlockSpec(memory_space=pltpu.VMEM)
    return pl.pallas_call(
        functools.partial(theta_kernel, n, entries),
        in_specs=[vmem] * 10,
        out_specs=[pl.BlockSpec(memory_space=pl.ANY), vmem],
        out_shape=[
            jax.ShapeDtypeStruct((depth, width), jnp.float32),
            jax.ShapeDtypeStruct((1, count // n), jnp.float32),
        ],
        scratch_shapes=[pltpu.VMEM((depth, width), jnp.float32), pltpu.SemaphoreType.DMA((depth // SAMPLE,))],
        compiler_params=pltpu.CompilerParams(vmem_limit_bytes=VMEM_BYTES),
        name="theta",
    )(*sums, own, along, across, bend, turned, adjoint)


def shards(n, tokens, cotangent, token_weight, weight, moment_one, moment_two, adjoint):
    entries = float(adjoint.shape[0] * adjoint.shape[1] * n)
    errands = [
        lambda after: fetch(n, weight, cotangent, token_weight.reshape(1, -1), after),
        lambda after: fetch_wide(moment_one, 9.0, after),
        lambda after: fetch_wide(moment_two, 19.0, after),
    ]
    blocks, ((weight_near, cot, weights), one, two) = gather(tokens, n, errands)
    half = len(blocks) // 2
    rows, turned, gate = early_call(blocks[:half], weight_near, cot.shape[0])
    _, turned, _, adjoint_near, along, across, bend, stats = replay_call(
        n, blocks[half:], adjoint, weight_near, cot, weights, one, two, rows, turned, gate
    )
    sums = all_sum(stats, n)
    theta_bar, scores = theta_call(n, entries, sums, stats, along, across, bend, turned, adjoint_near)
    return (theta_bar, scores.reshape(-1))


def solution(mesh):
    in_specs = (
        P(("group", "dp"), None),
        P("group", "dp"),
        P("group"),
        P(None, "dp"),
        P(None, "dp"),
        P(None, "dp"),
        P(None, "dp"),
    )
    out_specs = (P("group", "dp"), P(("group", "dp")))
    body = functools.partial(shards, mesh.shape["dp"])
    return jax.shard_map(body, mesh=mesh, in_specs=in_specs, out_specs=out_specs, check_vma=False)
```

```python
import functools

import jax
import jax.numpy as jnp
from jax import lax
from jax.experimental import pallas as pl
from jax.experimental.pallas import tpu as pltpu
from jax.sharding import PartitionSpec as P

TILE = 512
HALF = 256
ROWS = 16
COLUMNS = 256
COST = 4 << 30
SAMPLE = 256
VMEM_BYTES = 12 << 20
TN = (((0,), (0,)), ((), ()))
RATIO = 0.1 / 0.05**0.5


def f32dot(a, b):
    return jnp.dot(a, b, preferred_element_type=jnp.float32)


def swapped(value, n, mask):
    return lax.ppermute(value, "dp", [(d ^ mask, d) for d in range(n)])


def ring(n):
    chips = n // 2
    return [*range(0, chips, 2), *range(chips - 1 - chips % 2, 0, -2)]


def onward(value, n):
    order = ring(n)
    pairs = []
    for i, chip in enumerate(order):
        pairs.append((2 * order[i - 1], 2 * chip))
        pairs.append((2 * order[(i + 1) % len(order)] + 1, 2 * chip + 1))
    return lax.ppermute(value, "dp", pairs)


def gather(tokens, n, errands):
    hops = n // 4
    done = []
    here = [tokens, swapped(tokens, n, 1)]
    parts = list(here)
    for hop in range(1, hops + 1):
        after = in_hbm(tokens) if hop == 1 else here[0]
        here = [onward(x, n) for x in here]
        if errands[len(done) :]:
            done.append(errands[len(done)](after))
        parts += here
        if hop < hops:
            parts += [swapped(x, n, 1) for x in here]
    return parts, done


def owners(n):
    chips = n // 2
    me = lax.axis_index("dp")
    chip, core = me >> 1, me & 1
    at = jnp.where(chip & 1 == 0, chip >> 1, chips - 1 - (chip >> 1))
    way = 2 * core - 1
    blocks = [(0, core)]
    for hop in range(1, chips // 2 + 1):
        blocks.append((way * hop, core))
        if 2 * hop < chips:
            blocks.append((-way * hop, 1 - core))
    places = []
    for step, first in blocks:
        there = at + step
        there = jnp.where(there < 0, there + chips, jnp.where(there >= chips, there - chips, there))
        source = jnp.where(there < chips // 2, 2 * there, 2 * (chips - 1 - there) + 1)
        places += [2 * source + first, 2 * source + 1 - first]
    return places


def all_sum(value, n):
    total = value
    for mask in range(4, n, 4):
        total = total + swapped(value, n, mask)
    return [total] + [swapped(total, n, mask) for mask in (1, 2, 3)]


def over_columns(row):
    return jnp.transpose(jnp.broadcast_to(row, (8, row.shape[1])))[:, :1]


def fold(x):
    return jnp.sum(x.reshape(x.shape[0] // 8, 8, x.shape[1]), axis=0)


def update(grad, one, two):
    first = one + grad
    second = two + grad * grad
    over = lax.rsqrt(second)
    inv = pltpu.reciprocal(second * over + 1e-08 / 0.05**0.5, approx=True)
    return over, inv, first * inv


def fetch_params():
    return {
        "compiler_params": pltpu.CompilerParams(vmem_limit_bytes=6 << 20),
        "cost_estimate": pl.CostEstimate(flops=COST, bytes_accessed=8 << 20, transcendentals=0),
    }


def widen_kernel(factor, far, after, near, raw, sems):
    tiles = far.shape[0] // TILE

    def copy(i):
        return pltpu.make_async_copy(far.at[span(i), :], raw.at[span(i), :], sems.at[i])

    for i in range(tiles):
        copy(i).start()

    def step(i, _):
        copy(i).wait()
        near[span(i), :] = factor * raw[span(i), :].astype(jnp.float32)
        return 0

    lax.fori_loop(0, tiles, step, 0)


def fetch_wide(x, factor, after):
    return pl.pallas_call(
        functools.partial(widen_kernel, factor),
        in_specs=[pl.BlockSpec(memory_space=pl.ANY)] * 2,
        out_specs=pl.BlockSpec(memory_space=pltpu.VMEM),
        out_shape=pltpu.VMEM(x.shape, jnp.float32),
        scratch_shapes=[pltpu.VMEM(x.shape, x.dtype), pltpu.SemaphoreType.DMA((x.shape[0] // TILE,))],
        name="widen",
        **fetch_params(),
    )(in_hbm(x), after)


def fetch_kernel(n, far, far_cot, far_weight, after, near, cot, weights, token_weight, upright, sems, cot_sems):
    height = cot.shape[0] // n
    copy = pltpu.make_async_copy(far, near, sems.at[0])
    weight_copy = pltpu.make_async_copy(far_weight, token_weight, sems.at[1])
    weight_copy.start()
    copy.start()
    places = [pl.multiple_of(place * height, height) for place in owners(n)]
    cot_copies = [
        pltpu.make_async_copy(
            far_cot.at[pl.ds(place, height), :], cot.at[pl.ds(k * height, height), :], cot_sems.at[k]
        )
        for k, place in enumerate(places)
    ]
    for cot_copy in cot_copies:
        cot_copy.start()
    weight_copy.wait()
    upright[...] = jnp.broadcast_to(over_columns(token_weight[...]), upright.shape)
    for k, place in enumerate(places):
        weights[k * height : (k + 1) * height, :] = upright[pl.ds(place, height), :]
    for cot_copy in cot_copies:
        cot_copy.wait()
    copy.wait()


def fetch(n, weight, cot, token_weight, after):
    count = cot.shape[0]
    vmem = pl.BlockSpec(memory_space=pltpu.VMEM)
    return pl.pallas_call(
        functools.partial(fetch_kernel, n),
        in_specs=[pl.BlockSpec(memory_space=pl.ANY)] * 4,
        out_specs=[vmem] * 3,
        out_shape=[
            pltpu.VMEM(weight.shape, weight.dtype),
            pltpu.VMEM(cot.shape, cot.dtype),
            pltpu.VMEM((count, 128), jnp.float32),
        ],
        scratch_shapes=[
            pltpu.VMEM((1, count), jnp.float32),
            pltpu.VMEM((count, 128), jnp.float32),
            pltpu.SemaphoreType.DMA((2,)),
            pltpu.SemaphoreType.DMA((n,)),
        ],
        name="fetch",
        **fetch_params(),
    )(in_hbm(weight), in_hbm(cot), in_hbm(token_weight), after)


def span(i):
    return pl.ds(pl.multiple_of(i * TILE, TILE), TILE)


def gate_rows(blocks, first, sems, weight, tokens, turned, gate, beside):
    height, depth = blocks[0].shape
    count = len(blocks) * height
    rows = slice(first, first + count)
    copies = [
        pltpu.make_async_copy(ref, tokens.at[pl.ds(first + k * height, height), :], sems.at[k])
        for k, ref in enumerate(blocks)
    ]
    for copy in copies:
        copy.start()
    gate[rows, :] = jnp.zeros((count, gate.shape[1]), jnp.float32)
    for copy in copies:
        copy.wait()

    def step(i, _):
        beside(i)
        here = tokens[rows, span(i)]
        gate[rows, :] += f32dot(here, weight[span(i), :])
        turned[span(i), rows] = here.T
        return 0

    lax.fori_loop(0, depth // TILE, step, 0)


def early_kernel(half, *refs):
    blocks, weight, (tokens, turned, gate, sems) = refs[:half], refs[half], refs[half + 1 :]
    gate_rows(blocks, 0, sems, weight, tokens, turned, gate, lambda i: None)


def early_call(blocks, weight, count):
    half = len(blocks)
    depth, width = weight.shape
    vmem = pl.BlockSpec(memory_space=pltpu.VMEM)
    return pl.pallas_call(
        functools.partial(early_kernel, half),
        in_specs=[pl.BlockSpec(memory_space=pl.ANY)] * half + [vmem],
        out_specs=[vmem] * 3,
        out_shape=[
            pltpu.VMEM((count, depth), jnp.bfloat16),
            pltpu.VMEM((depth, count), jnp.bfloat16),
            pltpu.VMEM((count, width), jnp.float32),
        ],
        scratch_shapes=[pltpu.SemaphoreType.DMA((half,))],
        compiler_params=pltpu.CompilerParams(vmem_limit_bytes=4 << 20),
        cost_estimate=pl.CostEstimate(flops=COST, bytes_accessed=12 << 20, transcendentals=0),
        name="early",
    )(*blocks, weight)


def replay_kernel(n, half, *refs):
    blocks, (far, weight, cot, weights, one, two) = refs[:half], refs[half : half + 6]
    (tokens, turned, gate, adjoint, along, across, bend, stats) = refs[half + 9 : half + 17]
    (scaled, score, g0, g1, t0, t1, probes, sums, upright, sems, tile_sems) = refs[half + 17 :]
    grads, terms = (g0, g1), (t0, t1)
    depth = one.shape[0]
    count, width = scaled.shape
    tiles = depth // TILE

    def tile_copy(i):
        return pltpu.make_async_copy(far.at[span(i), :], adjoint.at[span(i), :], tile_sems.at[i])

    gate_rows(blocks, count // 2, sems, weight, tokens, turned, gate, lambda i: tile_copy(i).start())
    for r in range(0, count, 64):
        at = slice(r, r + 64)
        x = gate[at, :]
        token_weight = weights[at, 0:1]
        cot_f = cot[at, :].astype(jnp.float32)
        sig = 1.0 / (1.0 + jnp.exp(-x))
        slope = sig * (1.0 + x * (1.0 - sig))
        curve = sig * (1.0 - sig) * (2.0 + x * (1.0 - 2.0 * sig))
        scaled[at, :] = (token_weight * cot_f * slope).astype(jnp.bfloat16)
        bend[at, :] = token_weight * cot_f * curve
        score[at, :] = cot_f * slope

    probes[...] = jnp.zeros_like(probes)

    def grad_rows(i, slot, r):
        at = pl.ds(pl.multiple_of(i * TILE + r, HALF), HALF)
        grads[slot][r : r + HALF, :] = f32dot(turned[at, :], scaled[...])

    def probe(i, slot):
        probes[...] += lax.dot_general(
            terms[slot][...], turned[span(i), :], TN, preferred_element_type=jnp.float32
        )

    def pieces(i, slot, first, last):
        for r in range(first, last, ROWS):
            at = pl.ds(pl.multiple_of(i * TILE + r, ROWS), ROWS)
            for c in range(0, width, COLUMNS):
                cols = slice(c, min(c + COLUMNS, width))
                yield r, cols, grads[slot][r : r + ROWS, cols], one[at, cols], two[at, cols], adjoint[at, cols]

    for i in range(2):
        tile_copy(i).wait()
    for r in range(0, TILE, HALF):
        grad_rows(0, 0, r)
    sq, cross = {}, {}
    for r, cols, g, m1, m2, adj in pieces(0, 0, 0, SAMPLE):
        _, _, upd = update(g, m1, m2)
        sq[cols.start] = sq.get(cols.start, 0.0) + fold(upd * upd)
        cross[cols.start] = cross.get(cols.start, 0.0) + fold(adj * upd)
    sq = jnp.sum(sum(sq.values()), keepdims=True)
    cross = jnp.sum(sum(cross.values()), keepdims=True)
    clipped = sq * RATIO**2 > float(SAMPLE * width)
    guess = jnp.where(clipped, cross / jnp.maximum(sq, 1.0), 0.0)

    sums[...] = jnp.zeros_like(sums)

    def update_rows(i, slot, first, last):
        sq, cross = {}, {}
        for r, cols, g, m1, m2, adj in pieces(i, slot, first, last):
            over, inv, upd = update(g, m1, m2)
            sq[cols.start] = sq.get(cols.start, 0.0) + fold(upd * upd)
            cross[cols.start] = cross.get(cols.start, 0.0) + fold(adj * upd)
            pull = inv * (1.0 - g * (upd * over))
            others = slice(width + cols.start, width + cols.stop)
            terms[slot][r : r + ROWS, cols] = ((adj - guess * upd) * pull).astype(jnp.bfloat16)
            terms[slot][r : r + ROWS, others] = (upd * pull).astype(jnp.bfloat16)
        sums[0] += sum(sq.values())
        sums[1] += sum(cross.values())

    def body(i, slot, ahead=True, behind=True):
        for r in range(0, TILE, HALF):
            if ahead:
                grad_rows(i + 1, 1 - slot, r)
            update_rows(i, slot, r, r + HALF)
            if behind and r == 0:
                probe(i - 1, 1 - slot)

    body(0, 0, behind=False)

    def pair(k, _):
        tile_copy(2 * k + 2).wait()
        tile_copy(2 * k + 3).wait()
        body(2 * k + 1, 1)
        body(2 * k + 2, 0)
        return 0

    lax.fori_loop(0, tiles // 2 - 1, pair, 0)
    body(tiles - 1, 1, ahead=False)
    probe(tiles - 1, 1)
    along[...] = probes[0:width, :].T
    across[...] = probes[width:, :].T

    height = count // n
    places = owners(n)

    def spread(x):
        x = sum(x[:, i : i + 128] for i in range(0, width, 128))
        for k, place in enumerate(places):
            upright[pl.ds(pl.multiple_of(place * height, height), height), :] = x[k * height : (k + 1) * height, :]
        return jnp.sum(jnp.transpose(upright[...]), axis=0, keepdims=True)

    b = score[...] * across[...]
    a = score[...] * along[...] + guess * b
    whole = lambda x: jnp.broadcast_to(jnp.sum(x, keepdims=True), (1, count))
    stats[0:1, :] = RATIO * spread(a)
    stats[1:2, :] = RATIO**2 * spread(b)
    stats[2:3, :] = RATIO**2 * whole(sums[0])
    stats[3:4, :] = RATIO * whole(sums[1])
    stats[4:8, :] = jnp.broadcast_to(guess, (4, count))


def replay_call(n, blocks, adjoint, weight, cot, weights, one, two, tokens, turned, gate):
    half = len(blocks)
    depth = one.shape[0]
    count, width = cot.shape
    far = pl.BlockSpec(memory_space=pl.ANY)
    vmem = pl.BlockSpec(memory_space=pltpu.VMEM)
    like = lambda x: pltpu.VMEM(x.shape, x.dtype)
    return pl.pallas_call(
        functools.partial(replay_kernel, n, half),
        in_specs=[far] * (half + 1) + [vmem] * 8,
        out_specs=[vmem] * 8,
        out_shape=[
            like(tokens),
            like(turned),
            like(gate),
            pltpu.VMEM((depth, width), jnp.float32),
            pltpu.VMEM((count, width), jnp.float32),
            pltpu.VMEM((count, width), jnp.float32),
            pltpu.VMEM((count, width), jnp.float32),
            pltpu.VMEM((8, count), jnp.float32),
        ],
        scratch_shapes=[
            pltpu.VMEM((count, width), jnp.bfloat16),
            pltpu.VMEM((count, width), jnp.float32),
            pltpu.VMEM((TILE, width), jnp.float32),
            pltpu.VMEM((TILE, width), jnp.float32),
            pltpu.VMEM((TILE, 2 * width), jnp.bfloat16),
            pltpu.VMEM((TILE, 2 * width), jnp.bfloat16),
            pltpu.VMEM((2 * width, count), jnp.float32),
            pltpu.VMEM((2, 8, min(COLUMNS, width)), jnp.float32),
            pltpu.VMEM((count, 128), jnp.float32),
            pltpu.SemaphoreType.DMA((half,)),
            pltpu.SemaphoreType.DMA((depth // TILE,)),
        ],
        input_output_aliases={half + 6: 0, half + 7: 1, half + 8: 2},
        compiler_params=pltpu.CompilerParams(vmem_limit_bytes=VMEM_BYTES),
        name="replay",
    )(*blocks, in_hbm(adjoint), weight, cot, weights, one, two, tokens, turned, gate)


def in_hbm(x):
    return pltpu.with_memory_space_constraint(x, pltpu.HBM)


def theta_kernel(n, entries, s0, s1, s2, s3, own, along, across, bend, turned, adjoint, theta, scores, ready, sent):
    total = s0[...] + s1[...] + (s2[...] + s3[...])
    sq, cross = total[2:3, 0:1], total[3:4, 0:1]
    rms = jnp.sqrt(sq / entries)
    scale = 1.0 / jnp.maximum(1.0, rms)
    bind = jnp.where(rms > 1.0, 1.0 / (rms * rms * rms), 0.0)
    lead = -0.01 * scale
    rest = 0.01 * cross * bind / entries
    mine = lead * total[0:8, :] + rest * pltpu.roll(total, 7, 0)
    count = total.shape[1]
    height = count // n
    mine = pltpu.roll(mine, lax.rem(count - lax.axis_index("dp") * height, count), 1)
    scores[...] = mine[0:1, 0:height]
    lead_here = RATIO * lead
    rest_here = RATIO**2 * rest + lead_here * own[4:5, 0:1]
    bent = (bend[...] * (lead_here * along[...] + rest_here * across[...])).astype(jnp.bfloat16)

    def copy(i):
        at = pl.ds(i * SAMPLE, SAMPLE)
        return pltpu.make_async_copy(ready.at[at, :], theta.at[at, :], sent.at[i])

    tiles = theta.shape[0] // SAMPLE
    for i in range(tiles):
        at = pl.ds(i * SAMPLE, SAMPLE)
        ready[at, :] = 0.999 * adjoint[at, :] + f32dot(turned[at, :], bent)
        copy(i).start()
    for i in range(tiles):
        copy(i).wait()


def theta_call(n, entries, sums, own, along, across, bend, turned, adjoint):
    depth, width = adjoint.shape
    count = turned.shape[1]
    vmem = pl.BlockSpec(memory_space=pltpu.VMEM)
    return pl.pallas_call(
        functools.partial(theta_kernel, n, entries),
        in_specs=[vmem] * 10,
        out_specs=[pl.BlockSpec(memory_space=pl.ANY), vmem],
        out_shape=[
            jax.ShapeDtypeStruct((depth, width), jnp.float32),
            jax.ShapeDtypeStruct((1, count // n), jnp.float32),
        ],
        scratch_shapes=[pltpu.VMEM((depth, width), jnp.float32), pltpu.SemaphoreType.DMA((depth // SAMPLE,))],
        compiler_params=pltpu.CompilerParams(vmem_limit_bytes=VMEM_BYTES),
        name="theta",
    )(*sums, own, along, across, bend, turned, adjoint)


def shards(n, tokens, cotangent, token_weight, weight, moment_one, moment_two, adjoint):
    entries = float(adjoint.shape[0] * adjoint.shape[1] * n)
    errands = [
        lambda after: fetch(n, weight, cotangent, token_weight.reshape(1, -1), after),
        lambda after: fetch_wide(moment_one, 9.0, after),
        lambda after: fetch_wide(moment_two, 19.0, after),
    ]
    blocks, ((weight_near, cot, weights), one, two) = gather(tokens, n, errands)
    half = len(blocks) // 2
    rows, turned, gate = early_call(blocks[:half], weight_near, cot.shape[0])
    _, turned, _, adjoint_near, along, across, bend, stats = replay_call(
        n, blocks[half:], adjoint, weight_near, cot, weights, one, two, rows, turned, gate
    )
    sums = all_sum(stats, n)
    theta_bar, scores = theta_call(n, entries, sums, stats, along, across, bend, turned, adjoint_near)
    return (theta_bar, scores.reshape(-1))


def solution(mesh):
    in_specs = (
        P(("group", "dp"), None),
        P("group", "dp"),
        P("group"),
        P(None, "dp"),
        P(None, "dp"),
        P(None, "dp"),
        P(None, "dp"),
    )
    out_specs = (P("group", "dp"), P(("group", "dp")))
    body = functools.partial(shards, mesh.shape["dp"])
    return jax.shard_map(body, mesh=mesh, in_specs=in_specs, out_specs=out_specs, check_vma=False)
```

```python
import functools

import jax
import jax.numpy as jnp
from jax import lax
from jax.experimental import pallas as pl
from jax.experimental.pallas import tpu as pltpu
from jax.sharding import PartitionSpec as P

TILE = 512
HALF = 256
ROWS = 16
COLUMNS = 256
COST = 4 << 30
SAMPLE = 256
VMEM_BYTES = 12 << 20
RATIO = 0.1 / 0.05**0.5


def f32dot(a, b):
    return jnp.dot(a, b, preferred_element_type=jnp.float32)


def swapped(value, n, mask):
    return lax.ppermute(value, "dp", [(d ^ mask, d) for d in range(n)])


def ring(n):
    chips = n // 2
    return [*range(0, chips, 2), *range(chips - 1 - chips % 2, 0, -2)]


def onward(value, n):
    order = ring(n)
    pairs = []
    for i, chip in enumerate(order):
        pairs.append((2 * order[i - 1], 2 * chip))
        pairs.append((2 * order[(i + 1) % len(order)] + 1, 2 * chip + 1))
    return lax.ppermute(value, "dp", pairs)


def gather(tokens, n, errands):
    hops = n // 4
    done = []
    here = [tokens, swapped(tokens, n, 1)]
    parts = list(here)
    for hop in range(1, hops + 1):
        after = in_hbm(tokens) if hop == 1 else here[0]
        here = [onward(x, n) for x in here]
        if errands[len(done) :]:
            done.append(errands[len(done)](after))
        parts += here
        if hop < hops:
            parts += [swapped(x, n, 1) for x in here]
    return parts, done


def owners(n):
    chips = n // 2
    me = lax.axis_index("dp")
    chip, core = me >> 1, me & 1
    at = jnp.where(chip & 1 == 0, chip >> 1, chips - 1 - (chip >> 1))
    way = 2 * core - 1
    blocks = [(0, core)]
    for hop in range(1, chips // 2 + 1):
        blocks.append((way * hop, core))
        if 2 * hop < chips:
            blocks.append((-way * hop, 1 - core))
    places = []
    for step, first in blocks:
        there = at + step
        there = jnp.where(there < 0, there + chips, jnp.where(there >= chips, there - chips, there))
        source = jnp.where(there < chips // 2, 2 * there, 2 * (chips - 1 - there) + 1)
        places += [2 * source + first, 2 * source + 1 - first]
    return places


def all_sum(value, n):
    total = value
    for mask in range(4, n, 4):
        total = total + swapped(value, n, mask)
    return [total] + [swapped(total, n, mask) for mask in (1, 2, 3)]


def over_columns(row):
    return jnp.transpose(jnp.broadcast_to(row, (8, row.shape[1])))[:, :1]


def fold(x):
    return jnp.sum(x.reshape(x.shape[0] // 8, 8, x.shape[1]), axis=0)


def update(grad, one, two):
    first = one + grad
    second = two + grad * grad
    over = lax.rsqrt(second)
    den = second * over + 1e-08 / 0.05**0.5
    inv = over * (2.0 - den * over)
    return over, inv, first * inv


def fetch_params():
    return {
        "compiler_params": pltpu.CompilerParams(vmem_limit_bytes=6 << 20),
        "cost_estimate": pl.CostEstimate(flops=COST, bytes_accessed=8 << 20, transcendentals=0),
    }


def widen_kernel(factor, far, after, near, raw, sems):
    tiles = far.shape[0] // TILE

    def copy(i):
        return pltpu.make_async_copy(far.at[span(i), :], raw.at[span(i), :], sems.at[i])

    for i in range(tiles):
        copy(i).start()

    def step(i, _):
        copy(i).wait()
        near[span(i), :] = factor * raw[span(i), :].astype(jnp.float32)
        return 0

    lax.fori_loop(0, tiles, step, 0)


def fetch_wide(x, factor, after):
    return pl.pallas_call(
        functools.partial(widen_kernel, factor),
        in_specs=[pl.BlockSpec(memory_space=pl.ANY)] * 2,
        out_specs=pl.BlockSpec(memory_space=pltpu.VMEM),
        out_shape=pltpu.VMEM(x.shape, jnp.float32),
        scratch_shapes=[pltpu.VMEM(x.shape, x.dtype), pltpu.SemaphoreType.DMA((x.shape[0] // TILE,))],
        name="widen",
        **fetch_params(),
    )(in_hbm(x), after)


def fetch_kernel(n, far, far_cot, far_weight, after, near, cot, weights, token_weight, upright, sems, cot_sems):
    height = cot.shape[0] // n
    copy = pltpu.make_async_copy(far, near, sems.at[0])
    weight_copy = pltpu.make_async_copy(far_weight, token_weight, sems.at[1])
    weight_copy.start()
    copy.start()
    places = [pl.multiple_of(place * height, height) for place in owners(n)]
    cot_copies = [
        pltpu.make_async_copy(
            far_cot.at[pl.ds(place, height), :], cot.at[pl.ds(k * height, height), :], cot_sems.at[k]
        )
        for k, place in enumerate(places)
    ]
    for cot_copy in cot_copies:
        cot_copy.start()
    weight_copy.wait()
    upright[...] = jnp.broadcast_to(over_columns(token_weight[...]), upright.shape)
    for k, place in enumerate(places):
        weights[k * height : (k + 1) * height, :] = upright[pl.ds(place, height), :]
    for cot_copy in cot_copies:
        cot_copy.wait()
    copy.wait()


def fetch(n, weight, cot, token_weight, after):
    count = cot.shape[0]
    vmem = pl.BlockSpec(memory_space=pltpu.VMEM)
    return pl.pallas_call(
        functools.partial(fetch_kernel, n),
        in_specs=[pl.BlockSpec(memory_space=pl.ANY)] * 4,
        out_specs=[vmem] * 3,
        out_shape=[
            pltpu.VMEM(weight.shape, weight.dtype),
            pltpu.VMEM(cot.shape, cot.dtype),
            pltpu.VMEM((count, 128), jnp.float32),
        ],
        scratch_shapes=[
            pltpu.VMEM((1, count), jnp.float32),
            pltpu.VMEM((count, 128), jnp.float32),
            pltpu.SemaphoreType.DMA((2,)),
            pltpu.SemaphoreType.DMA((n,)),
        ],
        name="fetch",
        **fetch_params(),
    )(in_hbm(weight), in_hbm(cot), in_hbm(token_weight), after)


def span(i):
    return pl.ds(pl.multiple_of(i * TILE, TILE), TILE)


def gate_rows(blocks, first, sems, weight, tokens, turned, gate, beside):
    height, depth = blocks[0].shape
    count = len(blocks) * height
    rows = slice(first, first + count)
    copies = [
        pltpu.make_async_copy(ref, tokens.at[pl.ds(first + k * height, height), :], sems.at[k])
        for k, ref in enumerate(blocks)
    ]
    for copy in copies:
        copy.start()
    gate[rows, :] = jnp.zeros((count, gate.shape[1]), jnp.float32)
    for copy in copies:
        copy.wait()

    def step(i, _):
        beside(i)
        here = tokens[rows, span(i)]
        gate[rows, :] += f32dot(here, weight[span(i), :])
        turned[span(i), rows] = here.T
        return 0

    lax.fori_loop(0, depth // TILE, step, 0)


def early_kernel(half, *refs):
    blocks, weight, (tokens, turned, gate, sems) = refs[:half], refs[half], refs[half + 1 :]
    gate_rows(blocks, 0, sems, weight, tokens, turned, gate, lambda i: None)


def early_call(blocks, weight, count):
    half = len(blocks)
    depth, width = weight.shape
    vmem = pl.BlockSpec(memory_space=pltpu.VMEM)
    return pl.pallas_call(
        functools.partial(early_kernel, half),
        in_specs=[pl.BlockSpec(memory_space=pl.ANY)] * half + [vmem],
        out_specs=[vmem] * 3,
        out_shape=[
            pltpu.VMEM((count, depth), jnp.bfloat16),
            pltpu.VMEM((depth, count), jnp.bfloat16),
            pltpu.VMEM((count, width), jnp.float32),
        ],
        scratch_shapes=[pltpu.SemaphoreType.DMA((half,))],
        compiler_params=pltpu.CompilerParams(vmem_limit_bytes=4 << 20),
        cost_estimate=pl.CostEstimate(flops=COST, bytes_accessed=12 << 20, transcendentals=0),
        name="early",
    )(*blocks, weight)


def replay_kernel(n, half, *refs):
    blocks, (far, weight, cot, weights, one, two) = refs[:half], refs[half : half + 6]
    (tokens, turned, gate, adjoint, along, across, bend, stats) = refs[half + 9 : half + 17]
    (scaled, score, g0, g1, a0, a1, b0, b1, sums, upright, sems, tile_sems) = refs[half + 17 :]
    grads, firsts, seconds = (g0, g1), (a0, a1), (b0, b1)
    depth = one.shape[0]
    count, width = scaled.shape
    tiles = depth // TILE

    def tile_copy(i):
        return pltpu.make_async_copy(far.at[span(i), :], adjoint.at[span(i), :], tile_sems.at[i])

    gate_rows(blocks, count // 2, sems, weight, tokens, turned, gate, lambda i: tile_copy(i).start())
    for r in range(0, count, 64):
        at = slice(r, r + 64)
        x = gate[at, :]
        token_weight = weights[at, 0:1]
        cot_f = cot[at, :].astype(jnp.float32)
        sig = 1.0 / (1.0 + jnp.exp(-x))
        slope = sig * (1.0 + x * (1.0 - sig))
        curve = sig * (1.0 - sig) * (2.0 + x * (1.0 - 2.0 * sig))
        scaled[at, :] = (token_weight * cot_f * slope).astype(jnp.bfloat16)
        bend[at, :] = token_weight * cot_f * curve
        score[at, :] = cot_f * slope

    along[...] = jnp.zeros_like(along)
    across[...] = jnp.zeros_like(across)

    def grad_rows(i, slot, r):
        at = pl.ds(pl.multiple_of(i * TILE + r, HALF), HALF)
        grads[slot][r : r + HALF, :] = f32dot(turned[at, :], scaled[...])

    def probe(i, slot, target, terms):
        target[...] += f32dot(tokens[:, span(i)], terms[slot][...])

    def pieces(i, slot, first, last):
        for r in range(first, last, ROWS):
            at = pl.ds(pl.multiple_of(i * TILE + r, ROWS), ROWS)
            for c in range(0, width, COLUMNS):
                cols = slice(c, min(c + COLUMNS, width))
                yield r, cols, grads[slot][r : r + ROWS, cols], one[at, cols], two[at, cols], adjoint[at, cols]

    for i in range(2):
        tile_copy(i).wait()
    grad_rows(0, 0, 0)
    grad_rows(0, 0, HALF)
    sq, cross = {}, {}
    for r, cols, g, m1, m2, adj in pieces(0, 0, 0, SAMPLE):
        _, _, upd = update(g, m1, m2)
        sq[cols.start] = sq.get(cols.start, 0.0) + fold(upd * upd)
        cross[cols.start] = cross.get(cols.start, 0.0) + fold(adj * upd)
    sq = jnp.sum(sum(sq.values()), keepdims=True)
    cross = jnp.sum(sum(cross.values()), keepdims=True)
    clipped = sq * RATIO**2 > float(SAMPLE * width)
    guess = jnp.where(clipped, cross / jnp.maximum(sq, 1.0), 0.0)

    sums[...] = jnp.zeros_like(sums)

    def update_rows(i, slot, first):
        sq, cross = {}, {}
        for r, cols, g, m1, m2, adj in pieces(i, slot, first, first + HALF):
            over, inv, upd = update(g, m1, m2)
            sq[cols.start] = sq.get(cols.start, 0.0) + fold(upd * upd)
            cross[cols.start] = cross.get(cols.start, 0.0) + fold(adj * upd)
            pull = inv * (1.0 - g * (upd * over))
            firsts[slot][r : r + ROWS, cols] = ((adj - guess * upd) * pull).astype(jnp.bfloat16)
            seconds[slot][r : r + ROWS, cols] = (upd * pull).astype(jnp.bfloat16)
        sums[0] += sum(sq.values())
        sums[1] += sum(cross.values())

    def body(i, slot, ahead=True, behind=True):
        for r, target, terms in ((0, along, firsts), (HALF, across, seconds)):
            if ahead:
                grad_rows(i + 1, 1 - slot, r)
            update_rows(i, slot, r)
            if behind:
                probe(i - 1, 1 - slot, target, terms)

    body(0, 0, behind=False)

    def pair(k, _):
        tile_copy(2 * k + 2).wait()
        tile_copy(2 * k + 3).wait()
        body(2 * k + 1, 1)
        body(2 * k + 2, 0)
        return 0

    lax.fori_loop(0, tiles // 2 - 1, pair, 0)
    body(tiles - 1, 1, ahead=False)
    probe(tiles - 1, 1, along, firsts)
    probe(tiles - 1, 1, across, seconds)

    height = count // n
    places = owners(n)

    def spread(x):
        x = sum(x[:, i : i + 128] for i in range(0, width, 128))
        for k, place in enumerate(places):
            upright[pl.ds(pl.multiple_of(place * height, height), height), :] = x[k * height : (k + 1) * height, :]
        return jnp.sum(jnp.transpose(upright[...]), axis=0, keepdims=True)

    b = score[...] * across[...]
    a = score[...] * along[...] + guess * b
    whole = lambda x: jnp.broadcast_to(jnp.sum(x, keepdims=True), (1, count))
    stats[0:1, :] = RATIO * spread(a)
    stats[1:2, :] = RATIO**2 * spread(b)
    stats[2:3, :] = RATIO**2 * whole(sums[0])
    stats[3:4, :] = RATIO * whole(sums[1])
    stats[4:8, :] = jnp.broadcast_to(guess, (4, count))


def replay_call(n, blocks, adjoint, weight, cot, weights, one, two, tokens, turned, gate):
    half = len(blocks)
    depth = one.shape[0]
    count, width = cot.shape
    far = pl.BlockSpec(memory_space=pl.ANY)
    vmem = pl.BlockSpec(memory_space=pltpu.VMEM)
    like = lambda x: pltpu.VMEM(x.shape, x.dtype)
    block = lambda dtype: pltpu.VMEM((TILE, width), dtype)
    return pl.pallas_call(
        functools.partial(replay_kernel, n, half),
        in_specs=[far] * (half + 1) + [vmem] * 8,
        out_specs=[vmem] * 8,
        out_shape=[
            like(tokens),
            like(turned),
            like(gate),
            pltpu.VMEM((depth, width), jnp.float32),
            pltpu.VMEM((count, width), jnp.float32),
            pltpu.VMEM((count, width), jnp.float32),
            pltpu.VMEM((count, width), jnp.float32),
            pltpu.VMEM((8, count), jnp.float32),
        ],
        scratch_shapes=[
            pltpu.VMEM((count, width), jnp.bfloat16),
            pltpu.VMEM((count, width), jnp.float32),
            block(jnp.float32),
            block(jnp.float32),
            block(jnp.bfloat16),
            block(jnp.bfloat16),
            block(jnp.bfloat16),
            block(jnp.bfloat16),
            pltpu.VMEM((2, 8, min(COLUMNS, width)), jnp.float32),
            pltpu.VMEM((count, 128), jnp.float32),
            pltpu.SemaphoreType.DMA((half,)),
            pltpu.SemaphoreType.DMA((depth // TILE,)),
        ],
        input_output_aliases={half + 6: 0, half + 7: 1, half + 8: 2},
        compiler_params=pltpu.CompilerParams(vmem_limit_bytes=VMEM_BYTES),
        name="replay",
    )(*blocks, in_hbm(adjoint), weight, cot, weights, one, two, tokens, turned, gate)


def in_hbm(x):
    return pltpu.with_memory_space_constraint(x, pltpu.HBM)


def theta_kernel(n, entries, s0, s1, s2, s3, own, along, across, bend, turned, adjoint, theta, scores, ready, sent):
    total = s0[...] + s1[...] + (s2[...] + s3[...])
    sq, cross = total[2:3, 0:1], total[3:4, 0:1]
    rms = jnp.sqrt(sq / entries)
    scale = 1.0 / jnp.maximum(1.0, rms)
    bind = jnp.where(rms > 1.0, 1.0 / (rms * rms * rms), 0.0)
    lead = -0.01 * scale
    rest = 0.01 * cross * bind / entries
    mine = lead * total[0:8, :] + rest * pltpu.roll(total, 7, 0)
    count = total.shape[1]
    height = count // n
    mine = pltpu.roll(mine, lax.rem(count - lax.axis_index("dp") * height, count), 1)
    scores[...] = mine[0:1, 0:height]
    lead_here = RATIO * lead
    rest_here = RATIO**2 * rest + lead_here * own[4:5, 0:1]
    bent = (bend[...] * (lead_here * along[...] + rest_here * across[...])).astype(jnp.bfloat16)

    def copy(i):
        at = pl.ds(i * TILE, TILE)
        return pltpu.make_async_copy(ready.at[at, :], theta.at[at, :], sent.at[i])

    tiles = theta.shape[0] // TILE
    for i in range(tiles):
        at = pl.ds(i * TILE, TILE)
        ready[at, :] = 0.999 * adjoint[at, :] + f32dot(turned[at, :], bent)
        copy(i).start()
    for i in range(tiles):
        copy(i).wait()


def theta_call(n, entries, sums, own, along, across, bend, turned, adjoint):
    depth, width = adjoint.shape
    count = turned.shape[1]
    vmem = pl.BlockSpec(memory_space=pltpu.VMEM)
    return pl.pallas_call(
        functools.partial(theta_kernel, n, entries),
        in_specs=[vmem] * 10,
        out_specs=[pl.BlockSpec(memory_space=pl.ANY), vmem],
        out_shape=[
            jax.ShapeDtypeStruct((depth, width), jnp.float32),
            jax.ShapeDtypeStruct((1, count // n), jnp.float32),
        ],
        scratch_shapes=[pltpu.VMEM((depth, width), jnp.float32), pltpu.SemaphoreType.DMA((depth // TILE,))],
        compiler_params=pltpu.CompilerParams(vmem_limit_bytes=VMEM_BYTES),
        name="theta",
    )(*sums, own, along, across, bend, turned, adjoint)


def shards(n, tokens, cotangent, token_weight, weight, moment_one, moment_two, adjoint):
    entries = float(adjoint.shape[0] * adjoint.shape[1] * n)
    errands = [
        lambda after: fetch(n, weight, cotangent, token_weight.reshape(1, -1), after),
        lambda after: fetch_wide(moment_one, 9.0, after),
        lambda after: fetch_wide(moment_two, 19.0, after),
    ]
    blocks, ((weight_near, cot, weights), one, two) = gather(tokens, n, errands)
    half = len(blocks) // 2
    rows, turned, gate = early_call(blocks[:half], weight_near, cot.shape[0])
    _, turned, _, adjoint_near, along, across, bend, stats = replay_call(
        n, blocks[half:], adjoint, weight_near, cot, weights, one, two, rows, turned, gate
    )
    sums = all_sum(stats, n)
    theta_bar, scores = theta_call(n, entries, sums, stats, along, across, bend, turned, adjoint_near)
    return (theta_bar, scores.reshape(-1))


def solution(mesh):
    in_specs = (
        P(("group", "dp"), None),
        P("group", "dp"),
        P("group"),
        P(None, "dp"),
        P(None, "dp"),
        P(None, "dp"),
        P(None, "dp"),
    )
    out_specs = (P("group", "dp"), P(("group", "dp")))
    body = functools.partial(shards, mesh.shape["dp"])
    return jax.shard_map(body, mesh=mesh, in_specs=in_specs, out_specs=out_specs, check_vma=False)
```

```python
import functools
import itertools

import jax
import jax.numpy as jnp
from jax import lax
from jax.experimental import pallas as pl
from jax.experimental.pallas import tpu as pltpu
from jax.sharding import PartitionSpec as P

TILE = 512
QUARTER = 128
ROWS = 16
COLUMNS = 256
COST = 4 << 30
SAMPLE = 256
VMEM_BYTES = 12 << 20
RATIO = 0.1 / 0.05**0.5


def f32dot(a, b):
    return jnp.dot(a, b, preferred_element_type=jnp.float32)


def swapped(value, n, mask):
    return lax.ppermute(value, "dp", [(d ^ mask, d) for d in range(n)])


def ring(n):
    chips = n // 2
    return [*range(0, chips, 2), *range(chips - 1 - chips % 2, 0, -2)]


def onward(value, n):
    order = ring(n)
    pairs = []
    for i, chip in enumerate(order):
        pairs.append((2 * order[i - 1], 2 * chip))
        pairs.append((2 * order[(i + 1) % len(order)] + 1, 2 * chip + 1))
    return lax.ppermute(value, "dp", pairs)


def gather(tokens, n, errands):
    hops = n // 4
    done = []
    here = [tokens, swapped(tokens, n, 1)]
    parts = list(here)
    for hop in range(1, hops + 1):
        after = in_hbm(tokens) if hop == 1 else here[0]
        here = [onward(x, n) for x in here]
        if errands[len(done) :]:
            done.append(errands[len(done)](after))
        parts += here
        if hop < hops:
            parts += [swapped(x, n, 1) for x in here]
    return parts, done


def owners(n):
    chips = n // 2
    me = lax.axis_index("dp")
    chip, core = me >> 1, me & 1
    at = jnp.where(chip & 1 == 0, chip >> 1, chips - 1 - (chip >> 1))
    way = 2 * core - 1
    blocks = [(0, core)]
    for hop in range(1, chips // 2 + 1):
        blocks.append((way * hop, core))
        if 2 * hop < chips:
            blocks.append((-way * hop, 1 - core))
    places = []
    for step, first in blocks:
        there = at + step
        there = jnp.where(there < 0, there + chips, jnp.where(there >= chips, there - chips, there))
        source = jnp.where(there < chips // 2, 2 * there, 2 * (chips - 1 - there) + 1)
        places += [2 * source + first, 2 * source + 1 - first]
    return places


def all_sum(value, n):
    total = value
    for mask in range(4, n, 4):
        total = total + swapped(value, n, mask)
    return [total] + [swapped(total, n, mask) for mask in (1, 2, 3)]


def over_columns(row):
    return jnp.transpose(jnp.broadcast_to(row, (8, row.shape[1])))[:, :1]


def fold(x):
    return jnp.sum(x.reshape(x.shape[0] // 8, 8, x.shape[1]), axis=0)


def update(grad, one, two):
    first = one + grad
    second = two + grad * grad
    over = lax.rsqrt(second)
    inv = pltpu.reciprocal(second * over + 1e-08 / 0.05**0.5, approx=True)
    return over, inv, first * inv


def fetch_params():
    return {
        "compiler_params": pltpu.CompilerParams(vmem_limit_bytes=6 << 20),
        "cost_estimate": pl.CostEstimate(flops=COST, bytes_accessed=8 << 20, transcendentals=0),
    }


def widen_kernel(factor, far, after, near, raw, sems):
    tiles = far.shape[0] // TILE

    def copy(i):
        return pltpu.make_async_copy(far.at[span(i), :], raw.at[span(i), :], sems.at[i])

    for i in range(tiles):
        copy(i).start()

    def step(i, _):
        copy(i).wait()
        near[span(i), :] = factor * raw[span(i), :].astype(jnp.float32)
        return 0

    lax.fori_loop(0, tiles, step, 0)


def fetch_wide(x, factor, after):
    return pl.pallas_call(
        functools.partial(widen_kernel, factor),
        in_specs=[pl.BlockSpec(memory_space=pl.ANY)] * 2,
        out_specs=pl.BlockSpec(memory_space=pltpu.VMEM),
        out_shape=pltpu.VMEM(x.shape, jnp.float32),
        scratch_shapes=[pltpu.VMEM(x.shape, x.dtype), pltpu.SemaphoreType.DMA((x.shape[0] // TILE,))],
        name="widen",
        **fetch_params(),
    )(in_hbm(x), after)


def fetch_kernel(n, far, far_cot, far_weight, after, near, cot, weights, token_weight, upright, sems, cot_sems):
    height = cot.shape[0] // n
    copy = pltpu.make_async_copy(far, near, sems.at[0])
    weight_copy = pltpu.make_async_copy(far_weight, token_weight, sems.at[1])
    weight_copy.start()
    copy.start()
    places = [pl.multiple_of(place * height, height) for place in owners(n)]
    cot_copies = [
        pltpu.make_async_copy(
            far_cot.at[pl.ds(place, height), :], cot.at[pl.ds(k * height, height), :], cot_sems.at[k]
        )
        for k, place in enumerate(places)
    ]
    for cot_copy in cot_copies:
        cot_copy.start()
    weight_copy.wait()
    upright[...] = jnp.broadcast_to(over_columns(token_weight[...]), upright.shape)
    for k, place in enumerate(places):
        weights[k * height : (k + 1) * height, :] = upright[pl.ds(place, height), :]
    for cot_copy in cot_copies:
        cot_copy.wait()
    copy.wait()


def fetch(n, weight, cot, token_weight, after):
    count = cot.shape[0]
    vmem = pl.BlockSpec(memory_space=pltpu.VMEM)
    return pl.pallas_call(
        functools.partial(fetch_kernel, n),
        in_specs=[pl.BlockSpec(memory_space=pl.ANY)] * 4,
        out_specs=[vmem] * 3,
        out_shape=[
            pltpu.VMEM(weight.shape, weight.dtype),
            pltpu.VMEM(cot.shape, cot.dtype),
            pltpu.VMEM((count, 128), jnp.float32),
        ],
        scratch_shapes=[
            pltpu.VMEM((1, count), jnp.float32),
            pltpu.VMEM((count, 128), jnp.float32),
            pltpu.SemaphoreType.DMA((2,)),
            pltpu.SemaphoreType.DMA((n,)),
        ],
        name="fetch",
        **fetch_params(),
    )(in_hbm(weight), in_hbm(cot), in_hbm(token_weight), after)


def span(i):
    return pl.ds(pl.multiple_of(i * TILE, TILE), TILE)


def gate_rows(blocks, first, sems, weight, tokens, turned, gate, beside):
    height, depth = blocks[0].shape
    count = len(blocks) * height
    rows = slice(first, first + count)
    copies = [
        pltpu.make_async_copy(ref, tokens.at[pl.ds(first + k * height, height), :], sems.at[k])
        for k, ref in enumerate(blocks)
    ]
    for copy in copies:
        copy.start()
    gate[rows, :] = jnp.zeros((count, gate.shape[1]), jnp.float32)
    for copy in copies:
        copy.wait()

    def step(i, _):
        beside(i)
        here = tokens[rows, span(i)]
        gate[rows, :] += f32dot(here, weight[span(i), :])
        turned[span(i), rows] = here.T
        return 0

    lax.fori_loop(0, depth // TILE, step, 0)


def early_kernel(half, *refs):
    blocks, weight, (tokens, turned, gate, sems) = refs[:half], refs[half], refs[half + 1 :]
    gate_rows(blocks, 0, sems, weight, tokens, turned, gate, lambda i: None)


def early_call(blocks, weight, count):
    half = len(blocks)
    depth, width = weight.shape
    vmem = pl.BlockSpec(memory_space=pltpu.VMEM)
    return pl.pallas_call(
        functools.partial(early_kernel, half),
        in_specs=[pl.BlockSpec(memory_space=pl.ANY)] * half + [vmem],
        out_specs=[vmem] * 3,
        out_shape=[
            pltpu.VMEM((count, depth), jnp.bfloat16),
            pltpu.VMEM((depth, count), jnp.bfloat16),
            pltpu.VMEM((count, width), jnp.float32),
        ],
        scratch_shapes=[pltpu.SemaphoreType.DMA((half,))],
        compiler_params=pltpu.CompilerParams(vmem_limit_bytes=4 << 20),
        cost_estimate=pl.CostEstimate(flops=COST, bytes_accessed=12 << 20, transcendentals=0),
        name="early",
    )(*blocks, weight)


def replay_kernel(n, half, *refs):
    blocks, (far, weight, cot, weights, one, two) = refs[:half], refs[half : half + 6]
    (tokens, turned, gate, adjoint, along, across, bend, stats) = refs[half + 9 : half + 17]
    (scaled, score, g0, g1, a0, a1, b0, b1, sums, upright, sems, tile_sems) = refs[half + 17 :]
    grads, firsts, seconds = (g0, g1), (a0, a1), (b0, b1)
    depth = one.shape[0]
    count, width = scaled.shape
    tiles = depth // TILE

    def tile_copy(i):
        return pltpu.make_async_copy(far.at[span(i), :], adjoint.at[span(i), :], tile_sems.at[i])

    gate_rows(blocks, count // 2, sems, weight, tokens, turned, gate, lambda i: tile_copy(i).start())
    for r in range(0, count, 64):
        at = slice(r, r + 64)
        x = gate[at, :]
        token_weight = weights[at, 0:1]
        cot_f = cot[at, :].astype(jnp.float32)
        sig = 1.0 / (1.0 + jnp.exp(-x))
        slope = sig * (1.0 + x * (1.0 - sig))
        curve = sig * (1.0 - sig) * (2.0 + x * (1.0 - 2.0 * sig))
        scaled[at, :] = (token_weight * cot_f * slope).astype(jnp.bfloat16)
        bend[at, :] = token_weight * cot_f * curve
        score[at, :] = cot_f * slope

    along[...] = jnp.zeros_like(along)
    across[...] = jnp.zeros_like(across)

    def grad_rows(i, slot, r):
        at = pl.ds(pl.multiple_of(i * TILE + r, QUARTER), QUARTER)
        product = f32dot(turned[at, :], scaled[...])

        def store():
            grads[slot][r : r + QUARTER, :] = product

        return store

    def probe(i, slot, target, terms, cols):
        product = f32dot(tokens[:, span(i)], terms[slot][:, cols])

        def store():
            target[:, cols] += product

        return store

    def units(i, slot, ahead, behind):
        grad_units = [functools.partial(grad_rows, i + 1, 1 - slot, r) for r in range(0, TILE, QUARTER)]
        probe_units = [
            functools.partial(probe, i - 1, 1 - slot, target, terms, slice(c, min(c + COLUMNS, width)))
            for target, terms in ((along, firsts), (across, seconds))
            for c in range(0, width, COLUMNS)
        ]
        both = [unit for two in itertools.zip_longest(grad_units, probe_units) for unit in zip(two, (ahead, behind))]
        return [unit for unit, wanted in both if unit and wanted]

    def pieces(i, slot, first, last):
        for r in range(first, last, ROWS):
            at = pl.ds(pl.multiple_of(i * TILE + r, ROWS), ROWS)
            for c in range(0, width, COLUMNS):
                cols = slice(c, min(c + COLUMNS, width))
                yield r, cols, grads[slot][r : r + ROWS, cols], one[at, cols], two[at, cols], adjoint[at, cols]

    for i in range(2):
        tile_copy(i).wait()
    for r in range(0, TILE, QUARTER):
        grad_rows(0, 0, r)()
    sq, cross = {}, {}
    for r, cols, g, m1, m2, adj in pieces(0, 0, 0, SAMPLE):
        _, _, upd = update(g, m1, m2)
        sq[cols.start] = sq.get(cols.start, 0.0) + fold(upd * upd)
        cross[cols.start] = cross.get(cols.start, 0.0) + fold(adj * upd)
    sq = jnp.sum(sum(sq.values()), keepdims=True)
    cross = jnp.sum(sum(cross.values()), keepdims=True)
    clipped = sq * RATIO**2 > float(SAMPLE * width)
    guess = jnp.where(clipped, cross / jnp.maximum(sq, 1.0), 0.0)

    sums[...] = jnp.zeros_like(sums)

    def update_rows(i, slot, first, last):
        sq, cross = {}, {}
        for r, cols, g, m1, m2, adj in pieces(i, slot, first, last):
            over, inv, upd = update(g, m1, m2)
            sq[cols.start] = sq.get(cols.start, 0.0) + fold(upd * upd)
            cross[cols.start] = cross.get(cols.start, 0.0) + fold(adj * upd)
            pull = inv * (1.0 - g * (upd * over))
            firsts[slot][r : r + ROWS, cols] = ((adj - guess * upd) * pull).astype(jnp.bfloat16)
            seconds[slot][r : r + ROWS, cols] = (upd * pull).astype(jnp.bfloat16)
        sums[0] += sum(sq.values())
        sums[1] += sum(cross.values())

    def body(i, slot, ahead=True, behind=True):
        work = units(i, slot, ahead, behind)
        bounds = [TILE // ROWS * k // len(work) * ROWS for k in range(len(work) + 1)]
        for unit, first, last in zip(work, bounds, bounds[1:]):
            store = unit()
            update_rows(i, slot, first, last)
            store()

    body(0, 0, behind=False)

    def pair(k, _):
        tile_copy(2 * k + 2).wait()
        tile_copy(2 * k + 3).wait()
        body(2 * k + 1, 1)
        body(2 * k + 2, 0)
        return 0

    lax.fori_loop(0, tiles // 2 - 1, pair, 0)
    body(tiles - 1, 1, ahead=False)
    for unit in units(tiles, 0, False, True):
        unit()()

    height = count // n
    places = owners(n)

    def spread(x):
        x = sum(x[:, i : i + 128] for i in range(0, width, 128))
        for k, place in enumerate(places):
            upright[pl.ds(pl.multiple_of(place * height, height), height), :] = x[k * height : (k + 1) * height, :]
        return jnp.sum(jnp.transpose(upright[...]), axis=0, keepdims=True)

    b = score[...] * across[...]
    a = score[...] * along[...] + guess * b
    whole = lambda x: jnp.broadcast_to(jnp.sum(x, keepdims=True), (1, count))
    stats[0:1, :] = RATIO * spread(a)
    stats[1:2, :] = RATIO**2 * spread(b)
    stats[2:3, :] = RATIO**2 * whole(sums[0])
    stats[3:4, :] = RATIO * whole(sums[1])
    stats[4:8, :] = jnp.broadcast_to(guess, (4, count))


def replay_call(n, blocks, adjoint, weight, cot, weights, one, two, tokens, turned, gate):
    half = len(blocks)
    depth = one.shape[0]
    count, width = cot.shape
    far = pl.BlockSpec(memory_space=pl.ANY)
    vmem = pl.BlockSpec(memory_space=pltpu.VMEM)
    like = lambda x: pltpu.VMEM(x.shape, x.dtype)
    block = lambda dtype: pltpu.VMEM((TILE, width), dtype)
    return pl.pallas_call(
        functools.partial(replay_kernel, n, half),
        in_specs=[far] * (half + 1) + [vmem] * 8,
        out_specs=[vmem] * 8,
        out_shape=[
            like(tokens),
            like(turned),
            like(gate),
            pltpu.VMEM((depth, width), jnp.float32),
            pltpu.VMEM((count, width), jnp.float32),
            pltpu.VMEM((count, width), jnp.float32),
            pltpu.VMEM((count, width), jnp.float32),
            pltpu.VMEM((8, count), jnp.float32),
        ],
        scratch_shapes=[
            pltpu.VMEM((count, width), jnp.bfloat16),
            pltpu.VMEM((count, width), jnp.float32),
            block(jnp.float32),
            block(jnp.float32),
            block(jnp.bfloat16),
            block(jnp.bfloat16),
            block(jnp.bfloat16),
            block(jnp.bfloat16),
            pltpu.VMEM((2, 8, min(COLUMNS, width)), jnp.float32),
            pltpu.VMEM((count, 128), jnp.float32),
            pltpu.SemaphoreType.DMA((half,)),
            pltpu.SemaphoreType.DMA((depth // TILE,)),
        ],
        input_output_aliases={half + 6: 0, half + 7: 1, half + 8: 2},
        compiler_params=pltpu.CompilerParams(vmem_limit_bytes=VMEM_BYTES),
        name="replay",
    )(*blocks, in_hbm(adjoint), weight, cot, weights, one, two, tokens, turned, gate)


def in_hbm(x):
    return pltpu.with_memory_space_constraint(x, pltpu.HBM)


def theta_kernel(n, entries, s0, s1, s2, s3, own, along, across, bend, turned, adjoint, theta, scores, ready, sent):
    total = s0[...] + s1[...] + (s2[...] + s3[...])
    sq, cross = total[2:3, 0:1], total[3:4, 0:1]
    rms = jnp.sqrt(sq / entries)
    scale = 1.0 / jnp.maximum(1.0, rms)
    bind = jnp.where(rms > 1.0, 1.0 / (rms * rms * rms), 0.0)
    lead = -0.01 * scale
    rest = 0.01 * cross * bind / entries
    mine = lead * total[0:8, :] + rest * pltpu.roll(total, 7, 0)
    count = total.shape[1]
    height = count // n
    mine = pltpu.roll(mine, lax.rem(count - lax.axis_index("dp") * height, count), 1)
    scores[...] = mine[0:1, 0:height]
    lead_here = RATIO * lead
    rest_here = RATIO**2 * rest + lead_here * own[4:5, 0:1]
    bent = (bend[...] * (lead_here * along[...] + rest_here * across[...])).astype(jnp.bfloat16)

    def copy(i):
        at = pl.ds(i * TILE, TILE)
        return pltpu.make_async_copy(ready.at[at, :], theta.at[at, :], sent.at[i])

    tiles = theta.shape[0] // TILE
    for i in range(tiles):
        at = pl.ds(i * TILE, TILE)
        ready[at, :] = 0.999 * adjoint[at, :] + f32dot(turned[at, :], bent)
        copy(i).start()
    for i in range(tiles):
        copy(i).wait()


def theta_call(n, entries, sums, own, along, across, bend, turned, adjoint):
    depth, width = adjoint.shape
    count = turned.shape[1]
    vmem = pl.BlockSpec(memory_space=pltpu.VMEM)
    return pl.pallas_call(
        functools.partial(theta_kernel, n, entries),
        in_specs=[vmem] * 10,
        out_specs=[pl.BlockSpec(memory_space=pl.ANY), vmem],
        out_shape=[
            jax.ShapeDtypeStruct((depth, width), jnp.float32),
            jax.ShapeDtypeStruct((1, count // n), jnp.float32),
        ],
        scratch_shapes=[pltpu.VMEM((depth, width), jnp.float32), pltpu.SemaphoreType.DMA((depth // TILE,))],
        compiler_params=pltpu.CompilerParams(vmem_limit_bytes=VMEM_BYTES),
        name="theta",
    )(*sums, own, along, across, bend, turned, adjoint)


def shards(n, tokens, cotangent, token_weight, weight, moment_one, moment_two, adjoint):
    entries = float(adjoint.shape[0] * adjoint.shape[1] * n)
    errands = [
        lambda after: fetch(n, weight, cotangent, token_weight.reshape(1, -1), after),
        lambda after: fetch_wide(moment_one, 9.0, after),
        lambda after: fetch_wide(moment_two, 19.0, after),
    ]
    blocks, ((weight_near, cot, weights), one, two) = gather(tokens, n, errands)
    half = len(blocks) // 2
    rows, turned, gate = early_call(blocks[:half], weight_near, cot.shape[0])
    _, turned, _, adjoint_near, along, across, bend, stats = replay_call(
        n, blocks[half:], adjoint, weight_near, cot, weights, one, two, rows, turned, gate
    )
    sums = all_sum(stats, n)
    theta_bar, scores = theta_call(n, entries, sums, stats, along, across, bend, turned, adjoint_near)
    return (theta_bar, scores.reshape(-1))


def solution(mesh):
    in_specs = (
        P(("group", "dp"), None),
        P("group", "dp"),
        P("group"),
        P(None, "dp"),
        P(None, "dp"),
        P(None, "dp"),
        P(None, "dp"),
    )
    out_specs = (P("group", "dp"), P(("group", "dp")))
    body = functools.partial(shards, mesh.shape["dp"])
    return jax.shard_map(body, mesh=mesh, in_specs=in_specs, out_specs=out_specs, check_vma=False)
```

```python
import functools

import jax
import jax.numpy as jnp
from jax import lax
from jax.experimental import pallas as pl
from jax.experimental.pallas import tpu as pltpu
from jax.sharding import PartitionSpec as P

TILE = 512
HALF = 256
ROWS = 16
COLUMNS = 256
COST = 4 << 30
SAMPLE = 256
VMEM_BYTES = 12 << 20
RATIO = 0.1 / 0.05**0.5


def f32dot(a, b):
    return jnp.dot(a, b, preferred_element_type=jnp.float32)


def swapped(value, n, mask):
    return lax.ppermute(value, "dp", [(d ^ mask, d) for d in range(n)])


def ring(n):
    chips = n // 2
    return [*range(0, chips, 2), *range(chips - 1 - chips % 2, 0, -2)]


def onward(value, n):
    order = ring(n)
    pairs = []
    for i, chip in enumerate(order):
        pairs.append((2 * order[i - 1], 2 * chip))
        pairs.append((2 * order[(i + 1) % len(order)] + 1, 2 * chip + 1))
    return lax.ppermute(value, "dp", pairs)


def gather(tokens, n, errands):
    hops = n // 4
    done = []
    here = [tokens, swapped(tokens, n, 1)]
    parts = list(here)
    for hop in range(1, hops + 1):
        after = in_hbm(tokens) if hop == 1 else here[0]
        here = [onward(x, n) for x in here]
        if errands[len(done) :]:
            done.append(errands[len(done)](after))
        parts += here
        if hop < hops:
            parts += [swapped(x, n, 1) for x in here]
    return parts, done


def owners(n):
    chips = n // 2
    me = lax.axis_index("dp")
    chip, core = me >> 1, me & 1
    at = jnp.where(chip & 1 == 0, chip >> 1, chips - 1 - (chip >> 1))
    way = 2 * core - 1
    blocks = [(0, core)]
    for hop in range(1, chips // 2 + 1):
        blocks.append((way * hop, core))
        if 2 * hop < chips:
            blocks.append((-way * hop, 1 - core))
    places = []
    for step, first in blocks:
        there = at + step
        there = jnp.where(there < 0, there + chips, jnp.where(there >= chips, there - chips, there))
        source = jnp.where(there < chips // 2, 2 * there, 2 * (chips - 1 - there) + 1)
        places += [2 * source + first, 2 * source + 1 - first]
    return places


def to_all(copies):
    return lax.all_to_all(copies, "dp", split_axis=0, concat_axis=0, tiled=True)


def over_columns(row):
    return jnp.transpose(jnp.broadcast_to(row, (8, row.shape[1])))[:, :1]


def fold(x):
    return jnp.sum(x.reshape(x.shape[0] // 8, 8, x.shape[1]), axis=0)


def update(grad, one, two):
    first = one + grad
    second = two + grad * grad
    over = lax.rsqrt(second)
    inv = pltpu.reciprocal(second * over + 1e-08 / 0.05**0.5, approx=True)
    return over, inv, first * inv


def fetch_params():
    return {
        "compiler_params": pltpu.CompilerParams(vmem_limit_bytes=6 << 20),
        "cost_estimate": pl.CostEstimate(flops=COST, bytes_accessed=8 << 20, transcendentals=0),
    }


def widen_kernel(factor, far, after, near, raw, sems):
    tiles = far.shape[0] // TILE

    def copy(i):
        return pltpu.make_async_copy(far.at[span(i), :], raw.at[span(i), :], sems.at[i])

    for i in range(tiles):
        copy(i).start()

    def step(i, _):
        copy(i).wait()
        near[span(i), :] = factor * raw[span(i), :].astype(jnp.float32)
        return 0

    lax.fori_loop(0, tiles, step, 0)


def fetch_wide(x, factor, after):
    return pl.pallas_call(
        functools.partial(widen_kernel, factor),
        in_specs=[pl.BlockSpec(memory_space=pl.ANY)] * 2,
        out_specs=pl.BlockSpec(memory_space=pltpu.VMEM),
        out_shape=pltpu.VMEM(x.shape, jnp.float32),
        scratch_shapes=[pltpu.VMEM(x.shape, x.dtype), pltpu.SemaphoreType.DMA((x.shape[0] // TILE,))],
        name="widen",
        **fetch_params(),
    )(in_hbm(x), after)


def fetch_kernel(n, far, far_cot, far_weight, after, near, cot, weights, token_weight, upright, sems, cot_sems):
    height = cot.shape[0] // n
    copy = pltpu.make_async_copy(far, near, sems.at[0])
    weight_copy = pltpu.make_async_copy(far_weight, token_weight, sems.at[1])
    weight_copy.start()
    copy.start()
    places = [pl.multiple_of(place * height, height) for place in owners(n)]
    cot_copies = [
        pltpu.make_async_copy(
            far_cot.at[pl.ds(place, height), :], cot.at[pl.ds(k * height, height), :], cot_sems.at[k]
        )
        for k, place in enumerate(places)
    ]
    for cot_copy in cot_copies:
        cot_copy.start()
    weight_copy.wait()
    upright[...] = jnp.broadcast_to(over_columns(token_weight[...]), upright.shape)
    for k, place in enumerate(places):
        weights[k * height : (k + 1) * height, :] = upright[pl.ds(place, height), :]
    for cot_copy in cot_copies:
        cot_copy.wait()
    copy.wait()


def fetch(n, weight, cot, token_weight, after):
    count = cot.shape[0]
    vmem = pl.BlockSpec(memory_space=pltpu.VMEM)
    return pl.pallas_call(
        functools.partial(fetch_kernel, n),
        in_specs=[pl.BlockSpec(memory_space=pl.ANY)] * 4,
        out_specs=[vmem] * 3,
        out_shape=[
            pltpu.VMEM(weight.shape, weight.dtype),
            pltpu.VMEM(cot.shape, cot.dtype),
            pltpu.VMEM((count, 128), jnp.float32),
        ],
        scratch_shapes=[
            pltpu.VMEM((1, count), jnp.float32),
            pltpu.VMEM((count, 128), jnp.float32),
            pltpu.SemaphoreType.DMA((2,)),
            pltpu.SemaphoreType.DMA((n,)),
        ],
        name="fetch",
        **fetch_params(),
    )(in_hbm(weight), in_hbm(cot), in_hbm(token_weight), after)


def span(i):
    return pl.ds(pl.multiple_of(i * TILE, TILE), TILE)


def gate_rows(blocks, first, sems, weight, tokens, turned, gate, beside):
    height, depth = blocks[0].shape
    count = len(blocks) * height
    rows = slice(first, first + count)
    copies = [
        pltpu.make_async_copy(ref, tokens.at[pl.ds(first + k * height, height), :], sems.at[k])
        for k, ref in enumerate(blocks)
    ]
    for copy in copies:
        copy.start()
    gate[rows, :] = jnp.zeros((count, gate.shape[1]), jnp.float32)
    for copy in copies:
        copy.wait()

    def step(i, _):
        beside(i)
        here = tokens[rows, span(i)]
        gate[rows, :] += f32dot(here, weight[span(i), :])
        turned[span(i), rows] = here.T
        return 0

    lax.fori_loop(0, depth // TILE, step, 0)


def early_kernel(half, *refs):
    blocks, weight, (tokens, turned, gate, sems) = refs[:half], refs[half], refs[half + 1 :]
    gate_rows(blocks, 0, sems, weight, tokens, turned, gate, lambda i: None)


def early_call(blocks, weight, count):
    half = len(blocks)
    depth, width = weight.shape
    vmem = pl.BlockSpec(memory_space=pltpu.VMEM)
    return pl.pallas_call(
        functools.partial(early_kernel, half),
        in_specs=[pl.BlockSpec(memory_space=pl.ANY)] * half + [vmem],
        out_specs=[vmem] * 3,
        out_shape=[
            pltpu.VMEM((count, depth), jnp.bfloat16),
            pltpu.VMEM((depth, count), jnp.bfloat16),
            pltpu.VMEM((count, width), jnp.float32),
        ],
        scratch_shapes=[pltpu.SemaphoreType.DMA((half,))],
        compiler_params=pltpu.CompilerParams(vmem_limit_bytes=4 << 20),
        cost_estimate=pl.CostEstimate(flops=COST, bytes_accessed=12 << 20, transcendentals=0),
        name="early",
    )(*blocks, weight)


def replay_kernel(n, half, *refs):
    blocks, (far, weight, cot, weights, one, two) = refs[:half], refs[half : half + 6]
    (tokens, turned, gate, adjoint, along, across, bend, stats, copies) = refs[half + 9 : half + 18]
    (scaled, score, g0, g1, a0, a1, b0, b1, sums, upright, sems, tile_sems) = refs[half + 18 :]
    grads, firsts, seconds = (g0, g1), (a0, a1), (b0, b1)
    depth = one.shape[0]
    count, width = scaled.shape
    tiles = depth // TILE

    def tile_copy(i):
        return pltpu.make_async_copy(far.at[span(i), :], adjoint.at[span(i), :], tile_sems.at[i])

    gate_rows(blocks, count // 2, sems, weight, tokens, turned, gate, lambda i: tile_copy(i).start())
    for r in range(0, count, 64):
        at = slice(r, r + 64)
        x = gate[at, :]
        token_weight = weights[at, 0:1]
        cot_f = cot[at, :].astype(jnp.float32)
        sig = 1.0 / (1.0 + jnp.exp(-x))
        slope = sig * (1.0 + x * (1.0 - sig))
        curve = sig * (1.0 - sig) * (2.0 + x * (1.0 - 2.0 * sig))
        scaled[at, :] = (token_weight * cot_f * slope).astype(jnp.bfloat16)
        bend[at, :] = token_weight * cot_f * curve
        score[at, :] = cot_f * slope

    along[...] = jnp.zeros_like(along)
    across[...] = jnp.zeros_like(across)

    def grad_rows(i, slot, r):
        at = pl.ds(pl.multiple_of(i * TILE + r, HALF), HALF)
        grads[slot][r : r + HALF, :] = f32dot(turned[at, :], scaled[...])

    def probe(i, slot, target, terms):
        target[...] += f32dot(tokens[:, span(i)], terms[slot][...])

    def pieces(i, slot, first, last):
        for r in range(first, last, ROWS):
            at = pl.ds(pl.multiple_of(i * TILE + r, ROWS), ROWS)
            for c in range(0, width, COLUMNS):
                cols = slice(c, min(c + COLUMNS, width))
                yield r, cols, grads[slot][r : r + ROWS, cols], one[at, cols], two[at, cols], adjoint[at, cols]

    for i in range(2):
        tile_copy(i).wait()
    grad_rows(0, 0, 0)
    grad_rows(0, 0, HALF)
    sq, cross = {}, {}
    for r, cols, g, m1, m2, adj in pieces(0, 0, 0, SAMPLE):
        _, _, upd = update(g, m1, m2)
        sq[cols.start] = sq.get(cols.start, 0.0) + fold(upd * upd)
        cross[cols.start] = cross.get(cols.start, 0.0) + fold(adj * upd)
    sq = jnp.sum(sum(sq.values()), keepdims=True)
    cross = jnp.sum(sum(cross.values()), keepdims=True)
    clipped = sq * RATIO**2 > float(SAMPLE * width)
    guess = jnp.where(clipped, cross / jnp.maximum(sq, 1.0), 0.0)

    sums[...] = jnp.zeros_like(sums)

    def update_rows(i, slot, first):
        sq, cross = {}, {}
        for r, cols, g, m1, m2, adj in pieces(i, slot, first, first + HALF):
            over, inv, upd = update(g, m1, m2)
            sq[cols.start] = sq.get(cols.start, 0.0) + fold(upd * upd)
            cross[cols.start] = cross.get(cols.start, 0.0) + fold(adj * upd)
            pull = inv * (1.0 - g * (upd * over))
            firsts[slot][r : r + ROWS, cols] = ((adj - guess * upd) * pull).astype(jnp.bfloat16)
            seconds[slot][r : r + ROWS, cols] = (upd * pull).astype(jnp.bfloat16)
        sums[0] += sum(sq.values())
        sums[1] += sum(cross.values())

    def body(i, slot, ahead=True, behind=True):
        for r, target, terms in ((0, along, firsts), (HALF, across, seconds)):
            if ahead:
                grad_rows(i + 1, 1 - slot, r)
            update_rows(i, slot, r)
            if behind:
                probe(i - 1, 1 - slot, target, terms)

    body(0, 0, behind=False)

    def pair(k, _):
        tile_copy(2 * k + 2).wait()
        tile_copy(2 * k + 3).wait()
        body(2 * k + 1, 1)
        body(2 * k + 2, 0)
        return 0

    lax.fori_loop(0, tiles // 2 - 1, pair, 0)
    body(tiles - 1, 1, ahead=False)
    probe(tiles - 1, 1, along, firsts)
    probe(tiles - 1, 1, across, seconds)

    height = count // n
    places = owners(n)

    def spread(x):
        x = sum(x[:, i : i + 128] for i in range(0, width, 128))
        for k, place in enumerate(places):
            upright[pl.ds(pl.multiple_of(place * height, height), height), :] = x[k * height : (k + 1) * height, :]
        return jnp.sum(jnp.transpose(upright[...]), axis=0, keepdims=True)

    b = score[...] * across[...]
    a = score[...] * along[...] + guess * b
    whole = lambda x: jnp.broadcast_to(jnp.sum(x, keepdims=True), (1, count))
    stats[0:1, :] = RATIO * spread(a)
    stats[1:2, :] = RATIO**2 * spread(b)
    stats[2:3, :] = RATIO**2 * whole(sums[0])
    stats[3:4, :] = RATIO * whole(sums[1])
    stats[4:8, :] = jnp.broadcast_to(guess, (4, count))
    for k in range(n):
        copies[8 * k : 8 * (k + 1), :] = stats[...]


def replay_call(n, blocks, adjoint, weight, cot, weights, one, two, tokens, turned, gate):
    half = len(blocks)
    depth = one.shape[0]
    count, width = cot.shape
    far = pl.BlockSpec(memory_space=pl.ANY)
    vmem = pl.BlockSpec(memory_space=pltpu.VMEM)
    like = lambda x: pltpu.VMEM(x.shape, x.dtype)
    block = lambda dtype: pltpu.VMEM((TILE, width), dtype)
    return pl.pallas_call(
        functools.partial(replay_kernel, n, half),
        in_specs=[far] * (half + 1) + [vmem] * 8,
        out_specs=[vmem] * 9,
        out_shape=[
            like(tokens),
            like(turned),
            like(gate),
            pltpu.VMEM((depth, width), jnp.float32),
            pltpu.VMEM((count, width), jnp.float32),
            pltpu.VMEM((count, width), jnp.float32),
            pltpu.VMEM((count, width), jnp.float32),
            pltpu.VMEM((8, count), jnp.float32),
            jax.ShapeDtypeStruct((8 * n, count), jnp.float32),
        ],
        scratch_shapes=[
            pltpu.VMEM((count, width), jnp.bfloat16),
            pltpu.VMEM((count, width), jnp.float32),
            block(jnp.float32),
            block(jnp.float32),
            block(jnp.bfloat16),
            block(jnp.bfloat16),
            block(jnp.bfloat16),
            block(jnp.bfloat16),
            pltpu.VMEM((2, 8, min(COLUMNS, width)), jnp.float32),
            pltpu.VMEM((count, 128), jnp.float32),
            pltpu.SemaphoreType.DMA((half,)),
            pltpu.SemaphoreType.DMA((depth // TILE,)),
        ],
        input_output_aliases={half + 6: 0, half + 7: 1, half + 8: 2},
        compiler_params=pltpu.CompilerParams(vmem_limit_bytes=VMEM_BYTES),
        name="replay",
    )(*blocks, in_hbm(adjoint), weight, cot, weights, one, two, tokens, turned, gate)


def in_hbm(x):
    return pltpu.with_memory_space_constraint(x, pltpu.HBM)


def theta_kernel(n, entries, everyone, own, along, across, bend, turned, adjoint, theta, scores, ready, sent):
    total = sum(everyone[8 * k : 8 * (k + 1), :] for k in range(n))
    sq, cross = total[2:3, 0:1], total[3:4, 0:1]
    rms = jnp.sqrt(sq / entries)
    scale = 1.0 / jnp.maximum(1.0, rms)
    bind = jnp.where(rms > 1.0, 1.0 / (rms * rms * rms), 0.0)
    lead = -0.01 * scale
    rest = 0.01 * cross * bind / entries
    mine = lead * total[0:8, :] + rest * pltpu.roll(total, 7, 0)
    count = total.shape[1]
    height = count // n
    mine = pltpu.roll(mine, lax.rem(count - lax.axis_index("dp") * height, count), 1)
    scores[...] = mine[0:1, 0:height]
    lead_here = RATIO * lead
    rest_here = RATIO**2 * rest + lead_here * own[4:5, 0:1]
    bent = (bend[...] * (lead_here * along[...] + rest_here * across[...])).astype(jnp.bfloat16)

    def copy(i):
        at = pl.ds(i * TILE, TILE)
        return pltpu.make_async_copy(ready.at[at, :], theta.at[at, :], sent.at[i])

    tiles = theta.shape[0] // TILE
    for i in range(tiles):
        at = pl.ds(i * TILE, TILE)
        ready[at, :] = 0.999 * adjoint[at, :] + f32dot(turned[at, :], bent)
        copy(i).start()
    for i in range(tiles):
        copy(i).wait()


def theta_call(n, entries, everyone, own, along, across, bend, turned, adjoint):
    depth, width = adjoint.shape
    count = turned.shape[1]
    vmem = pl.BlockSpec(memory_space=pltpu.VMEM)
    return pl.pallas_call(
        functools.partial(theta_kernel, n, entries),
        in_specs=[vmem] * 7,
        out_specs=[pl.BlockSpec(memory_space=pl.ANY), vmem],
        out_shape=[
            jax.ShapeDtypeStruct((depth, width), jnp.float32),
            jax.ShapeDtypeStruct((1, count // n), jnp.float32),
        ],
        scratch_shapes=[pltpu.VMEM((depth, width), jnp.float32), pltpu.SemaphoreType.DMA((depth // TILE,))],
        compiler_params=pltpu.CompilerParams(vmem_limit_bytes=VMEM_BYTES),
        name="theta",
    )(everyone, own, along, across, bend, turned, adjoint)


def shards(n, tokens, cotangent, token_weight, weight, moment_one, moment_two, adjoint):
    entries = float(adjoint.shape[0] * adjoint.shape[1] * n)
    errands = [
        lambda after: fetch(n, weight, cotangent, token_weight.reshape(1, -1), after),
        lambda after: fetch_wide(moment_one, 9.0, after),
        lambda after: fetch_wide(moment_two, 19.0, after),
    ]
    blocks, ((weight_near, cot, weights), one, two) = gather(tokens, n, errands)
    half = len(blocks) // 2
    rows, turned, gate = early_call(blocks[:half], weight_near, cot.shape[0])
    _, turned, _, adjoint_near, along, across, bend, stats, copies = replay_call(
        n, blocks[half:], adjoint, weight_near, cot, weights, one, two, rows, turned, gate
    )
    everyone = to_all(copies)
    theta_bar, scores = theta_call(n, entries, everyone, stats, along, across, bend, turned, adjoint_near)
    return (theta_bar, scores.reshape(-1))


def solution(mesh):
    in_specs = (
        P(("group", "dp"), None),
        P("group", "dp"),
        P("group"),
        P(None, "dp"),
        P(None, "dp"),
        P(None, "dp"),
        P(None, "dp"),
    )
    out_specs = (P("group", "dp"), P(("group", "dp")))
    body = functools.partial(shards, mesh.shape["dp"])
    return jax.shard_map(body, mesh=mesh, in_specs=in_specs, out_specs=out_specs, check_vma=False)
```

```python
import functools

import jax
import jax.numpy as jnp
from jax import lax
from jax.experimental import pallas as pl
from jax.experimental.pallas import tpu as pltpu
from jax.sharding import PartitionSpec as P

TILE = 512
HALF = 256
ROWS = 16
COLUMNS = 256
COST = 4 << 30
SAMPLE = 64
VMEM_BYTES = 12 << 20
RATIO = 0.1 / 0.05**0.5


def f32dot(a, b):
    return jnp.dot(a, b, preferred_element_type=jnp.float32)


def swapped(value, n, mask):
    return lax.ppermute(value, "dp", [(d ^ mask, d) for d in range(n)])


def ring(n):
    chips = n // 2
    return [*range(0, chips, 2), *range(chips - 1 - chips % 2, 0, -2)]


def onward(value, n):
    order = ring(n)
    pairs = []
    for i, chip in enumerate(order):
        pairs.append((2 * order[i - 1], 2 * chip))
        pairs.append((2 * order[(i + 1) % len(order)] + 1, 2 * chip + 1))
    return lax.ppermute(value, "dp", pairs)


def gather(tokens, n, errands):
    hops = n // 4
    done = []
    here = [tokens, swapped(tokens, n, 1)]
    parts = list(here)
    for hop in range(1, hops + 1):
        after = in_hbm(tokens) if hop == 1 else here[0]
        here = [onward(x, n) for x in here]
        if errands[len(done) :]:
            done.append(errands[len(done)](after))
        parts += here
        if hop < hops:
            parts += [swapped(x, n, 1) for x in here]
    return parts, done


def owners(n):
    chips = n // 2
    me = lax.axis_index("dp")
    chip, core = me >> 1, me & 1
    at = jnp.where(chip & 1 == 0, chip >> 1, chips - 1 - (chip >> 1))
    way = 2 * core - 1
    blocks = [(0, core)]
    for hop in range(1, chips // 2 + 1):
        blocks.append((way * hop, core))
        if 2 * hop < chips:
            blocks.append((-way * hop, 1 - core))
    places = []
    for step, first in blocks:
        there = at + step
        there = jnp.where(there < 0, there + chips, jnp.where(there >= chips, there - chips, there))
        source = jnp.where(there < chips // 2, 2 * there, 2 * (chips - 1 - there) + 1)
        places += [2 * source + first, 2 * source + 1 - first]
    return places


def to_all(rows):
    return lax.all_to_all(rows, "dp", split_axis=0, concat_axis=0, tiled=True)


def over_columns(row):
    return jnp.transpose(jnp.broadcast_to(row, (8, row.shape[1])))[:, :1]


def fold(x):
    return jnp.sum(x.reshape(x.shape[0] // 8, 8, x.shape[1]), axis=0)


def update(grad, one, two):
    first = one + grad
    second = two + grad * grad
    over = lax.rsqrt(second)
    inv = pltpu.reciprocal(second * over + 1e-08 / 0.05**0.5, approx=True)
    return over, inv, first * inv


def fetch_params():
    return {
        "compiler_params": pltpu.CompilerParams(vmem_limit_bytes=6 << 20),
        "cost_estimate": pl.CostEstimate(flops=COST, bytes_accessed=8 << 20, transcendentals=0),
    }


def widen_kernel(factor, far, after, near, raw, sems):
    tiles = far.shape[0] // TILE

    def copy(i):
        return pltpu.make_async_copy(far.at[span(i), :], raw.at[span(i), :], sems.at[i])

    for i in range(tiles):
        copy(i).start()

    def step(i, _):
        copy(i).wait()
        near[span(i), :] = factor * raw[span(i), :].astype(jnp.float32)
        return 0

    lax.fori_loop(0, tiles, step, 0)


def fetch_wide(x, factor, after):
    return pl.pallas_call(
        functools.partial(widen_kernel, factor),
        in_specs=[pl.BlockSpec(memory_space=pl.ANY)] * 2,
        out_specs=pl.BlockSpec(memory_space=pltpu.VMEM),
        out_shape=pltpu.VMEM(x.shape, jnp.float32),
        scratch_shapes=[pltpu.VMEM(x.shape, x.dtype), pltpu.SemaphoreType.DMA((x.shape[0] // TILE,))],
        name="widen",
        **fetch_params(),
    )(in_hbm(x), after)


def fetch_kernel(n, far, far_cot, far_weight, after, near, cot, weights, token_weight, upright, sems, cot_sems):
    height = cot.shape[0] // n
    copy = pltpu.make_async_copy(far, near, sems.at[0])
    weight_copy = pltpu.make_async_copy(far_weight, token_weight, sems.at[1])
    weight_copy.start()
    copy.start()
    places = [pl.multiple_of(place * height, height) for place in owners(n)]
    cot_copies = [
        pltpu.make_async_copy(
            far_cot.at[pl.ds(place, height), :], cot.at[pl.ds(k * height, height), :], cot_sems.at[k]
        )
        for k, place in enumerate(places)
    ]
    for cot_copy in cot_copies:
        cot_copy.start()
    weight_copy.wait()
    upright[...] = jnp.broadcast_to(over_columns(token_weight[...]), upright.shape)
    for k, place in enumerate(places):
        weights[k * height : (k + 1) * height, :] = upright[pl.ds(place, height), :]
    for cot_copy in cot_copies:
        cot_copy.wait()
    copy.wait()


def fetch(n, weight, cot, token_weight, after):
    count = cot.shape[0]
    vmem = pl.BlockSpec(memory_space=pltpu.VMEM)
    return pl.pallas_call(
        functools.partial(fetch_kernel, n),
        in_specs=[pl.BlockSpec(memory_space=pl.ANY)] * 4,
        out_specs=[vmem] * 3,
        out_shape=[
            pltpu.VMEM(weight.shape, weight.dtype),
            pltpu.VMEM(cot.shape, cot.dtype),
            pltpu.VMEM((count, 128), jnp.float32),
        ],
        scratch_shapes=[
            pltpu.VMEM((1, count), jnp.float32),
            pltpu.VMEM((count, 128), jnp.float32),
            pltpu.SemaphoreType.DMA((2,)),
            pltpu.SemaphoreType.DMA((n,)),
        ],
        name="fetch",
        **fetch_params(),
    )(in_hbm(weight), in_hbm(cot), in_hbm(token_weight), after)


def span(i):
    return pl.ds(pl.multiple_of(i * TILE, TILE), TILE)


def gate_rows(blocks, first, sems, weight, tokens, turned, gate, beside):
    height, depth = blocks[0].shape
    count = len(blocks) * height
    rows = slice(first, first + count)
    copies = [
        pltpu.make_async_copy(ref, tokens.at[pl.ds(first + k * height, height), :], sems.at[k])
        for k, ref in enumerate(blocks)
    ]
    for copy in copies:
        copy.start()
    gate[rows, :] = jnp.zeros((count, gate.shape[1]), jnp.float32)
    for copy in copies:
        copy.wait()

    def step(i, _):
        beside(i)
        here = tokens[rows, span(i)]
        gate[rows, :] += f32dot(here, weight[span(i), :])
        turned[span(i), rows] = here.T
        return 0

    lax.fori_loop(0, depth // TILE, step, 0)


def early_kernel(half, *refs):
    blocks, weight, (tokens, turned, gate, sems) = refs[:half], refs[half], refs[half + 1 :]
    gate_rows(blocks, 0, sems, weight, tokens, turned, gate, lambda i: None)


def early_call(blocks, weight, count):
    half = len(blocks)
    depth, width = weight.shape
    vmem = pl.BlockSpec(memory_space=pltpu.VMEM)
    return pl.pallas_call(
        functools.partial(early_kernel, half),
        in_specs=[pl.BlockSpec(memory_space=pl.ANY)] * half + [vmem],
        out_specs=[vmem] * 3,
        out_shape=[
            pltpu.VMEM((count, depth), jnp.bfloat16),
            pltpu.VMEM((depth, count), jnp.bfloat16),
            pltpu.VMEM((count, width), jnp.float32),
        ],
        scratch_shapes=[pltpu.SemaphoreType.DMA((half,))],
        compiler_params=pltpu.CompilerParams(vmem_limit_bytes=4 << 20),
        cost_estimate=pl.CostEstimate(flops=COST, bytes_accessed=12 << 20, transcendentals=0),
        name="early",
    )(*blocks, weight)


def replay_kernel(n, half, *refs):
    blocks, (far, weight, cot, weights, one, two) = refs[:half], refs[half : half + 6]
    (tokens, turned, gate, adjoint, along, across, bend, own, deal) = refs[half + 9 : half + 18]
    (scaled, score, g0, g1, a0, a1, b0, b1, sums, upright, sems, tile_sems) = refs[half + 18 :]
    grads, firsts, seconds = (g0, g1), (a0, a1), (b0, b1)
    depth = one.shape[0]
    count, width = scaled.shape
    tiles = depth // TILE

    def tile_copy(i):
        return pltpu.make_async_copy(far.at[span(i), :], adjoint.at[span(i), :], tile_sems.at[i])

    gate_rows(blocks, count // 2, sems, weight, tokens, turned, gate, lambda i: tile_copy(i).start())
    for r in range(0, count, 64):
        at = slice(r, r + 64)
        x = gate[at, :]
        token_weight = weights[at, 0:1]
        cot_f = cot[at, :].astype(jnp.float32)
        sig = 1.0 / (1.0 + jnp.exp(-x))
        slope = sig * (1.0 + x * (1.0 - sig))
        curve = sig * (1.0 - sig) * (2.0 + x * (1.0 - 2.0 * sig))
        scaled[at, :] = (token_weight * cot_f * slope).astype(jnp.bfloat16)
        bend[at, :] = token_weight * cot_f * curve
        score[at, :] = cot_f * slope

    along[...] = jnp.zeros_like(along)
    across[...] = jnp.zeros_like(across)

    def grad_rows(i, slot, r):
        at = pl.ds(pl.multiple_of(i * TILE + r, HALF), HALF)
        grads[slot][r : r + HALF, :] = f32dot(turned[at, :], scaled[...])

    def probe(i, slot, target, terms):
        target[...] += f32dot(tokens[:, span(i)], terms[slot][...])

    def pieces(i, slot, first, last):
        for r in range(first, last, ROWS):
            at = pl.ds(pl.multiple_of(i * TILE + r, ROWS), ROWS)
            for c in range(0, width, COLUMNS):
                cols = slice(c, min(c + COLUMNS, width))
                yield r, cols, grads[slot][r : r + ROWS, cols], one[at, cols], two[at, cols], adjoint[at, cols]

    for i in range(2):
        tile_copy(i).wait()
    grad_rows(0, 0, 0)
    grad_rows(0, 0, HALF)
    sq, cross = {}, {}
    for r, cols, g, m1, m2, adj in pieces(0, 0, 0, SAMPLE):
        _, _, upd = update(g, m1, m2)
        sq[cols.start] = sq.get(cols.start, 0.0) + fold(upd * upd)
        cross[cols.start] = cross.get(cols.start, 0.0) + fold(adj * upd)
    sq = jnp.sum(sum(sq.values()), keepdims=True)
    cross = jnp.sum(sum(cross.values()), keepdims=True)
    clipped = sq * RATIO**2 > float(SAMPLE * width)
    guess = jnp.where(clipped, cross / jnp.maximum(sq, 1.0), 0.0)

    sums[...] = jnp.zeros_like(sums)

    def update_rows(i, slot, first):
        sq, cross = {}, {}
        for r, cols, g, m1, m2, adj in pieces(i, slot, first, first + HALF):
            over, inv, upd = update(g, m1, m2)
            sq[cols.start] = sq.get(cols.start, 0.0) + fold(upd * upd)
            cross[cols.start] = cross.get(cols.start, 0.0) + fold(adj * upd)
            pull = inv * (1.0 - g * (upd * over))
            firsts[slot][r : r + ROWS, cols] = ((adj - guess * upd) * pull).astype(jnp.bfloat16)
            seconds[slot][r : r + ROWS, cols] = (upd * pull).astype(jnp.bfloat16)
        sums[0] += sum(sq.values())
        sums[1] += sum(cross.values())

    def body(i, slot, ahead=True, behind=True):
        for r, target, terms in ((0, along, firsts), (HALF, across, seconds)):
            if ahead:
                grad_rows(i + 1, 1 - slot, r)
            update_rows(i, slot, r)
            if behind:
                probe(i - 1, 1 - slot, target, terms)

    body(0, 0, behind=False)

    def pair(k, _):
        tile_copy(2 * k + 2).wait()
        tile_copy(2 * k + 3).wait()
        body(2 * k + 1, 1)
        body(2 * k + 2, 0)
        return 0

    lax.fori_loop(0, tiles // 2 - 1, pair, 0)
    body(tiles - 1, 1, ahead=False)
    probe(tiles - 1, 1, along, firsts)
    probe(tiles - 1, 1, across, seconds)

    height = count // n
    places = owners(n)

    def spread(x):
        x = sum(x[:, i : i + 128] for i in range(0, width, 128))
        for k, place in enumerate(places):
            upright[pl.ds(pl.multiple_of(place * height, height), height), :] = x[k * height : (k + 1) * height, :]
        return jnp.sum(jnp.transpose(upright[...]), axis=0, keepdims=True)

    b = score[...] * across[...]
    a = score[...] * along[...] + guess * b
    whole = lambda x: jnp.broadcast_to(jnp.sum(x, keepdims=True), (1, count))
    own[...] = jnp.broadcast_to(guess, own.shape)

    total = lambda x: jnp.broadcast_to(jnp.sum(x, keepdims=True), (n, 1))
    deal[...] = jnp.zeros_like(deal)
    for part, row in enumerate((RATIO * spread(a), RATIO**2 * spread(b))):
        for k in range(n):
            deal[k : k + 1, part * height : (part + 1) * height] = row[:, k * height : (k + 1) * height]
    deal[:, 2 * height : 2 * height + 1] = RATIO**2 * total(sums[0])
    deal[:, 2 * height + 1 : 2 * height + 2] = RATIO * total(sums[1])


def replay_call(n, blocks, adjoint, weight, cot, weights, one, two, tokens, turned, gate):
    half = len(blocks)
    depth = one.shape[0]
    count, width = cot.shape
    far = pl.BlockSpec(memory_space=pl.ANY)
    vmem = pl.BlockSpec(memory_space=pltpu.VMEM)
    like = lambda x: pltpu.VMEM(x.shape, x.dtype)
    block = lambda dtype: pltpu.VMEM((TILE, width), dtype)
    return pl.pallas_call(
        functools.partial(replay_kernel, n, half),
        in_specs=[far] * (half + 1) + [vmem] * 8,
        out_specs=[vmem] * 9,
        out_shape=[
            like(tokens),
            like(turned),
            like(gate),
            pltpu.VMEM((depth, width), jnp.float32),
            pltpu.VMEM((count, width), jnp.float32),
            pltpu.VMEM((count, width), jnp.float32),
            pltpu.VMEM((count, width), jnp.float32),
            pltpu.VMEM((8, 128), jnp.float32),
            jax.ShapeDtypeStruct((n, 128), jnp.float32),
        ],
        scratch_shapes=[
            pltpu.VMEM((count, width), jnp.bfloat16),
            pltpu.VMEM((count, width), jnp.float32),
            block(jnp.float32),
            block(jnp.float32),
            block(jnp.bfloat16),
            block(jnp.bfloat16),
            block(jnp.bfloat16),
            block(jnp.bfloat16),
            pltpu.VMEM((2, 8, min(COLUMNS, width)), jnp.float32),
            pltpu.VMEM((count, 128), jnp.float32),
            pltpu.SemaphoreType.DMA((half,)),
            pltpu.SemaphoreType.DMA((depth // TILE,)),
        ],
        input_output_aliases={half + 6: 0, half + 7: 1, half + 8: 2},
        compiler_params=pltpu.CompilerParams(vmem_limit_bytes=VMEM_BYTES),
        name="replay",
    )(*blocks, in_hbm(adjoint), weight, cot, weights, one, two, tokens, turned, gate)


def in_hbm(x):
    return pltpu.with_memory_space_constraint(x, pltpu.HBM)


def theta_kernel(entries, everyone, own, along, across, bend, turned, adjoint, theta, scores, ready, sent):
    height = scores.shape[1]
    total = jnp.sum(everyone[...], axis=0, keepdims=True)
    sq, cross = total[:, 2 * height : 2 * height + 1], total[:, 2 * height + 1 : 2 * height + 2]
    rms = jnp.sqrt(sq / entries)
    scale = 1.0 / jnp.maximum(1.0, rms)
    bind = jnp.where(rms > 1.0, 1.0 / (rms * rms * rms), 0.0)
    lead = -0.01 * scale
    rest = 0.01 * cross * bind / entries
    scores[...] = lead * total[:, 0:height] + rest * total[:, height : 2 * height]
    lead_here = RATIO * lead
    rest_here = RATIO**2 * rest + lead_here * own[0:1, 0:1]
    bent = (bend[...] * (lead_here * along[...] + rest_here * across[...])).astype(jnp.bfloat16)

    def copy(i):
        at = pl.ds(i * TILE, TILE)
        return pltpu.make_async_copy(ready.at[at, :], theta.at[at, :], sent.at[i])

    tiles = theta.shape[0] // TILE
    for i in range(tiles):
        at = pl.ds(i * TILE, TILE)
        ready[at, :] = 0.999 * adjoint[at, :] + f32dot(turned[at, :], bent)
        copy(i).start()
    for i in range(tiles):
        copy(i).wait()


def theta_call(n, entries, everyone, own, along, across, bend, turned, adjoint):
    depth, width = adjoint.shape
    count = turned.shape[1]
    vmem = pl.BlockSpec(memory_space=pltpu.VMEM)
    return pl.pallas_call(
        functools.partial(theta_kernel, entries),
        in_specs=[vmem] * 7,
        out_specs=[pl.BlockSpec(memory_space=pl.ANY), vmem],
        out_shape=[
            jax.ShapeDtypeStruct((depth, width), jnp.float32),
            jax.ShapeDtypeStruct((1, count // n), jnp.float32),
        ],
        scratch_shapes=[pltpu.VMEM((depth, width), jnp.float32), pltpu.SemaphoreType.DMA((depth // TILE,))],
        compiler_params=pltpu.CompilerParams(vmem_limit_bytes=VMEM_BYTES),
        name="theta",
    )(everyone, own, along, across, bend, turned, adjoint)


def shards(n, tokens, cotangent, token_weight, weight, moment_one, moment_two, adjoint):
    entries = float(adjoint.shape[0] * adjoint.shape[1] * n)
    errands = [
        lambda after: fetch(n, weight, cotangent, token_weight.reshape(1, -1), after),
        lambda after: fetch_wide(moment_one, 9.0, after),
        lambda after: fetch_wide(moment_two, 19.0, after),
    ]
    blocks, ((weight_near, cot, weights), one, two) = gather(tokens, n, errands)
    half = len(blocks) // 2
    rows, turned, gate = early_call(blocks[:half], weight_near, cot.shape[0])
    _, turned, _, adjoint_near, along, across, bend, own, deal = replay_call(
        n, blocks[half:], adjoint, weight_near, cot, weights, one, two, rows, turned, gate
    )
    everyone = to_all(deal)
    theta_bar, scores = theta_call(n, entries, everyone, own, along, across, bend, turned, adjoint_near)
    return (theta_bar, scores.reshape(-1))


def solution(mesh):
    in_specs = (
        P(("group", "dp"), None),
        P("group", "dp"),
        P("group"),
        P(None, "dp"),
        P(None, "dp"),
        P(None, "dp"),
        P(None, "dp"),
    )
    out_specs = (P("group", "dp"), P(("group", "dp")))
    body = functools.partial(shards, mesh.shape["dp"])
    return jax.shard_map(body, mesh=mesh, in_specs=in_specs, out_specs=out_specs, check_vma=False)
```

```python
import functools

import jax
import jax.numpy as jnp
from jax import lax
from jax.experimental import pallas as pl
from jax.experimental.pallas import tpu as pltpu
from jax.sharding import PartitionSpec as P

TILE = 512
HALF = 256
ROWS = 16
COLUMNS = 256
COST = 4 << 30
SAMPLE = 64
VMEM_BYTES = 12 << 20
RATIO = 0.1 / 0.05**0.5


def f32dot(a, b):
    return jnp.dot(a, b, preferred_element_type=jnp.float32)


def swapped(value, n, mask):
    return lax.ppermute(value, "dp", [(d ^ mask, d) for d in range(n)])


def ring(n):
    chips = n // 2
    return [*range(0, chips, 2), *range(chips - 1 - chips % 2, 0, -2)]


def onward(value, n):
    order = ring(n)
    pairs = []
    for i, chip in enumerate(order):
        pairs.append((2 * order[i - 1], 2 * chip))
        pairs.append((2 * order[(i + 1) % len(order)] + 1, 2 * chip + 1))
    return lax.ppermute(value, "dp", pairs)


def gather(tokens, n, errands):
    hops = n // 4
    here = [tokens, swapped(tokens, n, 1)]
    parts = list(here)
    for hop in range(1, hops + 1):
        after = in_hbm(tokens) if hop == 1 else here[0]
        here = [onward(x, n) for x in here]
        for errand in errands[hop - 1 : hop]:
            errand(after)
        parts += here
        if hop < hops:
            parts += [swapped(x, n, 1) for x in here]
    return parts


def owners(n):
    chips = n // 2
    me = lax.axis_index("dp")
    chip, core = me >> 1, me & 1
    at = jnp.where(chip & 1 == 0, chip >> 1, chips - 1 - (chip >> 1))
    way = 2 * core - 1
    blocks = [(0, core)]
    for hop in range(1, chips // 2 + 1):
        blocks.append((way * hop, core))
        if 2 * hop < chips:
            blocks.append((-way * hop, 1 - core))
    places = []
    for step, first in blocks:
        there = at + step
        there = jnp.where(there < 0, there + chips, jnp.where(there >= chips, there - chips, there))
        source = jnp.where(there < chips // 2, 2 * there, 2 * (chips - 1 - there) + 1)
        places += [2 * source + first, 2 * source + 1 - first]
    return places


def to_all(rows):
    return lax.all_to_all(rows, "dp", split_axis=0, concat_axis=0, tiled=True)


def over_columns(row):
    return jnp.transpose(jnp.broadcast_to(row, (8, row.shape[1])))[:, :1]


def fold(x):
    return jnp.sum(x.reshape(x.shape[0] // 8, 8, x.shape[1]), axis=0)


def update(grad, one, two):
    first = one + grad
    second = two + grad * grad
    over = lax.rsqrt(second)
    inv = pltpu.reciprocal(second * over + 1e-08 / 0.05**0.5, approx=True)
    return over, inv, first * inv


def quarter_copy(k, far, near, sem):
    rows = far.shape[0] // 4
    at = pl.ds(k * rows, rows)
    return pltpu.make_async_copy(far.at[at, :], near.at[at, :], sem)


def fetch_params():
    return {
        "compiler_params": pltpu.CompilerParams(vmem_limit_bytes=6 << 20),
        "cost_estimate": pl.CostEstimate(flops=COST, bytes_accessed=8 << 20, transcendentals=0),
    }


def widen_kernel(factor, k, far, far_adjoint, _, after, near, adjoint, raw, sems, adjoint_sem):
    tiles = far.shape[0] // TILE

    def copy(i):
        return pltpu.make_async_copy(far.at[span(i), :], raw.at[span(i), :], sems.at[i])

    for i in range(tiles):
        copy(i).start()
    adjoint_copy = quarter_copy(k, far_adjoint, adjoint, adjoint_sem.at[0])
    adjoint_copy.start()

    def step(i, _):
        copy(i).wait()
        near[span(i), :] = factor * raw[span(i), :].astype(jnp.float32)
        return 0

    lax.fori_loop(0, tiles, step, 0)
    adjoint_copy.wait()


def fetch_wide(x, factor, k, far_adjoint, adjoint, after):
    far, vmem = pl.BlockSpec(memory_space=pl.ANY), pl.BlockSpec(memory_space=pltpu.VMEM)
    return pl.pallas_call(
        functools.partial(widen_kernel, factor, k),
        in_specs=[far, far, vmem, far],
        out_specs=[vmem] * 2,
        out_shape=[pltpu.VMEM(x.shape, jnp.float32), pltpu.VMEM(adjoint.shape, adjoint.dtype)],
        scratch_shapes=[
            pltpu.VMEM(x.shape, x.dtype),
            pltpu.SemaphoreType.DMA((x.shape[0] // TILE,)),
            pltpu.SemaphoreType.DMA((1,)),
        ],
        input_output_aliases={2: 1},
        name="widen",
        **fetch_params(),
    )(in_hbm(x), in_hbm(far_adjoint), adjoint, after)


def fetch_kernel(n, *refs):
    (far, far_cot, far_weight, far_adjoint, after, near, cot, weights, adjoint) = refs[:9]
    (token_weight, upright, sems, cot_sems) = refs[9:]
    height = cot.shape[0] // n
    adjoint_copy = quarter_copy(0, far_adjoint, adjoint, sems.at[2])
    copy = pltpu.make_async_copy(far, near, sems.at[0])
    weight_copy = pltpu.make_async_copy(far_weight, token_weight, sems.at[1])
    weight_copy.start()
    copy.start()
    places = [pl.multiple_of(place * height, height) for place in owners(n)]
    cot_copies = [
        pltpu.make_async_copy(
            far_cot.at[pl.ds(place, height), :], cot.at[pl.ds(k * height, height), :], cot_sems.at[k]
        )
        for k, place in enumerate(places)
    ]
    for cot_copy in cot_copies:
        cot_copy.start()
    adjoint_copy.start()
    weight_copy.wait()
    upright[...] = jnp.broadcast_to(over_columns(token_weight[...]), upright.shape)
    for k, place in enumerate(places):
        weights[k * height : (k + 1) * height, :] = upright[pl.ds(place, height), :]
    for cot_copy in cot_copies:
        cot_copy.wait()
    copy.wait()
    adjoint_copy.wait()


def fetch(n, weight, cot, token_weight, adjoint, after):
    count = cot.shape[0]
    vmem = pl.BlockSpec(memory_space=pltpu.VMEM)
    return pl.pallas_call(
        functools.partial(fetch_kernel, n),
        in_specs=[pl.BlockSpec(memory_space=pl.ANY)] * 5,
        out_specs=[vmem] * 4,
        out_shape=[
            pltpu.VMEM(weight.shape, weight.dtype),
            pltpu.VMEM(cot.shape, cot.dtype),
            pltpu.VMEM((count, 128), jnp.float32),
            pltpu.VMEM(adjoint.shape, adjoint.dtype),
        ],
        scratch_shapes=[
            pltpu.VMEM((1, count), jnp.float32),
            pltpu.VMEM((count, 128), jnp.float32),
            pltpu.SemaphoreType.DMA((3,)),
            pltpu.SemaphoreType.DMA((n,)),
        ],
        name="fetch",
        **fetch_params(),
    )(in_hbm(weight), in_hbm(cot), in_hbm(token_weight), in_hbm(adjoint), after)


def span(i):
    return pl.ds(pl.multiple_of(i * TILE, TILE), TILE)


def gate_rows(blocks, first, sems, weight, tokens, turned, gate):
    height, depth = blocks[0].shape
    count = len(blocks) * height
    rows = slice(first, first + count)
    copies = [
        pltpu.make_async_copy(ref, tokens.at[pl.ds(first + k * height, height), :], sems.at[k])
        for k, ref in enumerate(blocks)
    ]
    for copy in copies:
        copy.start()
    gate[rows, :] = jnp.zeros((count, gate.shape[1]), jnp.float32)
    for copy in copies:
        copy.wait()

    def step(i, _):
        here = tokens[rows, span(i)]
        gate[rows, :] += f32dot(here, weight[span(i), :])
        turned[span(i), rows] = here.T
        return 0

    lax.fori_loop(0, depth // TILE, step, 0)


def early_kernel(half, *refs):
    blocks, (weight, far_adjoint) = refs[:half], refs[half : half + 2]
    (tokens, turned, gate, adjoint, sems, adjoint_sem) = refs[half + 3 :]
    adjoint_copy = quarter_copy(3, far_adjoint, adjoint, adjoint_sem.at[0])
    adjoint_copy.start()
    gate_rows(blocks, 0, sems, weight, tokens, turned, gate)
    adjoint_copy.wait()


def early_call(blocks, weight, count, far_adjoint, adjoint):
    half = len(blocks)
    depth, width = weight.shape
    far, vmem = pl.BlockSpec(memory_space=pl.ANY), pl.BlockSpec(memory_space=pltpu.VMEM)
    return pl.pallas_call(
        functools.partial(early_kernel, half),
        in_specs=[far] * half + [vmem, far, vmem],
        out_specs=[vmem] * 4,
        out_shape=[
            pltpu.VMEM((count, depth), jnp.bfloat16),
            pltpu.VMEM((depth, count), jnp.bfloat16),
            pltpu.VMEM((count, width), jnp.float32),
            pltpu.VMEM(adjoint.shape, adjoint.dtype),
        ],
        scratch_shapes=[pltpu.SemaphoreType.DMA((half,)), pltpu.SemaphoreType.DMA((1,))],
        input_output_aliases={half + 2: 3},
        compiler_params=pltpu.CompilerParams(vmem_limit_bytes=4 << 20),
        cost_estimate=pl.CostEstimate(flops=COST, bytes_accessed=12 << 20, transcendentals=0),
        name="early",
    )(*blocks, weight, in_hbm(far_adjoint), adjoint)


def replay_kernel(n, half, *refs):
    blocks, (adjoint, weight, cot, weights, one, two) = refs[:half], refs[half : half + 6]
    (tokens, turned, gate, along, across, bend, own, deal) = refs[half + 9 : half + 17]
    (scaled, score, g0, g1, a0, a1, b0, b1, sums, upright, sems) = refs[half + 17 :]
    grads, firsts, seconds = (g0, g1), (a0, a1), (b0, b1)
    depth = one.shape[0]
    count, width = scaled.shape
    tiles = depth // TILE

    gate_rows(blocks, count // 2, sems, weight, tokens, turned, gate)
    for r in range(0, count, 64):
        at = slice(r, r + 64)
        x = gate[at, :]
        token_weight = weights[at, 0:1]
        cot_f = cot[at, :].astype(jnp.float32)
        sig = 1.0 / (1.0 + jnp.exp(-x))
        slope = sig * (1.0 + x * (1.0 - sig))
        curve = sig * (1.0 - sig) * (2.0 + x * (1.0 - 2.0 * sig))
        scaled[at, :] = (token_weight * cot_f * slope).astype(jnp.bfloat16)
        bend[at, :] = token_weight * cot_f * curve
        score[at, :] = cot_f * slope

    along[...] = jnp.zeros_like(along)
    across[...] = jnp.zeros_like(across)

    def grad_rows(i, slot, r):
        at = pl.ds(pl.multiple_of(i * TILE + r, HALF), HALF)
        grads[slot][r : r + HALF, :] = f32dot(turned[at, :], scaled[...])

    def probe(i, slot, target, terms):
        target[...] += f32dot(tokens[:, span(i)], terms[slot][...])

    def pieces(i, slot, first, last):
        for r in range(first, last, ROWS):
            at = pl.ds(pl.multiple_of(i * TILE + r, ROWS), ROWS)
            for c in range(0, width, COLUMNS):
                cols = slice(c, min(c + COLUMNS, width))
                yield r, cols, grads[slot][r : r + ROWS, cols], one[at, cols], two[at, cols], adjoint[at, cols]

    grad_rows(0, 0, 0)
    grad_rows(0, 0, HALF)
    sq, cross = {}, {}
    for r, cols, g, m1, m2, adj in pieces(0, 0, 0, SAMPLE):
        _, _, upd = update(g, m1, m2)
        sq[cols.start] = sq.get(cols.start, 0.0) + fold(upd * upd)
        cross[cols.start] = cross.get(cols.start, 0.0) + fold(adj * upd)
    sq = jnp.sum(sum(sq.values()), keepdims=True)
    cross = jnp.sum(sum(cross.values()), keepdims=True)
    clipped = sq * RATIO**2 > float(SAMPLE * width)
    guess = jnp.where(clipped, cross / jnp.maximum(sq, 1.0), 0.0)

    sums[...] = jnp.zeros_like(sums)

    def update_rows(i, slot, first):
        sq, cross = {}, {}
        for r, cols, g, m1, m2, adj in pieces(i, slot, first, first + HALF):
            over, inv, upd = update(g, m1, m2)
            sq[cols.start] = sq.get(cols.start, 0.0) + fold(upd * upd)
            cross[cols.start] = cross.get(cols.start, 0.0) + fold(adj * upd)
            pull = inv * (1.0 - g * (upd * over))
            firsts[slot][r : r + ROWS, cols] = ((adj - guess * upd) * pull).astype(jnp.bfloat16)
            seconds[slot][r : r + ROWS, cols] = (upd * pull).astype(jnp.bfloat16)
        sums[0] += sum(sq.values())
        sums[1] += sum(cross.values())

    def body(i, slot, ahead=True, behind=True):
        for r, target, terms in ((0, along, firsts), (HALF, across, seconds)):
            if ahead:
                grad_rows(i + 1, 1 - slot, r)
            update_rows(i, slot, r)
            if behind:
                probe(i - 1, 1 - slot, target, terms)

    body(0, 0, behind=False)

    def pair(k, _):
        body(2 * k + 1, 1)
        body(2 * k + 2, 0)
        return 0

    lax.fori_loop(0, tiles // 2 - 1, pair, 0)
    body(tiles - 1, 1, ahead=False)
    probe(tiles - 1, 1, along, firsts)
    probe(tiles - 1, 1, across, seconds)

    height = count // n
    places = owners(n)

    def spread(x):
        x = sum(x[:, i : i + 128] for i in range(0, width, 128))
        for k, place in enumerate(places):
            upright[pl.ds(pl.multiple_of(place * height, height), height), :] = x[k * height : (k + 1) * height, :]
        return jnp.sum(jnp.transpose(upright[...]), axis=0, keepdims=True)

    b = score[...] * across[...]
    a = score[...] * along[...] + guess * b
    whole = lambda x: jnp.broadcast_to(jnp.sum(x, keepdims=True), (1, count))
    own[...] = jnp.broadcast_to(guess, own.shape)

    total = lambda x: jnp.broadcast_to(jnp.sum(x, keepdims=True), (n, 1))
    deal[...] = jnp.zeros_like(deal)
    for part, row in enumerate((RATIO * spread(a), RATIO**2 * spread(b))):
        for k in range(n):
            deal[k : k + 1, part * height : (part + 1) * height] = row[:, k * height : (k + 1) * height]
    deal[:, 2 * height : 2 * height + 1] = RATIO**2 * total(sums[0])
    deal[:, 2 * height + 1 : 2 * height + 2] = RATIO * total(sums[1])


def replay_call(n, blocks, adjoint, weight, cot, weights, one, two, tokens, turned, gate):
    half = len(blocks)
    depth = one.shape[0]
    count, width = cot.shape
    far = pl.BlockSpec(memory_space=pl.ANY)
    vmem = pl.BlockSpec(memory_space=pltpu.VMEM)
    like = lambda x: pltpu.VMEM(x.shape, x.dtype)
    block = lambda dtype: pltpu.VMEM((TILE, width), dtype)
    return pl.pallas_call(
        functools.partial(replay_kernel, n, half),
        in_specs=[far] * half + [vmem] * 9,
        out_specs=[vmem] * 8,
        out_shape=[
            like(tokens),
            like(turned),
            like(gate),
            pltpu.VMEM((count, width), jnp.float32),
            pltpu.VMEM((count, width), jnp.float32),
            pltpu.VMEM((count, width), jnp.float32),
            pltpu.VMEM((8, 128), jnp.float32),
            jax.ShapeDtypeStruct((n, 128), jnp.float32),
        ],
        scratch_shapes=[
            pltpu.VMEM((count, width), jnp.bfloat16),
            pltpu.VMEM((count, width), jnp.float32),
            block(jnp.float32),
            block(jnp.float32),
            block(jnp.bfloat16),
            block(jnp.bfloat16),
            block(jnp.bfloat16),
            block(jnp.bfloat16),
            pltpu.VMEM((2, 8, min(COLUMNS, width)), jnp.float32),
            pltpu.VMEM((count, 128), jnp.float32),
            pltpu.SemaphoreType.DMA((half,)),
        ],
        input_output_aliases={half + 6: 0, half + 7: 1, half + 8: 2},
        compiler_params=pltpu.CompilerParams(vmem_limit_bytes=VMEM_BYTES),
        name="replay",
    )(*blocks, adjoint, weight, cot, weights, one, two, tokens, turned, gate)


def in_hbm(x):
    return pltpu.with_memory_space_constraint(x, pltpu.HBM)


def theta_kernel(entries, everyone, own, along, across, bend, turned, adjoint, theta, scores, ready, sent):
    height = scores.shape[1]
    total = jnp.sum(everyone[...], axis=0, keepdims=True)
    sq, cross = total[:, 2 * height : 2 * height + 1], total[:, 2 * height + 1 : 2 * height + 2]
    rms = jnp.sqrt(sq / entries)
    scale = 1.0 / jnp.maximum(1.0, rms)
    bind = jnp.where(rms > 1.0, 1.0 / (rms * rms * rms), 0.0)
    lead = -0.01 * scale
    rest = 0.01 * cross * bind / entries
    scores[...] = lead * total[:, 0:height] + rest * total[:, height : 2 * height]
    lead_here = RATIO * lead
    rest_here = RATIO**2 * rest + lead_here * own[0:1, 0:1]
    bent = (bend[...] * (lead_here * along[...] + rest_here * across[...])).astype(jnp.bfloat16)

    def copy(i):
        at = pl.ds(i * TILE, TILE)
        return pltpu.make_async_copy(ready.at[at, :], theta.at[at, :], sent.at[i])

    tiles = theta.shape[0] // TILE
    for i in range(tiles):
        at = pl.ds(i * TILE, TILE)
        ready[at, :] = 0.999 * adjoint[at, :] + f32dot(turned[at, :], bent)
        copy(i).start()
    for i in range(tiles):
        copy(i).wait()


def theta_call(n, entries, everyone, own, along, across, bend, turned, adjoint):
    depth, width = adjoint.shape
    count = turned.shape[1]
    vmem = pl.BlockSpec(memory_space=pltpu.VMEM)
    return pl.pallas_call(
        functools.partial(theta_kernel, entries),
        in_specs=[vmem] * 7,
        out_specs=[pl.BlockSpec(memory_space=pl.ANY), vmem],
        out_shape=[
            jax.ShapeDtypeStruct((depth, width), jnp.float32),
            jax.ShapeDtypeStruct((1, count // n), jnp.float32),
        ],
        scratch_shapes=[pltpu.VMEM((depth, width), jnp.float32), pltpu.SemaphoreType.DMA((depth // TILE,))],
        compiler_params=pltpu.CompilerParams(vmem_limit_bytes=VMEM_BYTES),
        name="theta",
    )(everyone, own, along, across, bend, turned, adjoint)


def shards(n, tokens, cotangent, token_weight, weight, moment_one, moment_two, adjoint):
    entries = float(adjoint.shape[0] * adjoint.shape[1] * n)
    near = {}

    def first(after):
        near["weight"], near["cot"], near["weights"], near["adjoint"] = fetch(
            n, weight, cotangent, token_weight.reshape(1, -1), adjoint, after
        )

    def second(after):
        near["one"], near["adjoint"] = fetch_wide(moment_one, 9.0, 1, adjoint, near["adjoint"], after)

    def third(after):
        near["two"], near["adjoint"] = fetch_wide(moment_two, 19.0, 2, adjoint, near["adjoint"], after)

    blocks = gather(tokens, n, [first, second, third])
    half = len(blocks) // 2
    rows, turned, gate, adjoint_near = early_call(
        blocks[:half], near["weight"], cotangent.shape[0], adjoint, near["adjoint"]
    )
    _, turned, _, along, across, bend, own, deal = replay_call(
        n, blocks[half:], adjoint_near, near["weight"], near["cot"], near["weights"], near["one"], near["two"], rows, turned, gate
    )
    everyone = to_all(deal)
    theta_bar, scores = theta_call(n, entries, everyone, own, along, across, bend, turned, adjoint_near)
    return (theta_bar, scores.reshape(-1))


def solution(mesh):
    in_specs = (
        P(("group", "dp"), None),
        P("group", "dp"),
        P("group"),
        P(None, "dp"),
        P(None, "dp"),
        P(None, "dp"),
        P(None, "dp"),
    )
    out_specs = (P("group", "dp"), P(("group", "dp")))
    body = functools.partial(shards, mesh.shape["dp"])
    return jax.shard_map(body, mesh=mesh, in_specs=in_specs, out_specs=out_specs, check_vma=False)
```

```python
import functools

import jax
import jax.numpy as jnp
from jax import lax
from jax.experimental import pallas as pl
from jax.experimental.pallas import tpu as pltpu
from jax.sharding import PartitionSpec as P

TILE = 512
HALF = 256
ROWS = 16
COLUMNS = 256
COST = 4 << 30
SAMPLE = 64
VMEM_BYTES = 12 << 20
RATIO = 0.1 / 0.05**0.5


def f32dot(a, b):
    return jnp.dot(a, b, preferred_element_type=jnp.float32)


def swapped(value, n, mask):
    return lax.ppermute(value, "dp", [(d ^ mask, d) for d in range(n)])


def ring(n):
    chips = n // 2
    return [*range(0, chips, 2), *range(chips - 1 - chips % 2, 0, -2)]


def onward(value, n):
    order = ring(n)
    pairs = []
    for i, chip in enumerate(order):
        pairs.append((2 * order[i - 1], 2 * chip))
        pairs.append((2 * order[(i + 1) % len(order)] + 1, 2 * chip + 1))
    return lax.ppermute(value, "dp", pairs)


def gather(tokens, n, errands):
    hops = n // 4
    done = []
    here = [tokens, swapped(tokens, n, 1)]
    parts = list(here)
    for hop in range(1, hops + 1):
        after = in_hbm(tokens) if hop == 1 else here[0]
        here = [onward(x, n) for x in here]
        if errands[len(done) :]:
            done.append(errands[len(done)](after))
        parts += here
        if hop < hops:
            parts += [swapped(x, n, 1) for x in here]
    return parts, done


def owners(n):
    chips = n // 2
    me = lax.axis_index("dp")
    chip, core = me >> 1, me & 1
    at = jnp.where(chip & 1 == 0, chip >> 1, chips - 1 - (chip >> 1))
    way = 2 * core - 1
    blocks = [(0, core)]
    for hop in range(1, chips // 2 + 1):
        blocks.append((way * hop, core))
        if 2 * hop < chips:
            blocks.append((-way * hop, 1 - core))
    places = []
    for step, first in blocks:
        there = at + step
        there = jnp.where(there < 0, there + chips, jnp.where(there >= chips, there - chips, there))
        source = jnp.where(there < chips // 2, 2 * there, 2 * (chips - 1 - there) + 1)
        places += [2 * source + first, 2 * source + 1 - first]
    return places


def to_all(rows):
    return lax.all_to_all(rows, "dp", split_axis=0, concat_axis=0, tiled=True)


def over_columns(row):
    return jnp.transpose(jnp.broadcast_to(row, (8, row.shape[1])))[:, :1]


def fold(x):
    return jnp.sum(x.reshape(x.shape[0] // 8, 8, x.shape[1]), axis=0)


def update(grad, one, two):
    first = one + grad
    second = two + grad * grad
    over = lax.rsqrt(second)
    inv = pltpu.reciprocal(second * over + 1e-08 / 0.05**0.5, approx=True)
    return over, inv, first * inv


def fetch_params():
    return {
        "compiler_params": pltpu.CompilerParams(vmem_limit_bytes=6 << 20),
        "cost_estimate": pl.CostEstimate(flops=COST, bytes_accessed=8 << 20, transcendentals=0),
    }


def widen_kernel(factor, far, after, near, raw, sems):
    tiles = far.shape[0] // TILE

    def copy(i):
        return pltpu.make_async_copy(far.at[span(i), :], raw.at[span(i), :], sems.at[i])

    for i in range(tiles):
        copy(i).start()

    def step(i, _):
        copy(i).wait()
        near[span(i), :] = factor * raw[span(i), :].astype(jnp.float32)
        return 0

    lax.fori_loop(0, tiles, step, 0)


def fetch_wide(x, factor, after):
    return pl.pallas_call(
        functools.partial(widen_kernel, factor),
        in_specs=[pl.BlockSpec(memory_space=pl.ANY)] * 2,
        out_specs=pl.BlockSpec(memory_space=pltpu.VMEM),
        out_shape=pltpu.VMEM(x.shape, jnp.float32),
        scratch_shapes=[pltpu.VMEM(x.shape, x.dtype), pltpu.SemaphoreType.DMA((x.shape[0] // TILE,))],
        name="widen",
        **fetch_params(),
    )(in_hbm(x), after)


def fetch_kernel(n, far, far_cot, far_weight, after, near, cot, weights, token_weight, upright, sems, cot_sems):
    height = cot.shape[0] // n
    copy = pltpu.make_async_copy(far, near, sems.at[0])
    weight_copy = pltpu.make_async_copy(far_weight, token_weight, sems.at[1])
    weight_copy.start()
    copy.start()
    places = [pl.multiple_of(place * height, height) for place in owners(n)]
    cot_copies = [
        pltpu.make_async_copy(
            far_cot.at[pl.ds(place, height), :], cot.at[pl.ds(k * height, height), :], cot_sems.at[k]
        )
        for k, place in enumerate(places)
    ]
    for cot_copy in cot_copies:
        cot_copy.start()
    weight_copy.wait()
    upright[...] = jnp.broadcast_to(over_columns(token_weight[...]), upright.shape)
    for k, place in enumerate(places):
        weights[k * height : (k + 1) * height, :] = upright[pl.ds(place, height), :]
    for cot_copy in cot_copies:
        cot_copy.wait()
    copy.wait()


def fetch(n, weight, cot, token_weight, after):
    count = cot.shape[0]
    vmem = pl.BlockSpec(memory_space=pltpu.VMEM)
    return pl.pallas_call(
        functools.partial(fetch_kernel, n),
        in_specs=[pl.BlockSpec(memory_space=pl.ANY)] * 4,
        out_specs=[vmem] * 3,
        out_shape=[
            pltpu.VMEM(weight.shape, weight.dtype),
            pltpu.VMEM(cot.shape, cot.dtype),
            pltpu.VMEM((count, 128), jnp.float32),
        ],
        scratch_shapes=[
            pltpu.VMEM((1, count), jnp.float32),
            pltpu.VMEM((count, 128), jnp.float32),
            pltpu.SemaphoreType.DMA((2,)),
            pltpu.SemaphoreType.DMA((n,)),
        ],
        name="fetch",
        **fetch_params(),
    )(in_hbm(weight), in_hbm(cot), in_hbm(token_weight), after)


def span(i):
    return pl.ds(pl.multiple_of(i * TILE, TILE), TILE)


def bring(blocks, first, sems, tokens):
    height = blocks[0].shape[0]
    copies = [
        pltpu.make_async_copy(ref, tokens.at[pl.ds(first + k * height, height), :], sems.at[k])
        for k, ref in enumerate(blocks)
    ]
    for copy in copies:
        copy.start()
    return copies


def gate_rows(rows, weight, tokens, turned, gate, beside):
    gate[rows, :] = jnp.zeros((rows.stop - rows.start, gate.shape[1]), jnp.float32)

    def step(i, _):
        beside(i)
        here = tokens[rows, span(i)]
        gate[rows, :] += f32dot(here, weight[span(i), :])
        turned[span(i), rows] = here.T
        return 0

    lax.fori_loop(0, weight.shape[0] // TILE, step, 0)


def slope_rows(rows, gate, cot, weights, scaled, bend, score):
    for r in range(rows.start, rows.stop, 64):
        at = slice(r, r + 64)
        x = gate[at, :]
        token_weight = weights[at, 0:1]
        cot_f = cot[at, :].astype(jnp.float32)
        sig = 1.0 / (1.0 + jnp.exp(-x))
        slope = sig * (1.0 + x * (1.0 - sig))
        curve = sig * (1.0 - sig) * (2.0 + x * (1.0 - 2.0 * sig))
        scaled[at, :] = (token_weight * cot_f * slope).astype(jnp.bfloat16)
        bend[at, :] = token_weight * cot_f * curve
        score[at, :] = cot_f * slope


def early_kernel(parts, *refs):
    blocks, (weight, cot, weights) = refs[:parts], refs[parts : parts + 3]
    (tokens, turned, gate, scaled, bend, score, sems) = refs[parts + 3 :]
    rows = slice(0, gate.shape[0] // 2)
    for copy in bring(blocks, 0, sems, tokens):
        copy.wait()
    gate_rows(rows, weight, tokens, turned, gate, lambda i: None)
    slope_rows(rows, gate, cot, weights, scaled, bend, score)


def early_call(blocks, weight, cot, weights):
    parts = len(blocks)
    depth, width = weight.shape
    count = cot.shape[0]
    vmem = pl.BlockSpec(memory_space=pltpu.VMEM)
    return pl.pallas_call(
        functools.partial(early_kernel, parts),
        in_specs=[pl.BlockSpec(memory_space=pl.ANY)] * parts + [vmem] * 3,
        out_specs=[vmem] * 6,
        out_shape=[
            pltpu.VMEM((count, depth), jnp.bfloat16),
            pltpu.VMEM((depth, count), jnp.bfloat16),
            pltpu.VMEM((count, width), jnp.float32),
            pltpu.VMEM((count, width), jnp.bfloat16),
            pltpu.VMEM((count, width), jnp.float32),
            pltpu.VMEM((count, width), jnp.float32),
        ],
        scratch_shapes=[pltpu.SemaphoreType.DMA((parts,))],
        compiler_params=pltpu.CompilerParams(vmem_limit_bytes=4 << 20),
        cost_estimate=pl.CostEstimate(flops=COST, bytes_accessed=12 << 20, transcendentals=0),
        name="early",
    )(*blocks, weight, cot, weights)


def replay_kernel(n, half, *refs):
    blocks, (far, weight, cot, weights, one, two) = refs[:half], refs[half : half + 6]
    (tokens, turned, gate, scaled, bend, score) = refs[half + 12 : half + 18]
    (adjoint, along, across, own, deal) = refs[half + 18 : half + 23]
    (g0, g1, a0, a1, b0, b1, sums, upright, sems, tile_sems) = refs[half + 23 :]
    grads, firsts, seconds = (g0, g1), (a0, a1), (b0, b1)
    depth = one.shape[0]
    count, width = scaled.shape
    tiles = depth // TILE

    def tile_copy(i):
        return pltpu.make_async_copy(far.at[span(i), :], adjoint.at[span(i), :], tile_sems.at[i])

    rows = slice(count // 2, count)
    for copy in bring(blocks, count - half * blocks[0].shape[0], sems, tokens):
        copy.wait()
    gate_rows(rows, weight, tokens, turned, gate, lambda i: tile_copy(i).start())
    slope_rows(rows, gate, cot, weights, scaled, bend, score)

    along[...] = jnp.zeros_like(along)
    across[...] = jnp.zeros_like(across)

    def grad_rows(i, slot, r):
        at = pl.ds(pl.multiple_of(i * TILE + r, HALF), HALF)
        grads[slot][r : r + HALF, :] = f32dot(turned[at, :], scaled[...])

    def probe(i, slot, target, terms):
        target[...] += f32dot(tokens[:, span(i)], terms[slot][...])

    def pieces(i, slot, first, last):
        for r in range(first, last, ROWS):
            at = pl.ds(pl.multiple_of(i * TILE + r, ROWS), ROWS)
            for c in range(0, width, COLUMNS):
                cols = slice(c, min(c + COLUMNS, width))
                yield r, cols, grads[slot][r : r + ROWS, cols], one[at, cols], two[at, cols], adjoint[at, cols]

    for i in range(2):
        tile_copy(i).wait()
    grad_rows(0, 0, 0)
    grad_rows(0, 0, HALF)
    sq, cross = {}, {}
    for r, cols, g, m1, m2, adj in pieces(0, 0, 0, SAMPLE):
        _, _, upd = update(g, m1, m2)
        sq[cols.start] = sq.get(cols.start, 0.0) + fold(upd * upd)
        cross[cols.start] = cross.get(cols.start, 0.0) + fold(adj * upd)
    sq = jnp.sum(sum(sq.values()), keepdims=True)
    cross = jnp.sum(sum(cross.values()), keepdims=True)
    clipped = sq * RATIO**2 > float(SAMPLE * width)
    guess = jnp.where(clipped, cross / jnp.maximum(sq, 1.0), 0.0)

    sums[...] = jnp.zeros_like(sums)

    def update_rows(i, slot, first):
        sq, cross = {}, {}
        for r, cols, g, m1, m2, adj in pieces(i, slot, first, first + HALF):
            over, inv, upd = update(g, m1, m2)
            sq[cols.start] = sq.get(cols.start, 0.0) + fold(upd * upd)
            cross[cols.start] = cross.get(cols.start, 0.0) + fold(adj * upd)
            pull = inv * (1.0 - g * (upd * over))
            firsts[slot][r : r + ROWS, cols] = ((adj - guess * upd) * pull).astype(jnp.bfloat16)
            seconds[slot][r : r + ROWS, cols] = (upd * pull).astype(jnp.bfloat16)
        sums[0] += sum(sq.values())
        sums[1] += sum(cross.values())

    def body(i, slot, ahead=True, behind=True):
        for r, target, terms in ((0, along, firsts), (HALF, across, seconds)):
            if ahead:
                grad_rows(i + 1, 1 - slot, r)
            update_rows(i, slot, r)
            if behind:
                probe(i - 1, 1 - slot, target, terms)

    body(0, 0, behind=False)

    def pair(k, _):
        tile_copy(2 * k + 2).wait()
        tile_copy(2 * k + 3).wait()
        body(2 * k + 1, 1)
        body(2 * k + 2, 0)
        return 0

    lax.fori_loop(0, tiles // 2 - 1, pair, 0)
    body(tiles - 1, 1, ahead=False)
    probe(tiles - 1, 1, along, firsts)
    probe(tiles - 1, 1, across, seconds)

    height = count // n
    places = owners(n)

    def spread(x):
        x = sum(x[:, i : i + 128] for i in range(0, width, 128))
        for k, place in enumerate(places):
            upright[pl.ds(pl.multiple_of(place * height, height), height), :] = x[k * height : (k + 1) * height, :]
        return jnp.sum(jnp.transpose(upright[...]), axis=0, keepdims=True)

    b = score[...] * across[...]
    a = score[...] * along[...] + guess * b
    whole = lambda x: jnp.broadcast_to(jnp.sum(x, keepdims=True), (1, count))
    own[...] = jnp.broadcast_to(guess, own.shape)

    total = lambda x: jnp.broadcast_to(jnp.sum(x, keepdims=True), (n, 1))
    deal[...] = jnp.zeros_like(deal)
    for part, row in enumerate((RATIO * spread(a), RATIO**2 * spread(b))):
        for k in range(n):
            deal[k : k + 1, part * height : (part + 1) * height] = row[:, k * height : (k + 1) * height]
    deal[:, 2 * height : 2 * height + 1] = RATIO**2 * total(sums[0])
    deal[:, 2 * height + 1 : 2 * height + 2] = RATIO * total(sums[1])


def replay_call(n, blocks, adjoint, weight, cot, weights, one, two, *rows):
    half = len(blocks)
    depth = one.shape[0]
    count, width = cot.shape
    far = pl.BlockSpec(memory_space=pl.ANY)
    vmem = pl.BlockSpec(memory_space=pltpu.VMEM)
    like = lambda x: pltpu.VMEM(x.shape, x.dtype)
    block = lambda dtype: pltpu.VMEM((TILE, width), dtype)
    return pl.pallas_call(
        functools.partial(replay_kernel, n, half),
        in_specs=[far] * (half + 1) + [vmem] * 11,
        out_specs=[vmem] * 11,
        out_shape=[
            *[like(x) for x in rows],
            pltpu.VMEM((depth, width), jnp.float32),
            pltpu.VMEM((count, width), jnp.float32),
            pltpu.VMEM((count, width), jnp.float32),
            pltpu.VMEM((8, 128), jnp.float32),
            jax.ShapeDtypeStruct((n, 128), jnp.float32),
        ],
        scratch_shapes=[
            block(jnp.float32),
            block(jnp.float32),
            block(jnp.bfloat16),
            block(jnp.bfloat16),
            block(jnp.bfloat16),
            block(jnp.bfloat16),
            pltpu.VMEM((2, 8, min(COLUMNS, width)), jnp.float32),
            pltpu.VMEM((count, 128), jnp.float32),
            pltpu.SemaphoreType.DMA((half,)),
            pltpu.SemaphoreType.DMA((depth // TILE,)),
        ],
        input_output_aliases={half + 6 + k: k for k in range(6)},
        compiler_params=pltpu.CompilerParams(vmem_limit_bytes=VMEM_BYTES),
        name="replay",
    )(*blocks, in_hbm(adjoint), weight, cot, weights, one, two, *rows)


def in_hbm(x):
    return pltpu.with_memory_space_constraint(x, pltpu.HBM)


def theta_kernel(entries, everyone, own, along, across, bend, turned, adjoint, theta, scores, ready, sent):
    height = scores.shape[1]
    total = jnp.sum(everyone[...], axis=0, keepdims=True)
    sq, cross = total[:, 2 * height : 2 * height + 1], total[:, 2 * height + 1 : 2 * height + 2]
    rms = jnp.sqrt(sq / entries)
    scale = 1.0 / jnp.maximum(1.0, rms)
    bind = jnp.where(rms > 1.0, 1.0 / (rms * rms * rms), 0.0)
    lead = -0.01 * scale
    rest = 0.01 * cross * bind / entries
    scores[...] = lead * total[:, 0:height] + rest * total[:, height : 2 * height]
    lead_here = RATIO * lead
    rest_here = RATIO**2 * rest + lead_here * own[0:1, 0:1]
    bent = (bend[...] * (lead_here * along[...] + rest_here * across[...])).astype(jnp.bfloat16)

    def copy(i):
        at = pl.ds(i * TILE, TILE)
        return pltpu.make_async_copy(ready.at[at, :], theta.at[at, :], sent.at[i])

    tiles = theta.shape[0] // TILE
    for i in range(tiles):
        at = pl.ds(i * TILE, TILE)
        ready[at, :] = 0.999 * adjoint[at, :] + f32dot(turned[at, :], bent)
        copy(i).start()
    for i in range(tiles):
        copy(i).wait()


def theta_call(n, entries, everyone, own, along, across, bend, turned, adjoint):
    depth, width = adjoint.shape
    count = turned.shape[1]
    vmem = pl.BlockSpec(memory_space=pltpu.VMEM)
    return pl.pallas_call(
        functools.partial(theta_kernel, entries),
        in_specs=[vmem] * 7,
        out_specs=[pl.BlockSpec(memory_space=pl.ANY), vmem],
        out_shape=[
            jax.ShapeDtypeStruct((depth, width), jnp.float32),
            jax.ShapeDtypeStruct((1, count // n), jnp.float32),
        ],
        scratch_shapes=[pltpu.VMEM((depth, width), jnp.float32), pltpu.SemaphoreType.DMA((depth // TILE,))],
        compiler_params=pltpu.CompilerParams(vmem_limit_bytes=VMEM_BYTES),
        name="theta",
    )(everyone, own, along, across, bend, turned, adjoint)


def shards(n, tokens, cotangent, token_weight, weight, moment_one, moment_two, adjoint):
    entries = float(adjoint.shape[0] * adjoint.shape[1] * n)
    errands = [
        lambda after: fetch(n, weight, cotangent, token_weight.reshape(1, -1), after),
        lambda after: fetch_wide(moment_one, 9.0, after),
        lambda after: fetch_wide(moment_two, 19.0, after),
    ]
    blocks, ((weight_near, cot, weights), one, two) = gather(tokens, n, errands)
    soon = len(blocks) // 2
    rows = early_call(blocks[:soon], weight_near, cot, weights)
    _, turned, _, _, bend, _, adjoint_near, along, across, own, deal = replay_call(
        n, blocks[soon:], adjoint, weight_near, cot, weights, one, two, *rows
    )
    everyone = to_all(deal)
    theta_bar, scores = theta_call(n, entries, everyone, own, along, across, bend, turned, adjoint_near)
    return (theta_bar, scores.reshape(-1))


def solution(mesh):
    in_specs = (
        P(("group", "dp"), None),
        P("group", "dp"),
        P("group"),
        P(None, "dp"),
        P(None, "dp"),
        P(None, "dp"),
        P(None, "dp"),
    )
    out_specs = (P("group", "dp"), P(("group", "dp")))
    body = functools.partial(shards, mesh.shape["dp"])
    return jax.shard_map(body, mesh=mesh, in_specs=in_specs, out_specs=out_specs, check_vma=False)
```

```python
import functools

import jax
import jax.numpy as jnp
from jax import lax
from jax.experimental import pallas as pl
from jax.experimental.pallas import tpu as pltpu
from jax.sharding import PartitionSpec as P

TILE = 512
HALF = 256
ROWS = 16
COLUMNS = 256
COST = 4 << 30
SAMPLE = 64
VMEM_BYTES = 12 << 20
RATIO = 0.1 / 0.05**0.5


def f32dot(a, b):
    return jnp.dot(a, b, preferred_element_type=jnp.float32)


def swapped(value, n, mask):
    return lax.ppermute(value, "dp", [(d ^ mask, d) for d in range(n)])


def ring(n):
    chips = n // 2
    return [*range(0, chips, 2), *range(chips - 1 - chips % 2, 0, -2)]


def onward(value, n):
    order = ring(n)
    pairs = []
    for i, chip in enumerate(order):
        pairs.append((2 * order[i - 1], 2 * chip))
        pairs.append((2 * order[(i + 1) % len(order)] + 1, 2 * chip + 1))
    return lax.ppermute(value, "dp", pairs)


def gather(tokens, n, errands):
    hops = n // 4
    done = []
    here = [tokens, swapped(tokens, n, 1)]
    parts, others = list(here), []
    for hop in range(1, hops + 1):
        after = in_hbm(tokens) if hop == 1 else here[0]
        here = [onward(x, n) for x in here]
        if errands[len(done) :]:
            done.append(errands[len(done)](after))
        if hop < hops:
            parts += here
            others += [swapped(x, n, 1) for x in here]
    return parts + others + here, done


def owners(n):
    chips = n // 2
    me = lax.axis_index("dp")
    chip, core = me >> 1, me & 1
    at = jnp.where(chip & 1 == 0, chip >> 1, chips - 1 - (chip >> 1))
    way = 2 * core - 1
    hops = range(1, chips // 2)
    blocks = [(0, core), *[(way * hop, core) for hop in hops], *[(-way * hop, 1 - core) for hop in hops]]
    blocks.append((way * (chips // 2), core))
    places = []
    for step, first in blocks:
        there = at + step
        there = jnp.where(there < 0, there + chips, jnp.where(there >= chips, there - chips, there))
        source = jnp.where(there < chips // 2, 2 * there, 2 * (chips - 1 - there) + 1)
        places += [2 * source + first, 2 * source + 1 - first]
    return places


def to_all(rows):
    return lax.all_to_all(rows, "dp", split_axis=0, concat_axis=0, tiled=True)


def over_columns(row):
    return jnp.transpose(jnp.broadcast_to(row, (8, row.shape[1])))[:, :1]


def fold(x):
    return jnp.sum(x.reshape(x.shape[0] // 8, 8, x.shape[1]), axis=0)


def update(grad, one, two):
    first = one + grad
    second = two + grad * grad
    over = lax.rsqrt(second)
    inv = pltpu.reciprocal(second * over + 1e-08 / 0.05**0.5, approx=True)
    return over, inv, first * inv


def fetch_params():
    return {
        "compiler_params": pltpu.CompilerParams(vmem_limit_bytes=6 << 20),
        "cost_estimate": pl.CostEstimate(flops=COST, bytes_accessed=8 << 20, transcendentals=0),
    }


def widen_kernel(factor, far, after, near, raw, sems):
    tiles = far.shape[0] // TILE

    def copy(i):
        return pltpu.make_async_copy(far.at[span(i), :], raw.at[span(i), :], sems.at[i])

    for i in range(tiles):
        copy(i).start()

    def step(i, _):
        copy(i).wait()
        near[span(i), :] = factor * raw[span(i), :].astype(jnp.float32)
        return 0

    lax.fori_loop(0, tiles, step, 0)


def fetch_wide(x, factor, after):
    return pl.pallas_call(
        functools.partial(widen_kernel, factor),
        in_specs=[pl.BlockSpec(memory_space=pl.ANY)] * 2,
        out_specs=pl.BlockSpec(memory_space=pltpu.VMEM),
        out_shape=pltpu.VMEM(x.shape, jnp.float32),
        scratch_shapes=[pltpu.VMEM(x.shape, x.dtype), pltpu.SemaphoreType.DMA((x.shape[0] // TILE,))],
        name="widen",
        **fetch_params(),
    )(in_hbm(x), after)


def fetch_kernel(n, far, far_cot, far_weight, after, near, cot, weights, token_weight, upright, sems, cot_sems):
    height = cot.shape[0] // n
    copy = pltpu.make_async_copy(far, near, sems.at[0])
    weight_copy = pltpu.make_async_copy(far_weight, token_weight, sems.at[1])
    weight_copy.start()
    copy.start()
    places = [pl.multiple_of(place * height, height) for place in owners(n)]
    cot_copies = [
        pltpu.make_async_copy(
            far_cot.at[pl.ds(place, height), :], cot.at[pl.ds(k * height, height), :], cot_sems.at[k]
        )
        for k, place in enumerate(places)
    ]
    for cot_copy in cot_copies:
        cot_copy.start()
    weight_copy.wait()
    upright[...] = jnp.broadcast_to(over_columns(token_weight[...]), upright.shape)
    for k, place in enumerate(places):
        weights[k * height : (k + 1) * height, :] = upright[pl.ds(place, height), :]
    for cot_copy in cot_copies:
        cot_copy.wait()
    copy.wait()


def fetch(n, weight, cot, token_weight, after):
    count = cot.shape[0]
    vmem = pl.BlockSpec(memory_space=pltpu.VMEM)
    return pl.pallas_call(
        functools.partial(fetch_kernel, n),
        in_specs=[pl.BlockSpec(memory_space=pl.ANY)] * 4,
        out_specs=[vmem] * 3,
        out_shape=[
            pltpu.VMEM(weight.shape, weight.dtype),
            pltpu.VMEM(cot.shape, cot.dtype),
            pltpu.VMEM((count, 128), jnp.float32),
        ],
        scratch_shapes=[
            pltpu.VMEM((1, count), jnp.float32),
            pltpu.VMEM((count, 128), jnp.float32),
            pltpu.SemaphoreType.DMA((2,)),
            pltpu.SemaphoreType.DMA((n,)),
        ],
        name="fetch",
        **fetch_params(),
    )(in_hbm(weight), in_hbm(cot), in_hbm(token_weight), after)


def span(i):
    return pl.ds(pl.multiple_of(i * TILE, TILE), TILE)


def bring(blocks, first, sems, tokens):
    height = blocks[0].shape[0]
    copies = [
        pltpu.make_async_copy(ref, tokens.at[pl.ds(first + k * height, height), :], sems.at[k])
        for k, ref in enumerate(blocks)
    ]
    for copy in copies:
        copy.start()
    return copies


def gate_rows(rows, weight, tokens, turned, gate, beside):
    gate[rows, :] = jnp.zeros((rows.stop - rows.start, gate.shape[1]), jnp.float32)

    def step(i, _):
        beside(i)
        here = tokens[rows, span(i)]
        gate[rows, :] += f32dot(here, weight[span(i), :])
        turned[span(i), rows] = here.T
        return 0

    lax.fori_loop(0, weight.shape[0] // TILE, step, 0)


def slope_rows(rows, gate, cot, weights, scaled, bend, score):
    for r in range(rows.start, rows.stop, 64):
        at = slice(r, r + 64)
        x = gate[at, :]
        token_weight = weights[at, 0:1]
        cot_f = cot[at, :].astype(jnp.float32)
        sig = 1.0 / (1.0 + jnp.exp(-x))
        slope = sig * (1.0 + x * (1.0 - sig))
        curve = sig * (1.0 - sig) * (2.0 + x * (1.0 - 2.0 * sig))
        scaled[at, :] = (token_weight * cot_f * slope).astype(jnp.bfloat16)
        bend[at, :] = token_weight * cot_f * curve
        score[at, :] = cot_f * slope


def early_kernel(parts, *refs):
    blocks, (weight, cot, weights) = refs[:parts], refs[parts : parts + 3]
    (tokens, turned, gate, scaled, bend, score, sems) = refs[parts + 3 :]
    rows = slice(0, gate.shape[0] // 2)
    for copy in bring(blocks, 0, sems, tokens):
        copy.wait()
    gate_rows(rows, weight, tokens, turned, gate, lambda i: None)
    slope_rows(rows, gate, cot, weights, scaled, bend, score)


def early_call(blocks, weight, cot, weights):
    parts = len(blocks)
    depth, width = weight.shape
    count = cot.shape[0]
    vmem = pl.BlockSpec(memory_space=pltpu.VMEM)
    return pl.pallas_call(
        functools.partial(early_kernel, parts),
        in_specs=[pl.BlockSpec(memory_space=pl.ANY)] * parts + [vmem] * 3,
        out_specs=[vmem] * 6,
        out_shape=[
            pltpu.VMEM((count, depth), jnp.bfloat16),
            pltpu.VMEM((depth, count), jnp.bfloat16),
            pltpu.VMEM((count, width), jnp.float32),
            pltpu.VMEM((count, width), jnp.bfloat16),
            pltpu.VMEM((count, width), jnp.float32),
            pltpu.VMEM((count, width), jnp.float32),
        ],
        scratch_shapes=[pltpu.SemaphoreType.DMA((parts,))],
        compiler_params=pltpu.CompilerParams(vmem_limit_bytes=4 << 20),
        cost_estimate=pl.CostEstimate(flops=COST, bytes_accessed=12 << 20, transcendentals=0),
        name="early",
    )(*blocks, weight, cot, weights)


def replay_kernel(n, half, *refs):
    blocks, (far, weight, cot, weights, one, two) = refs[:half], refs[half : half + 6]
    (tokens, turned, gate, scaled, bend, score) = refs[half + 12 : half + 18]
    (adjoint, along, across, own, deal) = refs[half + 18 : half + 23]
    (g0, g1, a0, a1, b0, b1, sums, upright, sems, tile_sems) = refs[half + 23 :]
    grads, firsts, seconds = (g0, g1), (a0, a1), (b0, b1)
    depth = one.shape[0]
    count, width = scaled.shape
    tiles = depth // TILE

    def tile_copy(i):
        return pltpu.make_async_copy(far.at[span(i), :], adjoint.at[span(i), :], tile_sems.at[i])

    rows = slice(count // 2, count)
    for copy in bring(blocks, count - half * blocks[0].shape[0], sems, tokens):
        copy.wait()
    gate_rows(rows, weight, tokens, turned, gate, lambda i: tile_copy(i).start())
    slope_rows(rows, gate, cot, weights, scaled, bend, score)

    along[...] = jnp.zeros_like(along)
    across[...] = jnp.zeros_like(across)

    def grad_rows(i, slot, r):
        at = pl.ds(pl.multiple_of(i * TILE + r, HALF), HALF)
        grads[slot][r : r + HALF, :] = f32dot(turned[at, :], scaled[...])

    def probe(i, slot, target, terms):
        target[...] += f32dot(tokens[:, span(i)], terms[slot][...])

    def pieces(i, slot, first, last):
        for r in range(first, last, ROWS):
            at = pl.ds(pl.multiple_of(i * TILE + r, ROWS), ROWS)
            for c in range(0, width, COLUMNS):
                cols = slice(c, min(c + COLUMNS, width))
                yield r, cols, grads[slot][r : r + ROWS, cols], one[at, cols], two[at, cols], adjoint[at, cols]

    for i in range(2):
        tile_copy(i).wait()
    grad_rows(0, 0, 0)
    grad_rows(0, 0, HALF)
    sq, cross = {}, {}
    for r, cols, g, m1, m2, adj in pieces(0, 0, 0, SAMPLE):
        _, _, upd = update(g, m1, m2)
        sq[cols.start] = sq.get(cols.start, 0.0) + fold(upd * upd)
        cross[cols.start] = cross.get(cols.start, 0.0) + fold(adj * upd)
    sq = jnp.sum(sum(sq.values()), keepdims=True)
    cross = jnp.sum(sum(cross.values()), keepdims=True)
    clipped = sq * RATIO**2 > float(SAMPLE * width)
    guess = jnp.where(clipped, cross / jnp.maximum(sq, 1.0), 0.0)

    sums[...] = jnp.zeros_like(sums)

    def update_rows(i, slot, first):
        sq, cross = {}, {}
        for r, cols, g, m1, m2, adj in pieces(i, slot, first, first + HALF):
            over, inv, upd = update(g, m1, m2)
            sq[cols.start] = sq.get(cols.start, 0.0) + fold(upd * upd)
            cross[cols.start] = cross.get(cols.start, 0.0) + fold(adj * upd)
            pull = inv * (1.0 - g * (upd * over))
            firsts[slot][r : r + ROWS, cols] = ((adj - guess * upd) * pull).astype(jnp.bfloat16)
            seconds[slot][r : r + ROWS, cols] = (upd * pull).astype(jnp.bfloat16)
        sums[0] += sum(sq.values())
        sums[1] += sum(cross.values())

    def body(i, slot, ahead=True, behind=True):
        for r, target, terms in ((0, along, firsts), (HALF, across, seconds)):
            if ahead:
                grad_rows(i + 1, 1 - slot, r)
            update_rows(i, slot, r)
            if behind:
                probe(i - 1, 1 - slot, target, terms)

    body(0, 0, behind=False)

    def pair(k, _):
        tile_copy(2 * k + 2).wait()
        tile_copy(2 * k + 3).wait()
        body(2 * k + 1, 1)
        body(2 * k + 2, 0)
        return 0

    lax.fori_loop(0, tiles // 2 - 1, pair, 0)
    body(tiles - 1, 1, ahead=False)
    probe(tiles - 1, 1, along, firsts)
    probe(tiles - 1, 1, across, seconds)

    height = count // n
    places = owners(n)

    def spread(x):
        x = sum(x[:, i : i + 128] for i in range(0, width, 128))
        for k, place in enumerate(places):
            upright[pl.ds(pl.multiple_of(place * height, height), height), :] = x[k * height : (k + 1) * height, :]
        return jnp.sum(jnp.transpose(upright[...]), axis=0, keepdims=True)

    b = score[...] * across[...]
    a = score[...] * along[...] + guess * b
    whole = lambda x: jnp.broadcast_to(jnp.sum(x, keepdims=True), (1, count))
    own[...] = jnp.broadcast_to(guess, own.shape)

    total = lambda x: jnp.broadcast_to(jnp.sum(x, keepdims=True), (n, 1))
    deal[...] = jnp.zeros_like(deal)
    for part, row in enumerate((RATIO * spread(a), RATIO**2 * spread(b))):
        for k in range(n):
            deal[k : k + 1, part * height : (part + 1) * height] = row[:, k * height : (k + 1) * height]
    deal[:, 2 * height : 2 * height + 1] = RATIO**2 * total(sums[0])
    deal[:, 2 * height + 1 : 2 * height + 2] = RATIO * total(sums[1])


def replay_call(n, blocks, adjoint, weight, cot, weights, one, two, *rows):
    half = len(blocks)
    depth = one.shape[0]
    count, width = cot.shape
    far = pl.BlockSpec(memory_space=pl.ANY)
    vmem = pl.BlockSpec(memory_space=pltpu.VMEM)
    like = lambda x: pltpu.VMEM(x.shape, x.dtype)
    block = lambda dtype: pltpu.VMEM((TILE, width), dtype)
    return pl.pallas_call(
        functools.partial(replay_kernel, n, half),
        in_specs=[far] * (half + 1) + [vmem] * 11,
        out_specs=[vmem] * 11,
        out_shape=[
            *[like(x) for x in rows],
            pltpu.VMEM((depth, width), jnp.float32),
            pltpu.VMEM((count, width), jnp.float32),
            pltpu.VMEM((count, width), jnp.float32),
            pltpu.VMEM((8, 128), jnp.float32),
            jax.ShapeDtypeStruct((n, 128), jnp.float32),
        ],
        scratch_shapes=[
            block(jnp.float32),
            block(jnp.float32),
            block(jnp.bfloat16),
            block(jnp.bfloat16),
            block(jnp.bfloat16),
            block(jnp.bfloat16),
            pltpu.VMEM((2, 8, min(COLUMNS, width)), jnp.float32),
            pltpu.VMEM((count, 128), jnp.float32),
            pltpu.SemaphoreType.DMA((half,)),
            pltpu.SemaphoreType.DMA((depth // TILE,)),
        ],
        input_output_aliases={half + 6 + k: k for k in range(6)},
        compiler_params=pltpu.CompilerParams(vmem_limit_bytes=VMEM_BYTES),
        name="replay",
    )(*blocks, in_hbm(adjoint), weight, cot, weights, one, two, *rows)


def in_hbm(x):
    return pltpu.with_memory_space_constraint(x, pltpu.HBM)


def theta_kernel(entries, everyone, own, along, across, bend, turned, adjoint, theta, scores, ready, sent):
    height = scores.shape[1]
    total = jnp.sum(everyone[...], axis=0, keepdims=True)
    sq, cross = total[:, 2 * height : 2 * height + 1], total[:, 2 * height + 1 : 2 * height + 2]
    rms = jnp.sqrt(sq / entries)
    scale = 1.0 / jnp.maximum(1.0, rms)
    bind = jnp.where(rms > 1.0, 1.0 / (rms * rms * rms), 0.0)
    lead = -0.01 * scale
    rest = 0.01 * cross * bind / entries
    scores[...] = lead * total[:, 0:height] + rest * total[:, height : 2 * height]
    lead_here = RATIO * lead
    rest_here = RATIO**2 * rest + lead_here * own[0:1, 0:1]
    bent = (bend[...] * (lead_here * along[...] + rest_here * across[...])).astype(jnp.bfloat16)

    def copy(i):
        at = pl.ds(i * TILE, TILE)
        return pltpu.make_async_copy(ready.at[at, :], theta.at[at, :], sent.at[i])

    tiles = theta.shape[0] // TILE
    for i in range(tiles):
        at = pl.ds(i * TILE, TILE)
        ready[at, :] = 0.999 * adjoint[at, :] + f32dot(turned[at, :], bent)
        copy(i).start()
    for i in range(tiles):
        copy(i).wait()


def theta_call(n, entries, everyone, own, along, across, bend, turned, adjoint):
    depth, width = adjoint.shape
    count = turned.shape[1]
    vmem = pl.BlockSpec(memory_space=pltpu.VMEM)
    return pl.pallas_call(
        functools.partial(theta_kernel, entries),
        in_specs=[vmem] * 7,
        out_specs=[pl.BlockSpec(memory_space=pl.ANY), vmem],
        out_shape=[
            jax.ShapeDtypeStruct((depth, width), jnp.float32),
            jax.ShapeDtypeStruct((1, count // n), jnp.float32),
        ],
        scratch_shapes=[pltpu.VMEM((depth, width), jnp.float32), pltpu.SemaphoreType.DMA((depth // TILE,))],
        compiler_params=pltpu.CompilerParams(vmem_limit_bytes=VMEM_BYTES),
        name="theta",
    )(everyone, own, along, across, bend, turned, adjoint)


def shards(n, tokens, cotangent, token_weight, weight, moment_one, moment_two, adjoint):
    entries = float(adjoint.shape[0] * adjoint.shape[1] * n)
    errands = [
        lambda after: fetch(n, weight, cotangent, token_weight.reshape(1, -1), after),
        lambda after: fetch_wide(moment_one, 9.0, after),
        lambda after: fetch_wide(moment_two, 19.0, after),
    ]
    blocks, ((weight_near, cot, weights), one, two) = gather(tokens, n, errands)
    soon = len(blocks) // 2
    rows = early_call(blocks[:soon], weight_near, cot, weights)
    _, turned, _, _, bend, _, adjoint_near, along, across, own, deal = replay_call(
        n, blocks[soon:], adjoint, weight_near, cot, weights, one, two, *rows
    )
    everyone = to_all(deal)
    theta_bar, scores = theta_call(n, entries, everyone, own, along, across, bend, turned, adjoint_near)
    return (theta_bar, scores.reshape(-1))


def solution(mesh):
    in_specs = (
        P(("group", "dp"), None),
        P("group", "dp"),
        P("group"),
        P(None, "dp"),
        P(None, "dp"),
        P(None, "dp"),
        P(None, "dp"),
    )
    out_specs = (P("group", "dp"), P(("group", "dp")))
    body = functools.partial(shards, mesh.shape["dp"])
    return jax.shard_map(body, mesh=mesh, in_specs=in_specs, out_specs=out_specs, check_vma=False)
```

```python
import functools

import jax
import jax.numpy as jnp
from jax import lax
from jax.experimental import pallas as pl
from jax.experimental.pallas import tpu as pltpu
from jax.sharding import PartitionSpec as P

TILE = 512
HALF = 256
ROWS = 16
COLUMNS = 128
COST = 4 << 30
SAMPLE = 64
VMEM_BYTES = 12 << 20
RATIO = 0.1 / 0.05**0.5


def f32dot(a, b):
    return jnp.dot(a, b, preferred_element_type=jnp.float32)


def swapped(value, n, mask):
    return lax.ppermute(value, "dp", [(d ^ mask, d) for d in range(n)])


def ring(n):
    chips = n // 2
    return [*range(0, chips, 2), *range(chips - 1 - chips % 2, 0, -2)]


def onward(value, n):
    order = ring(n)
    pairs = []
    for i, chip in enumerate(order):
        pairs.append((2 * order[i - 1], 2 * chip))
        pairs.append((2 * order[(i + 1) % len(order)] + 1, 2 * chip + 1))
    return lax.ppermute(value, "dp", pairs)


def gather(tokens, n, errands):
    hops = n // 4
    done = []
    here = [tokens, swapped(tokens, n, 1)]
    parts, others = list(here), []
    for hop in range(1, hops + 1):
        after = in_hbm(tokens) if hop == 1 else here[0]
        here = [onward(x, n) for x in here]
        if errands[len(done) :]:
            done.append(errands[len(done)](after))
        if hop < hops:
            parts += here
            others += [swapped(x, n, 1) for x in here]
    return parts + others + here, done


def owners(n):
    chips = n // 2
    me = lax.axis_index("dp")
    chip, core = me >> 1, me & 1
    at = jnp.where(chip & 1 == 0, chip >> 1, chips - 1 - (chip >> 1))
    way = 2 * core - 1
    hops = range(1, chips // 2)
    blocks = [(0, core), *[(way * hop, core) for hop in hops], *[(-way * hop, 1 - core) for hop in hops]]
    blocks.append((way * (chips // 2), core))
    places = []
    for step, first in blocks:
        there = at + step
        there = jnp.where(there < 0, there + chips, jnp.where(there >= chips, there - chips, there))
        source = jnp.where(there < chips // 2, 2 * there, 2 * (chips - 1 - there) + 1)
        places += [2 * source + first, 2 * source + 1 - first]
    return places


def to_all(rows):
    return lax.all_to_all(rows, "dp", split_axis=0, concat_axis=0, tiled=True)


def over_columns(row):
    return jnp.transpose(jnp.broadcast_to(row, (8, row.shape[1])))[:, :1]


def fold(x):
    return jnp.sum(x.reshape(x.shape[0] // 8, 8, x.shape[1]), axis=0)


def update(grad, one, two):
    first = one + grad
    second = two + grad * grad
    over = lax.rsqrt(second)
    inv = pltpu.reciprocal(second * over + 1e-08 / 0.05**0.5, approx=True)
    return over, inv, first * inv


def fetch_params():
    return {
        "compiler_params": pltpu.CompilerParams(vmem_limit_bytes=6 << 20),
        "cost_estimate": pl.CostEstimate(flops=COST, bytes_accessed=8 << 20, transcendentals=0),
    }


def widen_kernel(factor, far, after, near, raw, sems):
    tiles = far.shape[0] // TILE

    def copy(i):
        return pltpu.make_async_copy(far.at[span(i), :], raw.at[span(i), :], sems.at[i])

    for i in range(tiles):
        copy(i).start()

    def step(i, _):
        copy(i).wait()
        near[span(i), :] = factor * raw[span(i), :].astype(jnp.float32)
        return 0

    lax.fori_loop(0, tiles, step, 0)


def fetch_wide(x, factor, after):
    return pl.pallas_call(
        functools.partial(widen_kernel, factor),
        in_specs=[pl.BlockSpec(memory_space=pl.ANY)] * 2,
        out_specs=pl.BlockSpec(memory_space=pltpu.VMEM),
        out_shape=pltpu.VMEM(x.shape, jnp.float32),
        scratch_shapes=[pltpu.VMEM(x.shape, x.dtype), pltpu.SemaphoreType.DMA((x.shape[0] // TILE,))],
        name="widen",
        **fetch_params(),
    )(in_hbm(x), after)


def fetch_kernel(n, far, far_cot, far_weight, after, near, cot, weights, token_weight, upright, sems, cot_sems):
    height = cot.shape[0] // n
    copy = pltpu.make_async_copy(far, near, sems.at[0])
    weight_copy = pltpu.make_async_copy(far_weight, token_weight, sems.at[1])
    weight_copy.start()
    copy.start()
    places = [pl.multiple_of(place * height, height) for place in owners(n)]
    cot_copies = [
        pltpu.make_async_copy(
            far_cot.at[pl.ds(place, height), :], cot.at[pl.ds(k * height, height), :], cot_sems.at[k]
        )
        for k, place in enumerate(places)
    ]
    for cot_copy in cot_copies:
        cot_copy.start()
    weight_copy.wait()
    upright[...] = jnp.broadcast_to(over_columns(token_weight[...]), upright.shape)
    for k, place in enumerate(places):
        weights[k * height : (k + 1) * height, :] = upright[pl.ds(place, height), :]
    for cot_copy in cot_copies:
        cot_copy.wait()
    copy.wait()


def fetch(n, weight, cot, token_weight, after):
    count = cot.shape[0]
    vmem = pl.BlockSpec(memory_space=pltpu.VMEM)
    return pl.pallas_call(
        functools.partial(fetch_kernel, n),
        in_specs=[pl.BlockSpec(memory_space=pl.ANY)] * 4,
        out_specs=[vmem] * 3,
        out_shape=[
            pltpu.VMEM(weight.shape, weight.dtype),
            pltpu.VMEM(cot.shape, cot.dtype),
            pltpu.VMEM((count, 128), jnp.float32),
        ],
        scratch_shapes=[
            pltpu.VMEM((1, count), jnp.float32),
            pltpu.VMEM((count, 128), jnp.float32),
            pltpu.SemaphoreType.DMA((2,)),
            pltpu.SemaphoreType.DMA((n,)),
        ],
        name="fetch",
        **fetch_params(),
    )(in_hbm(weight), in_hbm(cot), in_hbm(token_weight), after)


def span(i):
    return pl.ds(pl.multiple_of(i * TILE, TILE), TILE)


def bring(blocks, first, sems, tokens):
    height = blocks[0].shape[0]
    copies = [
        pltpu.make_async_copy(ref, tokens.at[pl.ds(first + k * height, height), :], sems.at[k])
        for k, ref in enumerate(blocks)
    ]
    for copy in copies:
        copy.start()
    return copies


def gate_rows(rows, weight, tokens, turned, gate, beside):
    gate[rows, :] = jnp.zeros((rows.stop - rows.start, gate.shape[1]), jnp.float32)

    def step(i, _):
        beside(i)
        here = tokens[rows, span(i)]
        gate[rows, :] += f32dot(here, weight[span(i), :])
        turned[span(i), rows] = here.T
        return 0

    lax.fori_loop(0, weight.shape[0] // TILE, step, 0)


def slope_rows(rows, gate, cot, weights, scaled, bend, score):
    for r in range(rows.start, rows.stop, 64):
        at = slice(r, r + 64)
        x = gate[at, :]
        token_weight = weights[at, 0:1]
        cot_f = cot[at, :].astype(jnp.float32)
        sig = 1.0 / (1.0 + jnp.exp(-x))
        slope = sig * (1.0 + x * (1.0 - sig))
        curve = sig * (1.0 - sig) * (2.0 + x * (1.0 - 2.0 * sig))
        scaled[at, :] = (token_weight * cot_f * slope).astype(jnp.bfloat16)
        bend[at, :] = token_weight * cot_f * curve
        score[at, :] = cot_f * slope


def early_kernel(parts, *refs):
    blocks, (weight, cot, weights) = refs[:parts], refs[parts : parts + 3]
    (tokens, turned, gate, scaled, bend, score, sems) = refs[parts + 3 :]
    rows = slice(0, gate.shape[0] // 2)
    for copy in bring(blocks, 0, sems, tokens):
        copy.wait()
    gate_rows(rows, weight, tokens, turned, gate, lambda i: None)
    slope_rows(rows, gate, cot, weights, scaled, bend, score)


def early_call(blocks, weight, cot, weights):
    parts = len(blocks)
    depth, width = weight.shape
    count = cot.shape[0]
    vmem = pl.BlockSpec(memory_space=pltpu.VMEM)
    return pl.pallas_call(
        functools.partial(early_kernel, parts),
        in_specs=[pl.BlockSpec(memory_space=pl.ANY)] * parts + [vmem] * 3,
        out_specs=[vmem] * 6,
        out_shape=[
            pltpu.VMEM((count, depth), jnp.bfloat16),
            pltpu.VMEM((depth, count), jnp.bfloat16),
            pltpu.VMEM((count, width), jnp.float32),
            pltpu.VMEM((count, width), jnp.bfloat16),
            pltpu.VMEM((count, width), jnp.float32),
            pltpu.VMEM((count, width), jnp.float32),
        ],
        scratch_shapes=[pltpu.SemaphoreType.DMA((parts,))],
        compiler_params=pltpu.CompilerParams(vmem_limit_bytes=4 << 20),
        cost_estimate=pl.CostEstimate(flops=COST, bytes_accessed=12 << 20, transcendentals=0),
        name="early",
    )(*blocks, weight, cot, weights)


def replay_kernel(n, half, *refs):
    blocks, (far, weight, cot, weights, one, two) = refs[:half], refs[half : half + 6]
    (tokens, turned, gate, scaled, bend, score) = refs[half + 12 : half + 18]
    (adjoint, along, across, own, deal) = refs[half + 18 : half + 23]
    (g0, g1, a0, a1, b0, b1, sums, upright, sems, tile_sems) = refs[half + 23 :]
    grads, firsts, seconds = (g0, g1), (a0, a1), (b0, b1)
    depth = one.shape[0]
    count, width = scaled.shape
    tiles = depth // TILE

    def tile_copy(i):
        return pltpu.make_async_copy(far.at[span(i), :], adjoint.at[span(i), :], tile_sems.at[i])

    rows = slice(count // 2, count)
    for copy in bring(blocks, count - half * blocks[0].shape[0], sems, tokens):
        copy.wait()
    gate_rows(rows, weight, tokens, turned, gate, lambda i: tile_copy(i).start())
    slope_rows(rows, gate, cot, weights, scaled, bend, score)

    along[...] = jnp.zeros_like(along)
    across[...] = jnp.zeros_like(across)

    def grad_rows(i, slot, r):
        at = pl.ds(pl.multiple_of(i * TILE + r, HALF), HALF)
        grads[slot][r : r + HALF, :] = f32dot(turned[at, :], scaled[...])

    def probe(i, slot, target, terms):
        target[...] += f32dot(tokens[:, span(i)], terms[slot][...])

    def pieces(i, slot, first, last):
        for r in range(first, last, ROWS):
            at = pl.ds(pl.multiple_of(i * TILE + r, ROWS), ROWS)
            for c in range(0, width, COLUMNS):
                cols = slice(c, min(c + COLUMNS, width))
                yield r, cols, grads[slot][r : r + ROWS, cols], one[at, cols], two[at, cols], adjoint[at, cols]

    for i in range(2):
        tile_copy(i).wait()
    grad_rows(0, 0, 0)
    grad_rows(0, 0, HALF)
    sq, cross = {}, {}
    for r, cols, g, m1, m2, adj in pieces(0, 0, 0, SAMPLE):
        _, _, upd = update(g, m1, m2)
        sq[cols.start] = sq.get(cols.start, 0.0) + fold(upd * upd)
        cross[cols.start] = cross.get(cols.start, 0.0) + fold(adj * upd)
    sq = jnp.sum(sum(sq.values()), keepdims=True)
    cross = jnp.sum(sum(cross.values()), keepdims=True)
    clipped = sq * RATIO**2 > float(SAMPLE * width)
    guess = jnp.where(clipped, cross / jnp.maximum(sq, 1.0), 0.0)

    sums[...] = jnp.zeros_like(sums)

    def update_rows(i, slot, first):
        sq, cross = {}, {}
        for r, cols, g, m1, m2, adj in pieces(i, slot, first, first + HALF):
            over, inv, upd = update(g, m1, m2)
            sq[cols.start] = sq.get(cols.start, 0.0) + fold(upd * upd)
            cross[cols.start] = cross.get(cols.start, 0.0) + fold(adj * upd)
            pull = inv * (1.0 - g * (upd * over))
            firsts[slot][r : r + ROWS, cols] = ((adj - guess * upd) * pull).astype(jnp.bfloat16)
            seconds[slot][r : r + ROWS, cols] = (upd * pull).astype(jnp.bfloat16)
        sums[0] += sum(sq.values())
        sums[1] += sum(cross.values())

    def body(i, slot, ahead=True, behind=True):
        for r, target, terms in ((0, along, firsts), (HALF, across, seconds)):
            if ahead:
                grad_rows(i + 1, 1 - slot, r)
            update_rows(i, slot, r)
            if behind:
                probe(i - 1, 1 - slot, target, terms)

    body(0, 0, behind=False)

    def pair(k, _):
        tile_copy(2 * k + 2).wait()
        tile_copy(2 * k + 3).wait()
        body(2 * k + 1, 1)
        body(2 * k + 2, 0)
        return 0

    lax.fori_loop(0, tiles // 2 - 1, pair, 0)
    body(tiles - 1, 1, ahead=False)
    probe(tiles - 1, 1, along, firsts)
    probe(tiles - 1, 1, across, seconds)

    height = count // n
    places = owners(n)

    def spread(x):
        x = sum(x[:, i : i + 128] for i in range(0, width, 128))
        for k, place in enumerate(places):
            upright[pl.ds(pl.multiple_of(place * height, height), height), :] = x[k * height : (k + 1) * height, :]
        return jnp.sum(jnp.transpose(upright[...]), axis=0, keepdims=True)

    b = score[...] * across[...]
    a = score[...] * along[...] + guess * b
    whole = lambda x: jnp.broadcast_to(jnp.sum(x, keepdims=True), (1, count))
    own[...] = jnp.broadcast_to(guess, own.shape)

    total = lambda x: jnp.broadcast_to(jnp.sum(x, keepdims=True), (n, 1))
    deal[...] = jnp.zeros_like(deal)
    for part, row in enumerate((RATIO * spread(a), RATIO**2 * spread(b))):
        for k in range(n):
            deal[k : k + 1, part * height : (part + 1) * height] = row[:, k * height : (k + 1) * height]
    deal[:, 2 * height : 2 * height + 1] = RATIO**2 * total(sums[0])
    deal[:, 2 * height + 1 : 2 * height + 2] = RATIO * total(sums[1])


def replay_call(n, blocks, adjoint, weight, cot, weights, one, two, *rows):
    half = len(blocks)
    depth = one.shape[0]
    count, width = cot.shape
    far = pl.BlockSpec(memory_space=pl.ANY)
    vmem = pl.BlockSpec(memory_space=pltpu.VMEM)
    like = lambda x: pltpu.VMEM(x.shape, x.dtype)
    block = lambda dtype: pltpu.VMEM((TILE, width), dtype)
    return pl.pallas_call(
        functools.partial(replay_kernel, n, half),
        in_specs=[far] * (half + 1) + [vmem] * 11,
        out_specs=[vmem] * 11,
        out_shape=[
            *[like(x) for x in rows],
            pltpu.VMEM((depth, width), jnp.float32),
            pltpu.VMEM((count, width), jnp.float32),
            pltpu.VMEM((count, width), jnp.float32),
            pltpu.VMEM((8, 128), jnp.float32),
            jax.ShapeDtypeStruct((n, 128), jnp.float32),
        ],
        scratch_shapes=[
            block(jnp.float32),
            block(jnp.float32),
            block(jnp.bfloat16),
            block(jnp.bfloat16),
            block(jnp.bfloat16),
            block(jnp.bfloat16),
            pltpu.VMEM((2, 8, min(COLUMNS, width)), jnp.float32),
            pltpu.VMEM((count, 128), jnp.float32),
            pltpu.SemaphoreType.DMA((half,)),
            pltpu.SemaphoreType.DMA((depth // TILE,)),
        ],
        input_output_aliases={half + 6 + k: k for k in range(6)},
        compiler_params=pltpu.CompilerParams(vmem_limit_bytes=VMEM_BYTES),
        name="replay",
    )(*blocks, in_hbm(adjoint), weight, cot, weights, one, two, *rows)


def in_hbm(x):
    return pltpu.with_memory_space_constraint(x, pltpu.HBM)


def theta_kernel(entries, everyone, own, along, across, bend, turned, adjoint, theta, scores, ready, sent):
    height = scores.shape[1]
    total = jnp.sum(everyone[...], axis=0, keepdims=True)
    sq, cross = total[:, 2 * height : 2 * height + 1], total[:, 2 * height + 1 : 2 * height + 2]
    rms = jnp.sqrt(sq / entries)
    scale = 1.0 / jnp.maximum(1.0, rms)
    bind = jnp.where(rms > 1.0, 1.0 / (rms * rms * rms), 0.0)
    lead = -0.01 * scale
    rest = 0.01 * cross * bind / entries
    scores[...] = lead * total[:, 0:height] + rest * total[:, height : 2 * height]
    lead_here = RATIO * lead
    rest_here = RATIO**2 * rest + lead_here * own[0:1, 0:1]
    bent = (bend[...] * (lead_here * along[...] + rest_here * across[...])).astype(jnp.bfloat16)

    def copy(i):
        at = pl.ds(i * TILE, TILE)
        return pltpu.make_async_copy(ready.at[at, :], theta.at[at, :], sent.at[i])

    tiles = theta.shape[0] // TILE
    for i in range(tiles):
        at = pl.ds(i * TILE, TILE)
        ready[at, :] = 0.999 * adjoint[at, :] + f32dot(turned[at, :], bent)
        copy(i).start()
    for i in range(tiles):
        copy(i).wait()


def theta_call(n, entries, everyone, own, along, across, bend, turned, adjoint):
    depth, width = adjoint.shape
    count = turned.shape[1]
    vmem = pl.BlockSpec(memory_space=pltpu.VMEM)
    return pl.pallas_call(
        functools.partial(theta_kernel, entries),
        in_specs=[vmem] * 7,
        out_specs=[pl.BlockSpec(memory_space=pl.ANY), vmem],
        out_shape=[
            jax.ShapeDtypeStruct((depth, width), jnp.float32),
            jax.ShapeDtypeStruct((1, count // n), jnp.float32),
        ],
        scratch_shapes=[pltpu.VMEM((depth, width), jnp.float32), pltpu.SemaphoreType.DMA((depth // TILE,))],
        compiler_params=pltpu.CompilerParams(vmem_limit_bytes=VMEM_BYTES),
        name="theta",
    )(everyone, own, along, across, bend, turned, adjoint)


def shards(n, tokens, cotangent, token_weight, weight, moment_one, moment_two, adjoint):
    entries = float(adjoint.shape[0] * adjoint.shape[1] * n)
    errands = [
        lambda after: fetch(n, weight, cotangent, token_weight.reshape(1, -1), after),
        lambda after: fetch_wide(moment_one, 9.0, after),
        lambda after: fetch_wide(moment_two, 19.0, after),
    ]
    blocks, ((weight_near, cot, weights), one, two) = gather(tokens, n, errands)
    soon = len(blocks) // 2
    rows = early_call(blocks[:soon], weight_near, cot, weights)
    _, turned, _, _, bend, _, adjoint_near, along, across, own, deal = replay_call(
        n, blocks[soon:], adjoint, weight_near, cot, weights, one, two, *rows
    )
    everyone = to_all(deal)
    theta_bar, scores = theta_call(n, entries, everyone, own, along, across, bend, turned, adjoint_near)
    return (theta_bar, scores.reshape(-1))


def solution(mesh):
    in_specs = (
        P(("group", "dp"), None),
        P("group", "dp"),
        P("group"),
        P(None, "dp"),
        P(None, "dp"),
        P(None, "dp"),
        P(None, "dp"),
    )
    out_specs = (P("group", "dp"), P(("group", "dp")))
    body = functools.partial(shards, mesh.shape["dp"])
    return jax.shard_map(body, mesh=mesh, in_specs=in_specs, out_specs=out_specs, check_vma=False)
```
